128 devices in a mesh: dp: 32 (over x, y, core), seq: 4 (over z).
Axes of the slice: x: 4, y: 4, z: 4, core: 2. Of those that a mesh axis runs over, the one named last changes fastest.
Arguments:
- hidden_in: bfloat16 [2, 32, 1024, 1024], P(None, 'dp', 'seq'), may hold values from -6 to 6
- segments: int32 [2, 32, 1024], P(None, 'dp'), may hold values from 0 to 1023, as said below
- valid_mask: int32 [2, 32, 1024], P(None, 'dp'), may hold values from 0 to 1, as said below
- w_qkv: bfloat16 [1024, 3072], P(('dp', 'seq')), may hold values from -0.1875 to 0.1875
- w_out: bfloat16 [1024, 1024], P(('dp', 'seq')), may hold values from -1.5 to 1.5
- w_up: bfloat16 [1024, 4096], P(('dp', 'seq')), may hold values from -0.1875 to 0.1875
- w_down: bfloat16 [4096, 1024], P(('dp', 'seq')), may hold values from -0.09375 to 0.09375
- b_qkv: bfloat16 [3072], P(('dp', 'seq')), may hold values from -3 to 3
- b_out: bfloat16 [1024], P(('dp', 'seq')), may hold values from -3 to 3
- b_up: bfloat16 [4096], P(('dp', 'seq')), may hold values from -3 to 3
- b_down: bfloat16 [1024], P(('dp', 'seq')), may hold values from -3 to 3
- ln_gain: bfloat16 [1024], P(('dp', 'seq')), may hold values from 0.099609375 to 1.8984375
- ln_shift: bfloat16 [1024], P(('dp', 'seq')), may hold values from -3 to 3
- cotangent: bfloat16 [2, 32, 1024, 1024], P(None, 'dp', 'seq'), may hold values from -6 to 6
Outputs:
- out_hidden: bfloat16 [2, 32, 1024, 1024], P(None, 'dp', 'seq')
- grad_input: float32 [2, 32, 1024, 1024], P(None, 'dp', 'seq')
- grad_qkv: float32 [1024, 3072], P(('dp', 'seq'))
- grad_out: float32 [1024, 1024], P(('dp', 'seq'))
- grad_up: float32 [1024, 4096], P(('dp', 'seq'))
- grad_down: float32 [4096, 1024], P(('dp', 'seq'))
- grad_bqkv: float32 [3072], P(('dp', 'seq'))
- grad_bout: float32 [1024], P(('dp', 'seq'))
- grad_bup: float32 [4096], P(('dp', 'seq'))
- grad_bdown: float32 [1024], P(('dp', 'seq'))
- grad_gain: float32 [1024], P(('dp', 'seq'))
- grad_shift: float32 [1024], P(('dp', 'seq'))
The draws below stay inside these ranges and needn't reach their ends.
Inputs may be any that keep to these rules, and one draw needn't show every extreme that they name: `segments`: along a row, segment ids start at 0 and never fall; tokens of one document are contiguous; the padding tokens form the last segment, with id 1024 - 1. `valid_mask`: along a row the ones come first and at least one zero ends it.
All inputs are finite; a program needn't handle non-finite values.
Results may differ from the reference program's by a relative error of at most 0.011.
Values may be sent and summed in bfloat16 or wider, within the bound.
No kernel may reach another device: no remote copies, remote signals or barrier semaphores. Data moves between devices by JAX's collectives and lax.ppermute only.
A program may use at most 256 MiB of HBM per device.

```python
import jax
import jax.numpy as jnp
from jax import lax

D = 1024
HEADS = 16
HEAD_DIM = 64
ROT = 32
FF = 4096
GROUP = 256
MICRO = 2
ROWS = 32
LEN = 1024


def document_layout(key):
    grid_shape = (MICRO, ROWS, LEN)
    start_key, end_key, pad_key, cut_key = jax.random.split(key, 4)
    long_start = jax.random.randint(start_key, (MICRO, ROWS, 1), 0, GROUP)
    long_end = jax.random.randint(end_key, (MICRO, ROWS, 1), 3 * GROUP + 1, LEN - GROUP // 4 + 1)
    pad_count = jax.random.randint(pad_key, (MICRO, ROWS, 1), 1, GROUP // 8 + 1)
    boundary = jax.random.randint(cut_key, grid_shape, 0, GROUP // 4) == 0
    position = jnp.arange(LEN, dtype=jnp.int32)[None, None, :]
    inside = (position > long_start) & (position < long_end)
    boundary = boundary & ~inside | (position == long_start) | (position == long_end)
    running = jnp.cumsum(boundary.astype(jnp.int32), axis=2)
    valid_ids = (position < LEN - pad_count).astype(jnp.int32)
    segment_ids = jnp.where(valid_ids > 0, running - running[:, :, :1], LEN - 1).astype(jnp.int32)
    return (segment_ids, valid_ids)


def draw_segments(key, part):
    return document_layout(key)[0]


def draw_valid_mask(key, part):
    return document_layout(key)[1]


def level_of(own_key, dims, cuts, low, largest):
    level, own = 1.0, jax.random.fold_in(own_key, 6)
    for dim, shards_of in cuts:
        draws = jnp.exp(jax.random.uniform(jax.random.fold_in(own, dim), (shards_of,), jnp.float32, low / len(cuts), largest / len(cuts)))
        level = level * jnp.repeat(draws, dims[dim] // shards_of).reshape([-1 if axis == dim else 1 for axis in range(len(dims))])
    return level


def gaussian(key, shape, deviation, reach, cuts=(), held_as=jnp.bfloat16):
    entries = deviation * jax.random.normal(key, shape, jnp.float32)
    if cuts:
        entries = entries * level_of(key, shape, cuts, -0.22, 0.18)
    return jnp.clip(entries, -reach, reach).astype(held_as)


def setup_inputs(seed: int = 0) -> dict:
    streams_of = jax.random.split(jax.random.key(seed), 15)
    return {
        "hidden_in": gaussian(streams_of[0], (MICRO, ROWS, LEN, D), 1.0, 6.0, ((1, 32), (2, 4))),
        "segments": draw_segments(jax.random.fold_in(streams_of[14], 71), 0),
        "valid_mask": draw_valid_mask(jax.random.fold_in(streams_of[14], 71), 0),
        "w_qkv": gaussian(streams_of[3], (D, 3 * D), D ** -0.5, 0.1875, ((0, 128),)),
        "w_out": gaussian(streams_of[4], (D, D), (D // 64) ** -0.5, 1.5, ((0, 128),)),
        "w_up": gaussian(streams_of[5], (D, FF), D ** -0.5, 0.1875, ((0, 128),)),
        "w_down": gaussian(streams_of[6], (FF, D), FF ** -0.5, 0.09375, ((0, 128),)),
        "b_qkv": gaussian(streams_of[7], (3 * D,), 0.5, 3.0, ((0, 128),)),
        "b_out": gaussian(streams_of[8], (D,), 0.5, 3.0, ((0, 128),)),
        "b_up": gaussian(streams_of[9], (FF,), 0.5, 3.0, ((0, 128),)),
        "b_down": gaussian(streams_of[10], (D,), 0.5, 3.0, ((0, 128),)),
        "ln_gain": jnp.clip(1.0 + 0.18 * jax.random.normal(streams_of[11], (D,), jnp.float32), 0.099609375, 1.8984375).astype(jnp.bfloat16),
        "ln_shift": gaussian(streams_of[12], (D,), 0.5, 3.0, ((0, 128),)),
        "cotangent": gaussian(streams_of[13], (MICRO, ROWS, LEN, D), 1.0, 6.0, ((1, 32), (2, 4))),
    }


@jax.custom_vjp
def low(v):
    return lax.optimization_barrier(v.astype(jnp.bfloat16)).astype(jnp.float32)

@jax.custom_vjp
def low_back(v):
    return v

def low_keep(v):
    return (low(v), None)

def low_pass(kept, grad):
    return (grad,)

def back_keep(v):
    return (v, None)

def back_low(kept, grad):
    return (low(grad),)
low.defvjp(low_keep, low_pass)
low_back.defvjp(back_keep, back_low)

def matmul_hi(left, right):
    return jnp.dot(left, right, precision=lax.Precision.HIGHEST, preferred_element_type=jnp.float32)

def layer_norm(inputs, gain, shift):
    average = lax.optimization_barrier(jnp.mean(inputs, axis=-1, keepdims=True))
    centered = inputs - average
    spread = lax.optimization_barrier(jnp.mean(centered * centered, axis=-1, keepdims=True))
    return centered * lax.rsqrt(spread + 1e-05) * gain + shift

def doc_positions(seg_row):
    length = seg_row.shape[-1]
    token_index = jnp.arange(length, dtype=jnp.int32)
    previous = jnp.concatenate([seg_row[..., :1], seg_row[..., :-1]], axis=-1)
    starts = jnp.where((token_index == 0) | (seg_row != previous), token_index, 0).astype(jnp.int32)
    doc_start = lax.cummax(starts, axis=seg_row.ndim - 1)
    return token_index - doc_start

def rotary_tables(positions):
    half_dim = ROT // 2
    frequency = 10000.0 ** (-jnp.arange(half_dim, dtype=jnp.float32) * 2.0 / ROT)
    angles = positions.astype(jnp.float32)[..., None] * frequency
    return (jnp.cos(angles), jnp.sin(angles))

def rotate(tensor, cosine, sine_tab):
    half_dim = cosine.shape[-1]
    cos_b = cosine[..., None, :]
    sin_b = sine_tab[..., None, :]
    first_half = tensor[..., :half_dim]
    second = tensor[..., half_dim:2 * half_dim]
    passed = tensor[..., 2 * half_dim:]
    return jnp.concatenate([first_half * cos_b - second * sin_b, second * cos_b + first_half * sin_b, passed], axis=-1)

def allowed_keys(seg_query, seg_key, query_index, key_index, valid_key):
    same_doc = seg_query[:, None] == seg_key[None, :]
    causal = key_index[None, :] <= query_index[:, None]
    visible = (valid_key[None, :] > 0) | (key_index[None, :] == query_index[:, None])
    return same_doc & causal & visible

def gelu_tanh(values_in):
    return jax.nn.gelu(values_in, approximate=True)

def row_forward(params, row_in, seg_row, valid_row):
    w_qkv, w_out, w_up, w_down, b_qkv, b_out, b_up, b_down, ln_gain, ln_shift = params
    length = row_in.shape[0]
    normed = low(layer_norm(row_in, ln_gain, ln_shift))
    qkv = low_back(matmul_hi(normed, w_qkv) + b_qkv)
    cosine, sine_tab = rotary_tables(doc_positions(seg_row))
    split_shape = (length, HEADS, HEAD_DIM)
    queries = low(rotate(qkv[:, :D].reshape(split_shape), cosine, sine_tab))
    keys_rot = low(rotate(qkv[:, D:2 * D].reshape(split_shape), cosine, sine_tab))
    values = low(qkv[:, 2 * D:].reshape(split_shape))
    score_scale = HEAD_DIM ** (-0.5)
    scores = jnp.einsum('qhd,khd->hqk', queries, keys_rot, precision=lax.Precision.HIGHEST) * score_scale
    scores = low_back(scores)
    token_index = jnp.arange(length, dtype=jnp.int32)
    allowed = allowed_keys(seg_row, seg_row, token_index, token_index, valid_row)
    attn_probs = low(jax.nn.softmax(jnp.where(allowed[None], scores, -1e+30), axis=-1))
    mixed = jnp.einsum('hqk,khd->qhd', attn_probs, values, precision=lax.Precision.HIGHEST).reshape(length, D)
    mixed = low(low_back(mixed))
    attn_branch = matmul_hi(mixed, w_out) + b_out
    up_proj = low_back(matmul_hi(normed, w_up) + b_up)
    act = low(gelu_tanh(up_proj))
    mlp_branch = matmul_hi(act, w_down) + b_down
    return row_in + attn_branch + mlp_branch

def reference(hidden_in, segments, valid_mask, w_qkv, w_out, w_up, w_down, b_qkv, b_out, b_up, b_down, ln_gain, ln_shift, cotangent):
    params = tuple((weight_in.astype(jnp.float32) for weight_in in (w_qkv, w_out, w_up, w_down, b_qkv, b_out, b_up, b_down, ln_gain, ln_shift)))
    row_count = MICRO * ROWS
    inputs_f = hidden_in.astype(jnp.float32).reshape(row_count, LEN, D)
    seg_rows = segments.reshape(row_count, LEN)
    valid_rows = valid_mask.reshape(row_count, LEN)
    cot_f = cotangent.astype(jnp.float32).reshape(row_count, LEN, D)
    row_step = jax.checkpoint(row_forward)

    def forward(weights, inputs):

        def scan_step(carried, row_item):
            return (carried, row_step(weights, row_item[0], row_item[1], row_item[2]))
        _, outputs = lax.scan(scan_step, None, (inputs, seg_rows, valid_rows))
        return outputs
    outputs, pull_back = jax.vjp(forward, params, inputs_f)
    weight_grads, input_grad = pull_back(cot_f)
    out_hidden = outputs.astype(jnp.bfloat16).reshape(MICRO, ROWS, LEN, D)
    grad_input = input_grad.reshape(MICRO, ROWS, LEN, D)
    return (out_hidden, grad_input, weight_grads[0], weight_grads[1], weight_grads[2], weight_grads[3], weight_grads[4], weight_grads[5], weight_grads[6], weight_grads[7], weight_grads[8], weight_grads[9])
```

```python
import jax
import jax.numpy as jnp
from jax import lax
from jax.sharding import PartitionSpec as P

HEAD_DIM = 64
ROT = 32
NZ = 4
BF = jnp.bfloat16
F32 = jnp.float32


def doc_positions(seg_row):
    length = seg_row.shape[-1]
    token_index = jnp.arange(length, dtype=jnp.int32)
    previous = jnp.concatenate([seg_row[..., :1], seg_row[..., :-1]], axis=-1)
    starts = jnp.where((token_index == 0) | (seg_row != previous), token_index, 0)
    doc_start = lax.cummax(starts, axis=seg_row.ndim - 1)
    return token_index - doc_start


def rotary_tables(positions):
    half_dim = ROT // 2
    frequency = 10000.0 ** (-jnp.arange(half_dim, dtype=F32) * 2.0 / ROT)
    angles = positions.astype(F32)[..., None] * frequency
    return (jnp.cos(angles), jnp.sin(angles))


def rotate(tensor, cosine, sine_tab):
    half_dim = cosine.shape[-1]
    cos_b = cosine[..., None, :]
    sin_b = sine_tab[..., None, :]
    first_half = tensor[..., :half_dim]
    second = tensor[..., half_dim : 2 * half_dim]
    passed = tensor[..., 2 * half_dim :]
    return jnp.concatenate(
        [first_half * cos_b - second * sin_b, second * cos_b + first_half * sin_b, passed], axis=-1
    )


def gelu_tanh(values_in):
    return jax.nn.gelu(values_in, approximate=True)


def send_z(value, step):
    return lax.ppermute(value, "seq", [(i, (i + step) % NZ) for i in range(NZ)])


def send_dp(value, dx, dy, dc):
    pairs = []
    for x in range(4):
        for y in range(4):
            for c in range(2):
                to = (((x + dx) % 4) * 4 + (y + dy) % 4) * 2 + (c + dc) % 2
                pairs.append(((x * 4 + y) * 2 + c, to))
    return lax.ppermute(value, "dp", pairs)


def gather_ring(first, second, send):
    up0, up1 = send(first, 1), send(second, 1)
    down0, down1 = send(first, -1), send(second, -1)
    far0, far1 = send(up0, 1), send(down1, -1)
    return (first, down0, far0, up0), (second, down1, far1, up1)


def reduce_ring(first, second, send):
    far0, far1 = send(first[2], 1), send(second[2], -1)

    def add(left, right):
        return (left.astype(F32) + right.astype(F32)).astype(BF)

    to_up = (add(first[1], far0), second[1])
    to_down = (first[3], add(second[3], far1))
    got_up = [send(v, 1) for v in to_up]
    got_down = [send(v, -1) for v in to_down]
    return [
        own.astype(F32) + left.astype(F32) + right.astype(F32)
        for own, left, right in zip((first[0], second[0]), got_up, got_down)
    ]


def reduce_dp(grads, place):
    x, y, c = place
    rows, cols = grads.shape[0] // 32, grads.shape[1]
    split = grads.reshape(16, 2, rows, cols)
    own = lax.dynamic_index_in_dim(split, c, 1, keepdims=False)
    other = lax.dynamic_index_in_dim(split, 1 - c, 1, keepdims=False)
    got = send_dp(other, 0, 0, 1)
    mine = (own.astype(F32) + got.astype(F32)).astype(BF).reshape(4, 4, rows, cols)
    half = cols // 2
    left, right = mine[..., :half], mine[..., half:]

    def chunks(value, at, dim):
        return [
            lax.dynamic_index_in_dim(value, (at + k) % 4, dim, keepdims=False) for k in range(4)
        ]

    def ring(value, at, dim, send):
        parts = chunks(value, at, dim)
        mid = parts[0].shape[0] // 2
        lo, hi = [p[:mid] for p in parts], [p[mid:] for p in parts]
        return jnp.concatenate(reduce_ring(lo, hi, send), axis=0)

    def along_x(value, step):
        return send_dp(value, step, 0, 0)

    def along_y(value, step):
        return send_dp(value, 0, step, 0)

    left = ring(left, x, 0, along_x).astype(BF)
    right = ring(right, y, 1, along_y).astype(BF)
    left = left.reshape(4, rows, half)
    right = right.reshape(4, rows, half)

    def ring2(value, at, send):
        parts = chunks(value, at, 0)
        mid = rows // 2
        lo, hi = [p[:mid] for p in parts], [p[mid:] for p in parts]
        return jnp.concatenate(reduce_ring(lo, hi, send), axis=0)

    left = ring2(left, y, along_y)
    right = ring2(right, x, along_x)
    return jnp.concatenate([left, right], axis=1)


def body(
    hidden_in,
    segments,
    valid_mask,
    w_qkv,
    w_out,
    w_up,
    w_down,
    b_qkv,
    b_out,
    b_up,
    b_down,
    ln_gain,
    ln_shift,
    cotangent,
):
    z = lax.axis_index("seq")
    dp = lax.axis_index("dp")
    place = (dp // 8, (dp // 2) % 4, dp % 2)
    micro_count, _, group, width = hidden_in.shape
    row_len = group * NZ
    head_count = 4

    up_cols = w_up.reshape(8, 32, 4, 32).transpose(2, 0, 1, 3).reshape(4, 8, 1024)
    qkv_cols = w_qkv.reshape(8, 3, 4, 4, 64).transpose(3, 0, 1, 2, 4).reshape(4, 8, 768)
    vectors = jnp.concatenate([b_qkv, b_out, b_up, b_down, ln_gain, ln_shift])
    vec_block = jnp.zeros((8, 128), BF).at[0, :88].set(vectors)
    outgoing = jnp.concatenate(
        [up_cols, qkv_cols, jnp.broadcast_to(vec_block, (4, 8, 128))], axis=-1
    )
    incoming = lax.all_to_all(outgoing, "seq", 0, 0, tiled=True).reshape(32, 1920)
    to_heads, from_heads = [], []
    for a in range(4):
        for zt in range(4):
            for b in range(2):
                for zs in range(4):
                    source = (8 * a + 2 * zt + b) * 4 + zs
                    target = (8 * a + 4 * b + zs) * 4 + zt
                    to_heads.append((source, target))
                    from_heads.append((target, source))
    w_out_rows = lax.ppermute(w_out, ("dp", "seq"), to_heads)
    w_out_rows = w_out_rows.reshape(8, 4, 256).transpose(1, 0, 2).reshape(32, 256)
    payload = jnp.concatenate([incoming[:, :1792], w_down, w_out_rows, incoming[:, 1792:]], axis=1)
    weights = lax.all_gather(payload, "dp", axis=0, tiled=True)

    hid = gather_ring(hidden_in[0, 0], hidden_in[1, 0], send_z)
    hidden = jnp.stack([jnp.concatenate(h, axis=0) for h in hid])
    cot = gather_ring(cotangent[0, 0], cotangent[1, 0], send_z)
    cot = jnp.stack([jnp.concatenate(h, axis=0) for h in cot])

    w_in = weights[:, :1792]
    w_dn = weights[:, 1792:2816]
    w_o = weights[:, 2816:3072].reshape(32, 4, 8, 256).transpose(0, 2, 1, 3).reshape(256, 1024)
    vecs = weights[:, 3072:].reshape(32, 4, 8, 128)[:, :, 0, :88].astype(F32)
    bq = lax.dynamic_index_in_dim(vecs[..., :24].reshape(3, 4, 4, 64), z, 2, keepdims=False)
    bq = bq.reshape(768)
    b_sum = (vecs[..., 24:32] + vecs[..., 64:72]).reshape(width)
    bu = lax.dynamic_index_in_dim(vecs[..., 32:64], z, 1, keepdims=False).reshape(1024)
    gain = vecs[..., 72:80].reshape(width)
    shift = vecs[..., 80:88].reshape(width)

    inputs_f = hidden.astype(F32)
    average = jnp.mean(inputs_f, axis=-1, keepdims=True)
    centered = inputs_f - average
    spread = jnp.mean(centered * centered, axis=-1, keepdims=True)
    rs = lax.rsqrt(spread + 1e-05)
    xhat = centered * rs
    normed = (xhat * gain + shift).astype(BF)

    both = jnp.dot(normed, w_in, preferred_element_type=F32)
    up_f = both[..., :1024] + bu
    qkv = both[..., 1024:] + bq

    order = (z * group + jnp.arange(row_len, dtype=jnp.int32)) % row_len
    seg_all = segments[:, 0]

    def turned(rows):
        return lax.dynamic_slice_in_dim(
            jnp.concatenate([rows, rows], axis=1), z * group, row_len, 1
        )

    seg = turned(seg_all)
    valid = turned(valid_mask[:, 0])
    cosine, sine_tab = rotary_tables(turned(doc_positions(seg_all)))

    def rotate_local(tensor):
        return rotate(tensor, cosine, sine_tab)

    split = (micro_count, row_len, head_count, HEAD_DIM)
    raw_q = qkv[..., :256].reshape(split)
    raw_k = qkv[..., 256:512].reshape(split)
    queries = rotate_local(raw_q).astype(BF)
    keys = rotate_local(raw_k).astype(BF)
    values = qkv[..., 512:].astype(BF).reshape(split)
    scale = HEAD_DIM ** (-0.5)

    d_mixed = jnp.einsum("mcj,ij->mci", cot, w_o, preferred_element_type=F32).astype(BF)
    d_heads = d_mixed.reshape(split)
    d_act = jnp.einsum("mcj,ij->mci", cot, w_dn, preferred_element_type=F32)
    act = gelu_tanh(up_f).astype(BF)
    _, gelu_pull = jax.vjp(gelu_tanh, up_f)
    d_up = gelu_pull(d_act)[0].astype(BF)

    mixed, d_q, d_k, d_v = [], [], [], []
    for m in range(micro_count):
        allowed = (
            (seg[m][:, None] == seg[m][None, :])
            & (order[None, :] <= order[:, None])
            & ((valid[m][None, :] > 0) | (order[None, :] == order[:, None]))
        )
        scores = jnp.einsum("qhd,khd->hqk", queries[m], keys[m], preferred_element_type=F32) * scale
        masked = jnp.where(allowed[None], scores, -1e30)
        top = jnp.max(masked, axis=-1, keepdims=True)
        ex = jnp.exp(masked - top)
        probs = ex / jnp.sum(ex, axis=-1, keepdims=True)
        low = probs.astype(BF)
        mixed.append(
            jnp.einsum("hqk,khd->qhd", low, values[m], preferred_element_type=F32).reshape(
                row_len, 256
            )
        )
        d_probs = jnp.einsum("qhd,khd->hqk", d_heads[m], values[m], preferred_element_type=F32)
        total = jnp.sum(probs * d_probs, axis=-1, keepdims=True)
        d_scores = (probs * (d_probs - total)).astype(BF)
        d_q.append(
            jnp.einsum("hqk,khd->qhd", d_scores, keys[m], preferred_element_type=F32) * scale
        )
        d_k.append(
            jnp.einsum("hqk,qhd->khd", d_scores, queries[m], preferred_element_type=F32) * scale
        )
        d_v.append(jnp.einsum("hqk,qhd->khd", low, d_heads[m], preferred_element_type=F32))
    mixed = jnp.stack(mixed).astype(BF)
    _, rotate_pull = jax.vjp(rotate_local, raw_q)
    flat = (micro_count, row_len, 256)
    d_qkv = jnp.concatenate(
        [
            rotate_pull(jnp.stack(d_q))[0].reshape(flat),
            rotate_pull(jnp.stack(d_k))[0].reshape(flat),
            jnp.stack(d_v).reshape(flat),
        ],
        axis=-1,
    ).astype(BF)

    partial = jnp.dot(act, w_dn, preferred_element_type=F32) + jnp.dot(
        mixed, w_o, preferred_element_type=F32
    )
    partial = partial.astype(BF).reshape(micro_count, NZ, group, width)
    sums = reduce_ring([partial[0, k] for k in range(NZ)], [partial[1, k] for k in range(NZ)], send_z)
    out_hidden = (hidden_in.astype(F32) + (jnp.stack(sums) + b_sum)[:, None]).astype(BF)

    grad_mlp = jnp.concatenate(
        [
            jnp.einsum("mci,mcj->ij", normed, d_up, preferred_element_type=F32).astype(BF),
            jnp.einsum("mci,mcj->ij", act, cot, preferred_element_type=F32).astype(BF),
        ],
        axis=1,
    )
    grad_qkv = jnp.einsum("mci,mcj->ij", normed, d_qkv, preferred_element_type=F32).astype(BF)
    grad_out = jnp.einsum("mci,mcj->ij", mixed, cot, preferred_element_type=F32).astype(BF)
    grad_out = grad_out.reshape(32, 8, 4, 256).transpose(0, 2, 1, 3).reshape(1024, 256)

    d_normed = jnp.einsum("mcj,ij->mci", d_up, w_in[:, :1024], preferred_element_type=F32)
    d_normed = d_normed + jnp.einsum("mcj,ij->mci", d_qkv, w_in[:, 1024:], preferred_element_type=F32)
    sum_gain = jnp.sum(d_normed * xhat, axis=(0, 1))
    sum_shift = jnp.sum(d_normed, axis=(0, 1))
    sum_bqkv = jnp.sum(d_qkv.astype(F32), axis=(0, 1)).reshape(3, 4, 1, 64)
    sum_bup = jnp.sum(d_up.astype(F32), axis=(0, 1)).reshape(32, 1, 32)
    sum_cot = jnp.sum(cotangent.astype(F32), axis=(0, 1, 2)).reshape(32, 4, 8)
    mine = jnp.arange(4) == z
    sum_bqkv = jnp.where(mine[None, None, :, None], sum_bqkv, 0.0).reshape(32, 4, 24)
    sum_bup = jnp.where(mine[None, :, None], sum_bup, 0.0)
    vec_grads = jnp.concatenate(
        [
            sum_bqkv,
            sum_cot,
            sum_bup,
            sum_cot,
            sum_gain.reshape(32, 4, 8),
            sum_shift.reshape(32, 4, 8),
        ],
        axis=-1,
    ).astype(BF)
    vec_grads = jnp.pad(vec_grads[:, :, None, :], ((0, 0), (0, 0), (0, 7), (0, 40)))
    grad_att = jnp.concatenate([grad_qkv, grad_out, vec_grads.reshape(1024, 128)], axis=1)

    d_part = d_normed.astype(BF).reshape(micro_count, NZ, group, width)
    d_sums = reduce_ring([d_part[0, k] for k in range(NZ)], [d_part[1, k] for k in range(NZ)], send_z)
    own_xhat = xhat[:, :group]
    own_r = rs[:, :group]
    grads_n = jnp.stack(d_sums) * gain
    mean_g = jnp.mean(grads_n, axis=-1, keepdims=True)
    mean_gx = jnp.mean(grads_n * own_xhat, axis=-1, keepdims=True)
    grad_input = cotangent.astype(F32) + (own_r * (grads_n - mean_g - own_xhat * mean_gx))[:, None]

    red_mlp = reduce_dp(grad_mlp, place)
    red_att = reduce_dp(grad_att, place)
    final_down = red_mlp[:, 1024:]
    back = jnp.concatenate([red_mlp[:, :1024], red_att[:, :768], red_att[:, 1024:]], axis=1)
    back = lax.all_to_all(back.reshape(4, 8, 1920), "seq", 0, 0, tiled=True)
    final_up = back[..., :1024].reshape(4, 8, 32, 32).transpose(1, 2, 0, 3).reshape(8, 4096)
    final_qkv = back[..., 1024:1792].reshape(4, 8, 3, 4, 64).transpose(1, 2, 3, 0, 4)
    final_qkv = final_qkv.reshape(8, 3072)
    final_vec = jnp.sum(back[:, 0, 1792:1880], axis=0)
    final_out = red_att[:, 768:1024].reshape(4, 8, 256).transpose(1, 0, 2).reshape(8, 1024)
    final_out = lax.ppermute(final_out, ("dp", "seq"), from_heads)
    return (
        out_hidden,
        grad_input,
        final_qkv,
        final_out,
        final_up,
        final_down,
        final_vec[:24],
        final_vec[24:32],
        final_vec[32:64],
        final_vec[64:72],
        final_vec[72:80],
        final_vec[80:88],
    )


def solution(mesh):
    rows = P(None, "dp", "seq", None)
    tokens = P(None, "dp", None)
    matrix = P(("dp", "seq"), None)
    vector = P(("dp", "seq"))
    in_specs = (rows, tokens, tokens) + (matrix,) * 4 + (vector,) * 6 + (rows,)
    out_specs = (rows, rows) + (matrix,) * 4 + (vector,) * 6
    return jax.shard_map(body, mesh=mesh, in_specs=in_specs, out_specs=out_specs, check_vma=False)
```

```python
import jax
import jax.numpy as jnp
from jax import lax
from jax.experimental import pallas as pl
from jax.experimental.pallas import tpu as pltpu
from jax.sharding import PartitionSpec as P

BF = jnp.bfloat16
F32 = jnp.float32
MB = 1 << 20
HEAD_DIM = 64
ROT = 32
NZ = 4


def dot(left, right):
    return jnp.dot(left, right, preferred_element_type=F32)


def dot_nt(left, right):
    return lax.dot_general(left, right, (((1,), (1,)), ((), ())), preferred_element_type=F32)


def dot_tn(left, right):
    return lax.dot_general(left, right, (((0,), (0,)), ((), ())), preferred_element_type=F32)


def turn(value, cos, sin, sign):
    cos, sin = [jnp.concatenate([t, t], axis=1) for t in (cos, sin)]
    width = value.shape[1]
    right, left = pltpu.roll(value, 16, 1), pltpu.roll(value, width - 16, 1)
    first = lax.broadcasted_iota(jnp.int32, value.shape, 1) % 32 < 16
    return value * cos + jnp.where(first, left, right) * (sign * sin)


def spread(value, period):
    while period < 128:
        value = value + pltpu.roll(value, period, 1)
        period *= 2
    return value


def lay_out(value, period):
    fold = 128 // period
    lane = lax.broadcasted_iota(jnp.int32, value.shape, 1) // period
    row = lax.broadcasted_iota(jnp.int32, value.shape, 0) % fold
    value = jnp.where(lane == row, spread(value, period), 0.0)
    value = jnp.sum(value.reshape(8, fold, 128), axis=1)
    return jnp.concatenate([value[t : t + 1] for t in range(8)], axis=1)


def unpack_parameters(z, w_ref, wo_ref, vec_ref, block_s):
    rows = w_ref[:, 2816:3072].astype(F32).reshape(32, 4, 8, 256)
    for b in range(4):
        wo_ref[:, b * 256 : b * 256 + 256] = rows[:, b].reshape(256, 256).astype(BF)
    block_s[...] = w_ref[:, 3072:3200].astype(F32)

    def kind(k, first=0, count=128):
        return block_s[pl.ds(first * 8 + k, count, stride=8), :]

    vec_ref[0:1, :] = lay_out(kind(4), 8)
    vec_ref[1:2, :] = lay_out(kind(5), 8)
    vec_ref[2:3, :] = lay_out(kind(2, z * 32, 32), 32)
    vec_ref[4:5, :] = lay_out(kind(1) + kind(3), 8)
    lane = lax.broadcasted_iota(jnp.int32, (128, 128), 1)
    row = lax.broadcasted_iota(jnp.int32, (128, 128), 0)
    qkv = kind(0)
    groups = []
    for g in range(3):
        here = jnp.where(lane < 8, pltpu.roll(qkv, 128 - 8 * g, 1) if g else qkv, 0.0)
        groups.append(spread(here, 8))
    for part in range(3):
        for half in range(2):
            want = (part * 8 + z * 2 + half) * 16 + lane // 8
            total = jnp.zeros((128, 128), F32)
            for g in range(3):
                total = total + jnp.where(3 * row + g == want, groups[g], 0.0)
            at = part * 256 + half * 128
            vec_ref[3:4, at : at + 128] = jnp.sum(total, axis=0, keepdims=True)


def front_kernel(z_ref, *rest):
    z = z_ref[0]
    step = pl.program_id(0)
    x_ref, c_ref, n_ref, act_ref, dup_ref, q_ref, k_ref, v_ref, dm_ref, stat_ref, sum_ref = rest[
        -14:-3
    ]
    wo_ref, vec_ref, block_s = rest[-3:]
    if rest[0].shape[0] == 1:
        tile = x_ref.shape[1]
        pieces, (w_ref, wo_ref, vec_ref, cos_ref, sin_ref) = rest[:1], rest[1:6]
        x_ref[0], c_ref[0] = pieces[0][0, :tile], pieces[0][0, tile:]
    else:
        tile = x_ref.shape[1]
        pieces, (w_ref, cos_ref, sin_ref) = rest[:NZ], rest[NZ : NZ + 3]
        for at, piece in enumerate(pieces):

            @pl.when(step == at)
            def _(piece=piece):
                x_ref[0], c_ref[0] = piece[:tile], piece[tile:]

        @pl.when(step == 0)
        def _():
            unpack_parameters(z, w_ref, wo_ref, vec_ref, block_s)

    gain_ref, shift_ref, bu_ref, bq_ref = [vec_ref.at[k : k + 1] for k in range(4)]

    @pl.when(step == 0)
    def _():
        sum_ref[...] = jnp.zeros_like(sum_ref)

    def put(ref, value):
        for r in range(tile // 256):
            row = lax.rem(pl.program_id(0) * (tile // 256) + r + z, 4) * 256
            ref[0, pl.ds(pl.multiple_of(row, 256), 256), :] = value[r * 256 : r * 256 + 256]

    def d_act_of(j):
        return dot_nt(c_ref[0], w_ref[j * 256 : j * 256 + 256, 1792:2816])

    def in_of(j):
        return dot(n_ref[0], w_ref[:, j * 256 : j * 256 + 256])

    d_act = d_act_of(0)
    d_mixed = dot_nt(c_ref[0], wo_ref[...])
    x = x_ref[0].astype(F32)
    average = jnp.mean(x, axis=-1, keepdims=True)
    centered = x - average
    spread = jnp.mean(centered * centered, axis=-1, keepdims=True)
    rs = lax.rsqrt(spread + 1e-05)
    stat_ref[0, :, 0:1] = average
    stat_ref[0, :, 1:2] = rs
    n_ref[0] = (centered * rs * gain_ref[...] + shift_ref[...]).astype(BF)
    put(dm_ref, d_mixed.astype(BF))
    up = in_of(0)
    k0 = 0.7978845608028654
    k1 = k0 * 0.044715
    for j in range(4):
        cols = slice(j * 256, j * 256 + 256)
        if j < 3:
            next_up, next_act = in_of(j + 1), d_act_of(j + 1)
        else:
            q, k, v = in_of(4), in_of(5), in_of(6)
        up = up + bu_ref[:, cols]
        square = up * up
        half = 0.5 + 0.5 * jnp.tanh(up * (k0 + k1 * square))
        act = up * half
        slope = half + 2.0 * act * (1.0 - half) * (k0 + 3.0 * k1 * square)
        d_up = (slope * d_act).astype(BF)
        act_ref[0, :, cols] = act.astype(BF)
        dup_ref[0, :, cols] = d_up
        back = d_up.astype(F32)
        sum_ref[:, cols] += jnp.sum(back.reshape(back.shape[0] // 8, 8, 256), axis=0)
        up, d_act = next_up, next_act
    tabs = (cos_ref[0], sin_ref[0])
    q = turn(q + bq_ref[:, 0:256], *tabs, 1.0).astype(BF) * BF(0.125)
    put(q_ref, q)
    put(k_ref, turn(k + bq_ref[:, 256:512], *tabs, 1.0).astype(BF))
    put(v_ref, (v + bq_ref[:, 512:768]).astype(BF))


ANY = pl.BlockSpec(memory_space=pl.ANY)


def front(z, pieces, weights, known, cos, sin, after):
    tile, d = pieces[0].shape[-2] // 2, pieces[0].shape[-1]
    n = tile * NZ

    def tok(width):
        return pl.BlockSpec((1, tile, width), lambda j, z: (0, j, 0))

    def turned(width):
        return pl.BlockSpec((1, tile, width), lambda j, z: (0, lax.rem(j + z[0], NZ), 0))

    def row(width):
        return pl.BlockSpec((1, n, width), lambda j, z: (0, 0, 0))

    def whole(a):
        return pl.BlockSpec(a.shape, lambda j, z: (0, 0), pipeline_mode=pl.Buffered(1))

    def keep(*shape):
        return pl.BlockSpec(shape, lambda j, z: (0, 0))

    if len(pieces) == 1:
        first = [pl.BlockSpec((1, 2 * tile, d), lambda j, z: (lax.rem(j + z[0], NZ), 0, 0))]
    else:
        first = [whole(a) for a in pieces]
    fixed = (weights, *known)
    out_specs = [tok(d)] * 5 + [row(256)] * 4 + [tok(128), keep(8, 1024)]
    out_shape = [jax.ShapeDtypeStruct((1, n, w), BF) for w in [d] * 5 + [256] * 4]
    out_shape += [jax.ShapeDtypeStruct((1, n, 128), F32), jax.ShapeDtypeStruct((8, 1024), F32)]
    scratch = [pltpu.VMEM((256, d), BF), pltpu.VMEM((8, d), F32)]
    if not known:
        out_specs += [keep(256, d), keep(8, d)]
        out_shape += [jax.ShapeDtypeStruct((256, d), BF), jax.ShapeDtypeStruct((8, d), F32)]
        scratch = []
    return pl.pallas_call(
        front_kernel,
        grid_spec=pltpu.PrefetchScalarGridSpec(
            num_scalar_prefetch=1,
            grid=(NZ,),
            in_specs=first + [whole(a) for a in fixed] + [turned(128)] * 2 + [ANY] * len(after),
            out_specs=out_specs,
            scratch_shapes=scratch + [pltpu.VMEM((1024, 128), F32)],
        ),
        out_shape=out_shape,
        compiler_params=pltpu.CompilerParams(vmem_limit_bytes=58 * MB),
        cost_estimate=pl.CostEstimate(
            flops=2 * n * d * 3072, bytes_accessed=20 * MB, transcendentals=0
        ),
        name="front",
    )(z, *pieces, *fixed, cos, sin, *after)


def attend_kernel(
    z_ref, q_ref, k_ref, v_ref, dm_ref, row_ref, key_ref, cos_ref, sin_ref, *rest,
):
    mixed_ref, dqkv_ref, sum_ref, bias_s, s_s, dp_s, p_s, ds_s, qm_s, dmm_s, dk_s, dv_s = rest[-12:]
    B = 256
    z = z_ref[0]

    sum_ref[...] = jnp.zeros_like(sum_ref)

    def put(lo, hi, a, value):
        row = lax.rem(a - z + 4, 4) * B
        if hi is None:
            mixed_ref[0, pl.ds(pl.multiple_of(row, B), B), :] = value
        else:
            dqkv_ref[0, pl.ds(pl.multiple_of(row, B), B), lo:hi] = value
            sum_ref[0:1, lo:hi] += jnp.sum(value.astype(F32), axis=0, keepdims=True)

    key_col = key_ref[0].T
    lane_head = lax.broadcasted_iota(jnp.int32, (B, B), 1) // 64
    diff = lax.broadcasted_iota(jnp.int32, (B, B), 0) - lax.broadcasted_iota(jnp.int32, (B, B), 1)

    def prepare(aq):
        par, n, here = aq % 2, (aq + 1) * B, slice(aq * B, aq * B + B)
        bias = jnp.where(key_col[0:n, 0:1] == row_ref[0, 0:1, here], 0.0, -1e30)
        if aq:
            bias_s[par, 0 : aq * B, :] = bias[: aq * B]
        edge = jnp.where(diff <= 0, bias[aq * B :], -1e30)
        bias_s[par, here, :] = jnp.where(diff == 0, 0.0, edge)
        q_all, d_all = q_ref[0, here, :], dm_ref[0, here, :]
        for h in range(4):
            cols = slice(h * B, h * B + B)
            qm_s[par, cols, :] = jnp.where(lane_head == h, q_all, jnp.zeros_like(q_all))
            dmm_s[par, cols, :] = jnp.where(lane_head == h, d_all, jnp.zeros_like(d_all))

    def products(aq, h):
        par, n, cols = aq % 2, (aq + 1) * B, slice(h * B, h * B + B)
        s = dot_nt(k_ref[0, 0:n, :], qm_s[par, cols, :]) + bias_s[par, 0:n, :]
        s_s[h % 2, 0:n] = s
        dp_s[h % 2, 0:n] = dot_nt(v_ref[0, 0:n, :], dmm_s[par, cols, :])
        return jnp.max(s, axis=0, keepdims=True)

    def soften(aq, h, top):
        par, n, cols = aq % 2, (aq + 1) * B, slice(h * B, h * B + B)
        e = jnp.exp(s_s[h % 2, 0:n] - top)
        s_s[h % 2, 0:n] = e
        inv = 1.0 / jnp.sum(e, axis=0, keepdims=True)
        mean = jnp.sum(e * dp_s[h % 2, 0:n], axis=0, keepdims=True) * inv
        p = s_s[h % 2, 0:n] * inv
        p_s[par, 0:n, cols] = p.astype(BF)
        ds_s[par, 0:n, cols] = (p * (dp_s[h % 2, 0:n] - mean)).astype(BF)

    def pick(value):
        out = value[0:B]
        for h in range(1, 4):
            out = jnp.where(lane_head == h, value[h * B : h * B + B], out)
        return out

    def gather(aq, part):
        par, n, here = aq % 2, (aq + 1) * B, slice(aq * B, aq * B + B)
        if part == 0:
            put(None, None, aq, pick(dot_tn(p_s[par, 0:n, :], v_ref[0, 0:n, :])).astype(BF))
        elif part == 1:
            dq = pick(dot_tn(ds_s[par, 0:n, :], k_ref[0, 0:n, :])) * 0.125
            tabs = (cos_ref[0, here, :], sin_ref[0, here, :])
            put(0, 256, aq, turn(dq, *tabs, -1.0).astype(BF))
        else:
            left, right, to = (p_s, dmm_s, dv_s) if part == 2 else (ds_s, qm_s, dk_s)
            value = dot(left[par, 0:n, :], right[par])
            if aq:
                to[0 : aq * B, :] += value[: aq * B]
            to[here, :] = value[aq * B :]

    prepare(0)
    top = products(0, 0)
    for aq in range(4):
        for h in range(4):
            if aq:
                gather(aq - 1, h)
            ahead = None
            if h < 3:
                ahead = products(aq, h + 1)
            elif aq < 3:
                prepare(aq + 1)
                ahead = products(aq + 1, 0)
            soften(aq, h, top)
            top = ahead
    for part in range(4):
        gather(3, part)
    for a in range(4):
        here = slice(a * B, a * B + B)
        tabs = (cos_ref[0, here, :], sin_ref[0, here, :])
        put(256, 512, a, turn(dk_s[here, :], *tabs, -1.0).astype(BF))
        put(512, 768, a, dv_s[here, :].astype(BF))


def attend(z, q, k, v, dm, seg_row, seg_key, cos, sin, after):
    n = q.shape[1]

    def tok(width):
        return pl.BlockSpec((1, n, width), lambda i, z: (0, 0, 0))

    def out(width):
        return pl.BlockSpec((1, n, width), lambda i, z: (0, 0, 0))

    S = pltpu.VMEM
    return pl.pallas_call(
        attend_kernel,
        grid_spec=pltpu.PrefetchScalarGridSpec(
            num_scalar_prefetch=1,
            grid=(1,),
            in_specs=[tok(256)] * 4
            + [pl.BlockSpec((1, 8, n), lambda i, z: (0, 0, 0))] * 2
            + [tok(128)] * 2
            + [ANY] * len(after),
            out_specs=[out(256), out(768), pl.BlockSpec((8, 768), lambda i, z: (0, 0))],
            scratch_shapes=[
                S((2, 1024, 256), F32), S((2, 1024, 256), F32), S((2, 1024, 256), F32),
                S((2, 1024, 1024), BF), S((2, 1024, 1024), BF),
                S((2, 1024, 256), BF), S((2, 1024, 256), BF),
                S((1024, 256), F32), S((1024, 256), F32),
            ],
        ),
        out_shape=[
            jax.ShapeDtypeStruct((1, n, 256), BF),
            jax.ShapeDtypeStruct((1, n, 768), BF),
            jax.ShapeDtypeStruct((8, 768), F32),
        ],
        compiler_params=pltpu.CompilerParams(vmem_limit_bytes=58 * MB),
        cost_estimate=pl.CostEstimate(
            flops=15 * 10**9, bytes_accessed=10 * MB, transcendentals=0
        ),
        name="attend",
    )(z, q, k, v, dm, seg_row, seg_key, cos, sin, *after)


def back_kernel(
    z_ref, act_ref, mix_ref, dup_ref, dqkv_ref, x_ref, stat_ref, wd_ref, wo_ref, wi_ref, *rest,
):
    cut, gain_ref, shift_ref = rest[-3:]
    z = z_ref[0]
    out = dot(act_ref[0], wd_ref[...]) + dot(mix_ref[0], wo_ref[...])
    dn = dot_nt(dup_ref[0], wi_ref[:, 0:1024]) + dot_nt(dqkv_ref[0], wi_ref[:, 1024:1792])
    xhat = (x_ref[0].astype(F32) - stat_ref[0, :, 0:1]) * stat_ref[0, :, 1:2]
    gain_ref[...] = jnp.sum((dn * xhat).reshape(-1, 8, 256), axis=0)
    shift_ref[...] = jnp.sum(dn.reshape(-1, 8, 256), axis=0)
    for r in range(NZ):
        rows = slice(r * 256, r * 256 + 256)
        first = pl.multiple_of(lax.rem(r + z, NZ) * 512, 512)
        cut[pl.ds(first, 256), :] = out[rows].astype(BF)
        cut[pl.ds(first + 256, 256), :] = dn[rows].astype(BF)


def back(z, act, mixed, d_up, d_qkv, x, stat, weights, w_o, after):
    def rows(a):
        return pl.BlockSpec(a.shape, lambda j, z: (0, 0, 0), pipeline_mode=pl.Buffered(1))

    def cols(n, first=0):
        return pl.BlockSpec((n, 256), lambda j, z: (0, first + j))

    return pl.pallas_call(
        back_kernel,
        grid_spec=pltpu.PrefetchScalarGridSpec(
            num_scalar_prefetch=1,
            grid=(4,),
            in_specs=[rows(a) for a in (act, mixed, d_up, d_qkv)]
            + [
                pl.BlockSpec((1, 1024, 256), lambda j, z: (0, 0, j)),
                rows(stat),
                cols(1024, 7),
                cols(256),
                pl.BlockSpec((256, 1792), lambda j, z: (j, 0)),
            ]
            + [ANY] * len(after),
            out_specs=[cols(2048)] + [cols(8)] * 2,
        ),
        out_shape=[jax.ShapeDtypeStruct((2048, 1024), BF)]
        + [jax.ShapeDtypeStruct((8, 1024), F32)] * 2,
        compiler_params=pltpu.CompilerParams(vmem_limit_bytes=58 * MB),
        cost_estimate=pl.CostEstimate(
            flops=2 * 1024 * 1024 * 3072, bytes_accessed=20 * MB, transcendentals=0
        ),
        name="back",
    )(z, act, mixed, d_up, d_qkv, x, stat, weights, w_o, weights, *after)


def put_halves(c, value, own_ref, other_ref, lo):
    value = value.reshape(4, 2, 32, value.shape[1])
    first, second = [value[:, k].reshape(128, value.shape[3]) for k in range(2)]
    hi = lo + value.shape[3]
    own_ref[:, lo:hi] = jnp.where(c == 0, first, second).astype(BF)
    other_ref[:, lo:hi] = jnp.where(c == 0, second, first).astype(BF)


def grads_mlp_kernel(
    c_ref, n0_ref, n1_ref, dup0_ref, dup1_ref, act0_ref, act1_ref, cot0_ref, cot1_ref, *rest,
):
    own_ref, other_ref = rest[-2:]
    c = c_ref[0]
    up = dot_tn(n0_ref[0], dup0_ref[0]) + dot_tn(n1_ref[0], dup1_ref[0])
    put_halves(c, up, own_ref, other_ref, 0)
    down = dot_tn(act0_ref[0], cot0_ref[0]) + dot_tn(act1_ref[0], cot1_ref[0])
    put_halves(c, down, own_ref, other_ref, 1024)


def grads_mlp(c, normed, d_up, act, cot, after):
    tokens, width = normed[0].shape[1:]

    def whole(a):
        return pl.BlockSpec(a.shape, lambda i, c: (0, 0, 0), pipeline_mode=pl.Buffered(1))

    part = pl.BlockSpec((1, tokens, 256), lambda i, c: (0, 0, i))
    return pl.pallas_call(
        grads_mlp_kernel,
        grid_spec=pltpu.PrefetchScalarGridSpec(
            num_scalar_prefetch=1,
            grid=(width // 256,),
            in_specs=[part] * 2
            + [whole(a) for a in d_up]
            + [part] * 2
            + [whole(a) for a in cot]
            + [ANY] * len(after),
            out_specs=[pl.BlockSpec((128, 2048), lambda i, c: (i, 0))] * 2,
        ),
        out_shape=[jax.ShapeDtypeStruct((width // 2, 2048), BF)] * 2,
        compiler_params=pltpu.CompilerParams(vmem_limit_bytes=58 * MB),
        cost_estimate=pl.CostEstimate(
            flops=8 * tokens * width * width, bytes_accessed=20 * MB, transcendentals=0
        ),
        name="grads_mlp",
    )(c, *normed, *d_up, *act, *cot, *after)


def grads_att_kernel(
    c_ref, n0_ref, n1_ref, dqkv0_ref, dqkv1_ref, mix0_ref, mix1_ref, cot0_ref, cot1_ref,
    *rest,
):
    own_ref, other_ref, out_s = rest[-3:]
    c = c_ref[0]
    i = pl.program_id(0)

    @pl.when(i == 0)
    def _():
        out_s[...] = dot_tn(mix0_ref[0], cot0_ref[0]) + dot_tn(mix1_ref[0], cot1_ref[0])

    both = dot_tn(n0_ref[0], dqkv0_ref[0]) + dot_tn(n1_ref[0], dqkv1_ref[0])
    put_halves(c, both, own_ref, other_ref, 0)
    rows = out_s[pl.ds(pl.multiple_of(i * 64, 64), 64), :]
    rows = [rows[d * 8 : d * 8 + 8, b * 256 : b * 256 + 256] for d in range(8) for b in range(4)]
    put_halves(c, jnp.concatenate(rows), own_ref, other_ref, 768)


def grads_att(c, normed, d_qkv, mixed, cot, after):
    tokens, width = normed[0].shape[1:]

    def whole(a):
        return pl.BlockSpec(a.shape, lambda i, c: (0,) * a.ndim, pipeline_mode=pl.Buffered(1))

    return pl.pallas_call(
        grads_att_kernel,
        grid_spec=pltpu.PrefetchScalarGridSpec(
            num_scalar_prefetch=1,
            grid=(4,),
            in_specs=[pl.BlockSpec((1, tokens, 256), lambda i, c: (0, 0, i))] * 2
            + [whole(a) for a in (*d_qkv, *mixed, *cot)]
            + [ANY] * len(after),
            out_specs=[pl.BlockSpec((128, 1024), lambda i, c: (i, 0))] * 2,
            scratch_shapes=[pltpu.VMEM((256, 1024), F32)],
        ),
        out_shape=[jax.ShapeDtypeStruct((512, 1024), BF)] * 2,
        compiler_params=pltpu.CompilerParams(vmem_limit_bytes=58 * MB),
        cost_estimate=pl.CostEstimate(
            flops=4 * tokens * width * 1024, bytes_accessed=16 * MB, transcendentals=0
        ),
        name="grads_att",
    )(c, *normed, *d_qkv, *mixed, *cot, *after)


def finish_kernel(
    x_ref, c_ref, vec_ref, *rest,
):
    parts, (out_ref, dx_ref) = rest[:-3], rest[-2:]
    x = x_ref[...].astype(F32)
    branch, g = [
        sum([p[k].astype(F32) for p in parts[1:]], parts[0][k].astype(F32)) for k in range(2)
    ]
    out_ref[...] = (x + (branch + vec_ref[4:5, :])).astype(BF)
    centered = x - jnp.mean(x, axis=-1, keepdims=True)
    rs = lax.rsqrt(jnp.mean(centered * centered, axis=-1, keepdims=True) + 1e-05)
    xhat = centered * rs
    g = g * vec_ref[0:1, :]
    mean_g = jnp.mean(g, axis=-1, keepdims=True)
    mean_gx = jnp.mean(g * xhat, axis=-1, keepdims=True)
    dx_ref[...] = c_ref[...].astype(F32) + rs * (g - mean_g - xhat * mean_gx)


def finish(x, cot, parts, vectors, after):
    n, d = x.shape
    tile = pl.BlockSpec((128, d), lambda i: (i, 0))
    row = pl.BlockSpec((8, d), lambda i: (0, 0))
    both = pl.BlockSpec((2, 128, d), lambda i: (0, i, 0))
    return pl.pallas_call(
        finish_kernel,
        grid=(n // 128,),
        in_specs=[tile] * 2 + [row] + [both] * len(parts) + [ANY],
        out_specs=[tile] * 2,
        out_shape=[jax.ShapeDtypeStruct((n, d), BF), jax.ShapeDtypeStruct((n, d), F32)],
        compiler_params=pltpu.CompilerParams(vmem_limit_bytes=32 * MB),
        name="finish",
    )(x, cot, vectors, *[p.reshape(2, n, d) for p in parts], after)


def add_kernel(a_ref, b_ref, after_ref, out_ref):
    out_ref[...] = (a_ref[...].astype(F32) + b_ref[...].astype(F32)).astype(BF)


def add_after(a, b, after):
    n, d = a.shape
    part = pl.BlockSpec((n // 4, d), lambda i: (i, 0))
    return pl.pallas_call(
        add_kernel,
        grid=(4,),
        in_specs=[part, part, ANY],
        out_specs=part,
        out_shape=jax.ShapeDtypeStruct((n, d), BF),
        compiler_params=pltpu.CompilerParams(vmem_limit_bytes=32 * MB),
        name="add_after",
    )(a, b, after)


def total_of(refs, rows):
    return sum([r[rows, :].astype(F32) for r in refs[1:]], refs[0][rows, :].astype(F32))


def to_x_kernel(at_ref, a_ref, b_ref, va_ref, vb_ref, *outs):
    x, c = at_ref[0], at_ref[1]
    for k, out in enumerate(outs):
        rows = pl.ds(pl.multiple_of(lax.rem(x + k, 4) * 128, 128), 128)
        out[:, 0:1024] = total_of((a_ref, b_ref), rows).astype(BF)
        rows = pl.ds(pl.multiple_of(lax.rem(x + k, 4) * 256, 256), 256)
        vec = (va_ref[rows, :] + vb_ref[rows, :]).reshape(4, 2, 32, 128)
        vec = jnp.where(c == 0, vec[:, 0], vec[:, 1])
        out[:, 1024:1152] = vec.reshape(128, 128).astype(BF)


def to_y_kernel(at_ref, mlp_ref, *refs):
    parts, outs = refs[:4], refs[4:]
    for k, out in enumerate(outs):
        rows = pl.ds(pl.multiple_of(lax.rem(at_ref[0] + k, 4) * 32, 32), 32)
        out[:, 0:2048] = mlp_ref[rows, :]
        out[:, 2048:3200] = total_of(parts, rows).astype(BF)


def to_z_kernel(a_ref, b_ref, c_ref, d_ref, after_ref, home_ref, rows_ref):
    total = total_of((a_ref, b_ref, c_ref, d_ref), slice(0, 32))
    home = jnp.concatenate([total[:, :1024], total[:, 2048:2816], total[:, 3072:3200]], axis=1)
    home_ref[...] = home.reshape(4, 8, 1920)
    rows_ref[0:32, :] = total[:, 1024:2048]
    out = total[:, 2816:3072].reshape(4, 8, 256)
    for b in range(4):
        rows_ref[32:40, b * 256 : b * 256 + 256] = out[b]


def home_kernel(home_ref, up_ref, qkv_ref, vec_ref):
    for k in range(NZ):
        up_ref[:, k * 1024 : k * 1024 + 1024] = home_ref[k, :, 0:1024]
        for part in range(3):
            at = part * 1024 + k * 256
            own = 1024 + part * 256
            qkv_ref[:, at : at + 256] = home_ref[k, :, own : own + 256]
    vec_ref[...] = jnp.sum(home_ref[:, :, 1792:1920], axis=0)


def in_vmem(kernel, name, operands, shapes, scalars=None, after=0):
    specs = [pl.BlockSpec(memory_space=pltpu.VMEM)] * (len(operands) - after) + [ANY] * after
    if scalars is not None:
        specs = [pl.BlockSpec(memory_space=pltpu.SMEM)] + specs
        operands = (scalars, *operands)
    return pl.pallas_call(
        kernel,
        in_specs=specs,
        out_specs=[pl.BlockSpec(memory_space=pltpu.VMEM)] * len(shapes),
        out_shape=[jax.ShapeDtypeStruct(*s) for s in shapes],
        compiler_params=pltpu.CompilerParams(vmem_limit_bytes=32 * MB),
        name=name,
    )(*operands)


def pack_kernel(a_ref, b_ref, after_ref, out_ref):
    out_ref[0] = a_ref[...]
    out_ref[1] = b_ref[...]


def pack(a, b, after):
    n, d = a.shape
    part = pl.BlockSpec((n // 2, d), lambda i: (i, 0))
    return pl.pallas_call(
        pack_kernel,
        grid=(2,),
        in_specs=[part, part, ANY],
        out_specs=pl.BlockSpec((2, n // 2, d), lambda i: (0, i, 0)),
        out_shape=jax.ShapeDtypeStruct((2, n, d), BF),
        name="pack",
    )(a, b, after).reshape(2 * n, d)


def doc_positions(seg_row):
    length = seg_row.shape[-1]
    token_index = jnp.arange(length, dtype=jnp.int32)
    previous = jnp.concatenate([seg_row[..., :1], seg_row[..., :-1]], axis=-1)
    starts = jnp.where((token_index == 0) | (seg_row != previous), token_index, 0)
    doc_start = lax.cummax(starts, axis=seg_row.ndim - 1)
    return token_index - doc_start


def rotary_tables(positions):
    dim = jnp.arange(128, dtype=jnp.int32) % HEAD_DIM
    frequency = 10000.0 ** (-(dim % (ROT // 2)).astype(F32) * 2.0 / ROT)
    frequency = jnp.where(dim < ROT, frequency, 0.0)
    angles = positions.astype(F32)[..., None] * frequency
    return jnp.cos(angles), jnp.sin(angles) * jnp.where(dim < ROT // 2, -1.0, 1.0)


def send(value, axis, step):
    size = lax.axis_size(axis)
    return lax.ppermute(value, axis, [(i, (i + step) % size) for i in range(size)])


def add(*values):
    return sum([v.astype(F32) for v in values[1:]], values[0].astype(F32))


def exchange(parts, axis):
    return [parts[0]] + [send(parts[k], axis, k) for k in range(1, 4)]


def body(
    hidden_in,
    segments,
    valid_mask,
    w_qkv,
    w_out,
    w_up,
    w_down,
    b_qkv,
    b_out,
    b_up,
    b_down,
    ln_gain,
    ln_shift,
    cotangent,
):
    z = lax.axis_index("z")
    c = lax.axis_index("c").astype(jnp.int32).reshape(1)
    micro_count, _, group, width = hidden_in.shape
    row_len = group * NZ
    z_arr = z.astype(jnp.int32).reshape(1)

    up_cols = w_up.reshape(8, 4, 1024).transpose(1, 0, 2)
    qkv_cols = w_qkv.reshape(8, 3, 4, 256).transpose(2, 0, 1, 3).reshape(4, 8, 768)
    vectors = (b_qkv, b_out, b_up, b_down, ln_gain, ln_shift)
    vec_block = [jnp.concatenate([v, jnp.zeros(128 - v.shape[0], BF)]) for v in vectors]
    vec_block = jnp.concatenate(vec_block + [jnp.zeros(256, BF)]).reshape(8, 128)
    columns = jnp.concatenate([up_cols, qkv_cols], axis=-1)
    got = []
    for step in range(NZ):
        piece = lax.dynamic_index_in_dim(columns, (z + step) % NZ, 0, keepdims=False)
        piece = jnp.concatenate([piece, vec_block], axis=-1)
        got.append(send(piece, "z", step) if step else piece)
    incoming = jnp.stack([got[3], got[2], got[1], got[0], got[3], got[2], got[1]])
    incoming = lax.dynamic_slice_in_dim(incoming, NZ - 1 - z, NZ, 0).reshape(32, 1920)
    there, back_home = [], []
    for d in range(32):
        for s in range(4):
            pair = (d * 4 + s, ((d % 8) * 4 + s) * 4 + d // 8)
            there.append(pair)
            back_home.append(pair[::-1])
    w_rows = lax.ppermute(jnp.concatenate([w_down, w_out]), ("x", "y", "c", "z"), there)
    w_out_rows = w_rows[32:].reshape(8, 4, 256).transpose(1, 0, 2).reshape(32, 256)
    payload = jnp.concatenate(
        [incoming[:, :1792], w_rows[:32], w_out_rows, incoming[:, 1792:]], axis=1
    )
    weights = lax.all_gather(payload, ("x", "y", "c"), axis=0, tiled=True)

    x_own = [hidden_in[m, 0] for m in range(micro_count)]
    c_own = [cotangent[m, 0] for m in range(micro_count)]
    mine0 = jnp.concatenate([x_own[0], c_own[0]])
    pieces0 = [mine0] + [send(mine0, "z", -step) for step in range(1, NZ)]
    pieces1 = lax.all_gather(pack(x_own[1], c_own[1], payload), "z", axis=0)

    seg = segments[:, 0]
    key_seg = jnp.where(valid_mask[:, 0] > 0, seg, -1)
    seg_row, seg_key = [
        jnp.broadcast_to(s.astype(F32)[:, None, :], (micro_count, 8, row_len)) for s in (seg, key_seg)
    ]
    tables = rotary_tables(doc_positions(seg))

    tables = [[t[m : m + 1] for t in tables] for m in range(micro_count)]

    def run_attend(m, heads, after):
        return attend(z_arr, *heads, seg_row[m : m + 1], seg_key[m : m + 1], *tables[m], after)

    hid0, cot0, n0, act0, dup0, *heads0, stat0, bup0, w_o, vecs = front(
        z_arr, pieces0, weights, (), *tables[0], ()
    )
    mix0, dqkv0, bqkv0 = run_attend(0, heads0, ())
    cuts0, gain0, shift0 = back(
        z_arr, act0, mix0, dup0, dqkv0, hid0, stat0, weights, w_o, ()
    )
    sum0 = lax.psum_scatter(cuts0, "z", scatter_dimension=0, tiled=True)
    hid1, cot1, n1, act1, dup1, *heads1, stat1, bup1 = front(
        z_arr, [pieces1], weights, (w_o, vecs), *tables[1], (cuts0,)
    )
    cot = (cot0, cot1)
    mlp = grads_mlp(c, (n0, n1), (dup0, dup1), (act0, act1), cot, ())
    mix1, dqkv1, bqkv1 = run_attend(1, heads1, (mlp[0],))
    mlp = add_after(mlp[0], send(mlp[1], "c", 1), mix1)
    mixed, d_qkv, normed = (mix0, mix1), (dqkv0, dqkv1), (n0, n1)
    att = grads_att(c, normed, d_qkv, mixed, cot, (mlp,))
    cuts1, gain1, shift1 = back(
        z_arr, act1, mix1, dup1, dqkv1, hid1, stat1, weights, w_o, (att[0], sum0)
    )
    mlp = lax.psum_scatter(mlp, "x", scatter_dimension=0, tiled=True)
    sum1 = lax.psum_scatter(cuts1, "z", scatter_dimension=0, tiled=True)
    sums = ((bqkv0, gain0, shift0), (bqkv1, gain1, shift1))
    sum_bup = bup0 + bup1
    sum_bqkv, sum_gain, sum_shift = [jnp.sum(a + b, axis=0) for a, b in zip(*sums)]

    mine = jnp.arange(NZ) == z
    sum_cot = jnp.sum(cotangent.astype(F32), axis=(0, 1, 2)).reshape(128, 8)
    sum_bqkv = jnp.where(mine[None, :, None], sum_bqkv.reshape(3, 1, 256), 0.0)
    sum_bup = jnp.where(mine[:, None], jnp.sum(sum_bup, axis=0)[None, :], 0.0)
    parts = (
        sum_bqkv.reshape(128, 24),
        sum_cot,
        sum_bup.reshape(128, 32),
        sum_cot,
        sum_gain.reshape(128, 8),
        sum_shift.reshape(128, 8),
    )
    vec_grads = jnp.stack(
        [jnp.pad(p, ((0, 0), (0, 128 - p.shape[1]))) for p in parts] + [jnp.zeros((128, 128), F32)] * 2,
        axis=1,
    ).reshape(1024, 128)
    place = jnp.stack([lax.axis_index("x"), lax.axis_index("c")]).astype(jnp.int32)
    parts = in_vmem(
        to_x_kernel,
        "to_x",
        (att[0], send(att[1], "c", 1), vec_grads, send(vec_grads, "c", 1)),
        [((128, 1152), BF)] * 4,
        place,
    )
    parts = in_vmem(
        to_y_kernel,
        "to_y",
        (mlp, *exchange(parts, "x")),
        [((32, 3200), BF)] * 4,
        lax.axis_index("y").astype(jnp.int32).reshape(1),
    )
    done0 = finish(x_own[0], c_own[0], [sum0], vecs, parts[0])
    done1 = finish(x_own[1], c_own[1], [sum1], vecs, parts[0])
    out_hidden, grad_input = [jnp.stack(v)[:, None] for v in zip(done0, done1)]
    home, rows_home = in_vmem(
        to_z_kernel,
        "to_z",
        (*exchange(parts, "y"), done1[0]),
        [((4, 8, 1920), F32), ((40, 1024), F32)],
        after=1,
    )
    home = lax.all_to_all(home, "z", 0, 0, tiled=True)
    rows_home = lax.ppermute(rows_home, ("x", "y", "c", "z"), back_home)
    final_up, final_qkv, final_vec = in_vmem(
        home_kernel, "home", (home,), [((8, 4096), F32), ((8, 3072), F32), ((8, 128), F32)]
    )
    return (
        out_hidden,
        grad_input,
        final_qkv,
        rows_home[32:],
        final_up,
        rows_home[:32],
        final_vec[0, :24],
        final_vec[1, :8],
        final_vec[2, :32],
        final_vec[3, :8],
        final_vec[4, :8],
        final_vec[5, :8],
    )


def solution(mesh):
    parts = jax.sharding.Mesh(mesh.devices.reshape(4, 4, 2, NZ), ("x", "y", "c", "z"))
    dp = ("x", "y", "c")
    rows = P(None, dp, "z", None)
    tokens = P(None, dp, None)
    matrix = P(dp + ("z",), None)
    vector = P(dp + ("z",))
    in_specs = (rows, tokens, tokens) + (matrix,) * 4 + (vector,) * 6 + (rows,)
    out_specs = (rows, rows) + (matrix,) * 4 + (vector,) * 6
    return jax.shard_map(body, mesh=parts, in_specs=in_specs, out_specs=out_specs, check_vma=False)
```

```python
import functools

import jax
import jax.numpy as jnp
from jax import lax
from jax.experimental import pallas as pl
from jax.experimental.pallas import tpu as pltpu
from jax.sharding import PartitionSpec as P

BF = jnp.bfloat16
F32 = jnp.float32
MB = 1 << 20
HEAD_DIM = 64
ROT = 32
NZ = 4


def dot(left, right):
    return jnp.dot(left, right, preferred_element_type=F32)


def dot_nt(left, right):
    return lax.dot_general(left, right, (((1,), (1,)), ((), ())), preferred_element_type=F32)


def dot_tn(left, right):
    return lax.dot_general(left, right, (((0,), (0,)), ((), ())), preferred_element_type=F32)


def turn(value, cos, sin, sign):
    right, left = pltpu.roll(value, 16, 1), pltpu.roll(value, 112, 1)
    first = lax.broadcasted_iota(jnp.int32, value.shape, 1) % 32 < 16
    return value * cos + jnp.where(first, left, right) * (sign * sin)


def spread(value, period):
    while period < 128:
        value = value + pltpu.roll(value, period, 1)
        period *= 2
    return value


def lay_out(value, period):
    fold = 128 // period
    lane = lax.broadcasted_iota(jnp.int32, value.shape, 1) // period
    row = lax.broadcasted_iota(jnp.int32, value.shape, 0) % fold
    value = jnp.where(lane == row, spread(value, period), 0.0)
    value = jnp.sum(value.reshape(8, fold, 128), axis=1)
    return jnp.concatenate([value[t : t + 1] for t in range(8)], axis=1)


def unpack_parameters(z, w_ref, wo_ref, vec_ref, block_s):
    rows = w_ref[:, 2816:3072].astype(F32).reshape(32, 4, 8, 256)
    for b in range(4):
        wo_ref[:, b * 256 : b * 256 + 256] = rows[:, b].reshape(256, 256).astype(BF)
    block_s[...] = w_ref[:, 3072:3200].astype(F32)

    def kind(k, first=0, count=128):
        return block_s[pl.ds(first * 8 + k, count, stride=8), :]

    vec_ref[0:1, :] = lay_out(kind(4), 8)
    vec_ref[1:2, :] = lay_out(kind(5), 8)
    vec_ref[2:3, :] = lay_out(kind(2, z * 32, 32), 32)
    vec_ref[4:5, :] = lay_out(kind(1) + kind(3), 8)
    lane = lax.broadcasted_iota(jnp.int32, (128, 128), 1)
    row = lax.broadcasted_iota(jnp.int32, (128, 128), 0)
    qkv = kind(0)
    groups = []
    for g in range(3):
        here = jnp.where(lane < 8, pltpu.roll(qkv, 128 - 8 * g, 1) if g else qkv, 0.0)
        groups.append(spread(here, 8))
    for part in range(3):
        for half in range(2):
            want = (part * 8 + z * 2 + half) * 16 + lane // 8
            total = jnp.zeros((128, 128), F32)
            for g in range(3):
                total = total + jnp.where(3 * row + g == want, groups[g], 0.0)
            at = part * 256 + half * 128
            vec_ref[3:4, at : at + 128] = jnp.sum(total, axis=0, keepdims=True)


def front_kernel(known, z_ref, *rest):
    z = z_ref[0]
    step = pl.program_id(0)
    if not known:
        rest, (wo_ref, vec_ref, block_s) = rest[:-3], rest[-3:]
    x_ref, c_ref, n_ref, act_ref, dup_ref, q_ref, k_ref, v_ref, dm_ref, stat_ref, sum_ref = rest[
        -11:
    ]
    tile = x_ref.shape[1]
    for at, piece in enumerate(rest[:NZ]):

        @pl.when(step == at)
        def _(piece=piece):
            x_ref[0], c_ref[0] = piece[:tile], piece[tile:]

    w_ref = rest[NZ]
    if known:
        wo_ref, vec_ref, cos_ref, sin_ref = rest[NZ + 1 : NZ + 5]
    else:
        cos_ref, sin_ref = rest[NZ + 1 : NZ + 3]

        @pl.when(step == 0)
        def _():
            unpack_parameters(z, w_ref, wo_ref, vec_ref, block_s)

    gain_ref, shift_ref, bu_ref, bq_ref = [vec_ref.at[k : k + 1] for k in range(4)]

    @pl.when(step == 0)
    def _():
        sum_ref[...] = jnp.zeros_like(sum_ref)

    def put(ref, value):
        for r in range(tile // 256):
            row = lax.rem(pl.program_id(0) * (tile // 256) + r + z, 4) * 256
            ref[0, pl.ds(pl.multiple_of(row, 256), 256), :] = value[r * 256 : r * 256 + 256]

    def d_act_of(j):
        return dot_nt(c_ref[0], w_ref[j * 256 : j * 256 + 256, 1792:2816])

    def in_of(j):
        return dot(n_ref[0], w_ref[:, j * 256 : j * 256 + 256])

    d_act = d_act_of(0)
    d_mixed = dot_nt(c_ref[0], wo_ref[...])
    x = x_ref[0].astype(F32)
    average = jnp.mean(x, axis=-1, keepdims=True)
    centered = x - average
    spread = jnp.mean(centered * centered, axis=-1, keepdims=True)
    rs = lax.rsqrt(spread + 1e-05)
    stat_ref[0, :, 0:1] = average
    stat_ref[0, :, 1:2] = rs
    n_ref[0] = (centered * rs * gain_ref[...] + shift_ref[...]).astype(BF)
    put(dm_ref, d_mixed.astype(BF))
    up = in_of(0)
    k0 = 0.7978845608028654
    k1 = k0 * 0.044715
    for j in range(4):
        cols = slice(j * 256, j * 256 + 256)
        if j < 3:
            next_up, next_act = in_of(j + 1), d_act_of(j + 1)
        else:
            q, k, v = in_of(4), in_of(5), in_of(6)
        up = up + bu_ref[:, cols]
        square = up * up
        half = 0.5 + 0.5 * jnp.tanh(up * (k0 + k1 * square))
        act = up * half
        slope = half + 2.0 * act * (1.0 - half) * (k0 + 3.0 * k1 * square)
        d_up = (slope * d_act).astype(BF)
        act_ref[0, :, cols] = act.astype(BF)
        dup_ref[0, :, cols] = d_up
        back = d_up.astype(F32)
        sum_ref[:, cols] += jnp.sum(back.reshape(back.shape[0] // 8, 8, 256), axis=0)
        up, d_act = next_up, next_act
    tabs = (cos_ref[0], sin_ref[0])
    def turn_both(value):
        return jnp.concatenate(
            [turn(value[:, h : h + 128], *tabs, 1.0) for h in (0, 128)], axis=1
        ).astype(BF)

    q = turn_both(q + bq_ref[:, 0:256]) * BF(0.125)
    put(q_ref, q)
    put(k_ref, turn_both(k + bq_ref[:, 256:512]))
    put(v_ref, (v + bq_ref[:, 512:768]).astype(BF))


ANY = pl.BlockSpec(memory_space=pl.ANY)
QUICK = pl.CostEstimate(flops=1024, bytes_accessed=1024, transcendentals=0)


def front(z, pieces, weights, known, cos, sin, after):
    tile, d = pieces[0].shape[-2] // 2, pieces[0].shape[-1]
    n = tile * NZ

    def tok(width):
        return pl.BlockSpec((1, tile, width), lambda j, z: (0, j, 0))

    def turned(width):
        return pl.BlockSpec((1, tile, width), lambda j, z: (0, lax.rem(j + z[0], NZ), 0))

    def row(width):
        return pl.BlockSpec((1, n, width), lambda j, z: (0, 0, 0))

    def whole(a):
        return pl.BlockSpec(a.shape, lambda j, z: (0, 0), pipeline_mode=pl.Buffered(1))

    def keep(*shape):
        return pl.BlockSpec(shape, lambda j, z: (0, 0))

    first = [whole(a) for a in pieces]
    fixed = (weights, *known)
    out_specs = [tok(d)] * 5 + [row(256)] * 4 + [tok(128), keep(8, 1024)]
    out_shape = [jax.ShapeDtypeStruct((1, n, w), BF) for w in [d] * 5 + [256] * 4]
    out_shape += [jax.ShapeDtypeStruct((1, n, 128), F32), jax.ShapeDtypeStruct((8, 1024), F32)]
    scratch = []
    if not known:
        out_specs += [keep(256, d), keep(8, d)]
        out_shape += [jax.ShapeDtypeStruct((256, d), BF), jax.ShapeDtypeStruct((8, d), F32)]
        scratch = [pltpu.VMEM((1024, 128), F32)]
    return pl.pallas_call(
        functools.partial(front_kernel, bool(known)),
        grid_spec=pltpu.PrefetchScalarGridSpec(
            num_scalar_prefetch=1,
            grid=(NZ,),
            in_specs=first + [whole(a) for a in fixed] + [turned(128)] * 2 + [ANY] * len(after),
            out_specs=out_specs,
            scratch_shapes=scratch,
        ),
        out_shape=out_shape,
        compiler_params=pltpu.CompilerParams(vmem_limit_bytes=58 * MB),
        cost_estimate=QUICK,
        name="front",
    )(z, *pieces, *fixed, cos, sin, *after)


def attend_kernel(
    z_ref, q_ref, k_ref, v_ref, dm_ref, row_ref, key_ref, cos_ref, sin_ref, *rest,
):
    mixed_ref, dqkv_ref, sum_ref, bias_s, s_s, dp_s, p_s, ds_s, qm_s, dmm_s, dk_s, dv_s = rest[-12:]
    B = 256
    z = z_ref[0]
    sum_ref[...] = jnp.zeros_like(sum_ref)

    def put(part, a, value):
        rows = pl.ds(pl.multiple_of(lax.rem(a - z + 4, 4) * B, B), B)
        if part is None:
            mixed_ref[0, rows, :] = value
        else:
            dqkv_ref[0, part, rows, :] = value
            sum_ref[part, 0:1, :] += jnp.sum(value.astype(F32), axis=0, keepdims=True)

    key_col = key_ref[0].T
    lane_head = lax.broadcasted_iota(jnp.int32, (B, 128), 1) // 64
    diff = lax.broadcasted_iota(jnp.int32, (B, B), 0) - lax.broadcasted_iota(jnp.int32, (B, B), 1)

    def prepare(aq):
        par, n, here = aq % 2, (aq + 1) * B, slice(aq * B, aq * B + B)
        bias = jnp.where(key_col[0:n, 0:1] == row_ref[0, 0:1, here], 0.0, -1e30)
        if aq:
            bias_s[par, 0 : aq * B, :] = bias[: aq * B]
        edge = jnp.where(diff <= 0, bias[aq * B :], -1e30)
        bias_s[par, here, :] = jnp.where(diff == 0, 0.0, edge)
        q_all, d_all = q_ref[0, here, :], dm_ref[0, here, :]
        for h in range(2):
            cols = slice(h * B, h * B + B)
            qm_s[par, cols, :] = jnp.where(lane_head == h, q_all, jnp.zeros_like(q_all))
            dmm_s[par, cols, :] = jnp.where(lane_head == h, d_all, jnp.zeros_like(d_all))

    def products(aq, h):
        par, n, cols = aq % 2, (aq + 1) * B, slice(h * B, h * B + B)
        s = dot_nt(k_ref[0, 0:n, :], qm_s[par, cols, :]) + bias_s[par, 0:n, :]
        s_s[h, 0:n] = s
        dp_s[h, 0:n] = dot_nt(v_ref[0, 0:n, :], dmm_s[par, cols, :])
        return jnp.max(s, axis=0, keepdims=True)

    def soften(aq, h, top):
        par, n, cols = aq % 2, (aq + 1) * B, slice(h * B, h * B + B)
        e = jnp.exp(s_s[h, 0:n] - top)
        s_s[h, 0:n] = e
        inv = 1.0 / jnp.sum(e, axis=0, keepdims=True)
        mean = jnp.sum(e * dp_s[h, 0:n], axis=0, keepdims=True) * inv
        p = s_s[h, 0:n] * inv
        p_s[par, 0:n, cols] = p.astype(BF)
        ds_s[par, 0:n, cols] = (p * (dp_s[h, 0:n] - mean)).astype(BF)

    def pick(value):
        return jnp.where(lane_head == 0, value[0:B], value[B:])

    def gather(aq, part):
        par, n, here = aq % 2, (aq + 1) * B, slice(aq * B, aq * B + B)
        if part == 0:
            put(None, aq, pick(dot_tn(p_s[par, 0:n, :], v_ref[0, 0:n, :])).astype(BF))
        elif part == 1:
            dq = pick(dot_tn(ds_s[par, 0:n, :], k_ref[0, 0:n, :])) * 0.125
            put(0, aq, turn(dq, cos_ref[0, here, :], sin_ref[0, here, :], -1.0).astype(BF))
        else:
            left, right, to = (p_s, dmm_s, dv_s) if part == 2 else (ds_s, qm_s, dk_s)
            value = dot(left[par, 0:n, :], right[par])
            if aq:
                to[0 : aq * B, :] += value[: aq * B]
            to[here, :] = value[aq * B :]

    prepare(0)
    top = products(0, 0)
    for aq in range(4):
        ahead = products(aq, 1)
        if aq:
            gather(aq - 1, 0)
            gather(aq - 1, 1)
        soften(aq, 0, top)
        if aq:
            gather(aq - 1, 2)
            gather(aq - 1, 3)
        if aq < 3:
            prepare(aq + 1)
            top = products(aq + 1, 0)
        soften(aq, 1, ahead)
    for part in range(4):
        gather(3, part)
    for a in range(4):
        here = slice(a * B, a * B + B)
        put(1, a, turn(dk_s[here, :], cos_ref[0, here, :], sin_ref[0, here, :], -1.0).astype(BF))
        put(2, a, dv_s[here, :].astype(BF))


def attend(z, q, k, v, dm, seg_row, seg_key, cos, sin, after):
    n = q.shape[1]
    half = pl.BlockSpec((1, n, 128), lambda g, z: (0, 0, g))
    table = pl.BlockSpec((1, n, 128), lambda g, z: (0, 0, 0))
    line = pl.BlockSpec((1, 8, n), lambda g, z: (0, 0, 0))
    S = pltpu.VMEM
    return pl.pallas_call(
        attend_kernel,
        grid_spec=pltpu.PrefetchScalarGridSpec(
            num_scalar_prefetch=1,
            grid=(2,),
            in_specs=[half] * 4 + [line] * 2 + [table] * 2 + [ANY] * len(after),
            out_specs=[
                half,
                pl.BlockSpec((1, 3, n, 128), lambda g, z: (0, 0, 0, g)),
                pl.BlockSpec((3, 8, 128), lambda g, z: (0, 0, g)),
            ],
            scratch_shapes=[
                S((2, n, 256), F32), S((2, n, 256), F32), S((2, n, 256), F32),
                S((2, n, 512), BF), S((2, n, 512), BF),
                S((2, 512, 128), BF), S((2, 512, 128), BF),
                S((n, 128), F32), S((n, 128), F32),
            ],
        ),
        out_shape=[
            jax.ShapeDtypeStruct((1, n, 256), BF),
            jax.ShapeDtypeStruct((1, 3, n, 256), BF),
            jax.ShapeDtypeStruct((3, 8, 256), F32),
        ],
        compiler_params=pltpu.CompilerParams(vmem_limit_bytes=58 * MB),
        cost_estimate=QUICK,
        name="attend",
    )(z, q, k, v, dm, seg_row, seg_key, cos, sin, *after)


def back_kernel(
    z_ref, act_ref, mix_ref, dup_ref, dqkv_ref, x_ref, stat_ref, wd_ref, wo_ref, wi_ref, *rest,
):
    cut, gain_ref, shift_ref = rest[-3:]
    z = z_ref[0]
    out = dot(act_ref[0], wd_ref[...]) + dot(mix_ref[0], wo_ref[...])
    dn = dot_nt(dup_ref[0], wi_ref[:, 0:1024])
    for part in range(3):
        at = 1024 + part * 256
        dn = dn + dot_nt(dqkv_ref[0, part], wi_ref[:, at : at + 256])
    xhat = (x_ref[0].astype(F32) - stat_ref[0, :, 0:1]) * stat_ref[0, :, 1:2]
    gain_ref[...] = jnp.sum((dn * xhat).reshape(-1, 8, 256), axis=0)
    shift_ref[...] = jnp.sum(dn.reshape(-1, 8, 256), axis=0)
    for r in range(NZ):
        rows = slice(r * 256, r * 256 + 256)
        first = pl.multiple_of(lax.rem(r + z, NZ) * 512, 512)
        cut[pl.ds(first, 256), :] = out[rows].astype(BF)
        cut[pl.ds(first + 256, 256), :] = dn[rows].astype(BF)


def back(z, act, mixed, d_up, d_qkv, x, stat, weights, w_o, after):
    def rows(a):
        return pl.BlockSpec(a.shape, lambda j, z: (0,) * a.ndim, pipeline_mode=pl.Buffered(1))

    def cols(n, first=0):
        return pl.BlockSpec((n, 256), lambda j, z: (0, first + j))

    return pl.pallas_call(
        back_kernel,
        grid_spec=pltpu.PrefetchScalarGridSpec(
            num_scalar_prefetch=1,
            grid=(4,),
            in_specs=[rows(a) for a in (act, mixed, d_up, d_qkv)]
            + [
                pl.BlockSpec((1, 1024, 256), lambda j, z: (0, 0, j)),
                rows(stat),
                cols(1024, 7),
                cols(256),
                pl.BlockSpec((256, 1792), lambda j, z: (j, 0)),
            ]
            + [ANY] * len(after),
            out_specs=[cols(2048)] + [cols(8)] * 2,
        ),
        out_shape=[jax.ShapeDtypeStruct((2048, 1024), BF)]
        + [jax.ShapeDtypeStruct((8, 1024), F32)] * 2,
        compiler_params=pltpu.CompilerParams(vmem_limit_bytes=58 * MB),
        cost_estimate=QUICK,
        name="back",
    )(z, act, mixed, d_up, d_qkv, x, stat, weights, w_o, weights, *after)


def put_halves(c, value, own_ref, other_ref, lo):
    value = value.reshape(4, 2, 32, value.shape[1])
    first, second = [value[:, k].reshape(128, value.shape[3]) for k in range(2)]
    hi = lo + value.shape[3]
    own_ref[:, lo:hi] = jnp.where(c == 0, first, second).astype(BF)
    other_ref[:, lo:hi] = jnp.where(c == 0, second, first).astype(BF)


def grads_mlp0_kernel(n_ref, dup_ref, act_ref, cot_ref, *rest):
    rest[-1][:, 0:1024] = dot_tn(n_ref[0], dup_ref[0])
    rest[-1][:, 1024:2048] = dot_tn(act_ref[0], cot_ref[0])


def grads_mlp1_kernel(c_ref, n_ref, dup_ref, act_ref, cot_ref, sum_ref, own_ref, other_ref):
    c = c_ref[0]
    up = sum_ref[:, 0:1024] + dot_tn(n_ref[0], dup_ref[0])
    put_halves(c, up, own_ref, other_ref, 0)
    down = sum_ref[:, 1024:2048] + dot_tn(act_ref[0], cot_ref[0])
    put_halves(c, down, own_ref, other_ref, 1024)


def grads_mlp0(normed, d_up, act, cot, after):
    tokens, width = normed.shape[1:]
    part = pl.BlockSpec((1, tokens, 256), lambda i: (0, 0, i))
    whole = pl.BlockSpec(d_up.shape, lambda i: (0, 0, 0), pipeline_mode=pl.Buffered(1))
    return pl.pallas_call(
        grads_mlp0_kernel,
        grid=(width // 256,),
        in_specs=[part, whole, part, whole] + [ANY] * len(after),
        out_specs=pl.BlockSpec((256, 2048), lambda i: (i, 0)),
        out_shape=jax.ShapeDtypeStruct((width, 2048), F32),
        compiler_params=pltpu.CompilerParams(vmem_limit_bytes=58 * MB),
        cost_estimate=QUICK,
        name="grads_mlp0",
    )(normed, d_up, act, cot, *after)


def grads_mlp1(c, normed, d_up, act, cot, first):
    tokens, width = normed.shape[1:]
    part = pl.BlockSpec((1, tokens, 256), lambda i, c: (0, 0, i))
    whole = pl.BlockSpec(d_up.shape, lambda i, c: (0, 0, 0), pipeline_mode=pl.Buffered(1))
    return pl.pallas_call(
        grads_mlp1_kernel,
        grid_spec=pltpu.PrefetchScalarGridSpec(
            num_scalar_prefetch=1,
            grid=(width // 256,),
            in_specs=[part, whole, part, whole, pl.BlockSpec((256, 2048), lambda i, c: (i, 0))],
            out_specs=[pl.BlockSpec((128, 2048), lambda i, c: (i, 0))] * 2,
        ),
        out_shape=[jax.ShapeDtypeStruct((width // 2, 2048), BF)] * 2,
        compiler_params=pltpu.CompilerParams(vmem_limit_bytes=58 * MB),
        cost_estimate=QUICK,
        name="grads_mlp1",
    )(c, normed, d_up, act, cot, first)


def grads_att_kernel(
    c_ref, n0_ref, n1_ref, dqkv0_ref, dqkv1_ref, mix0_ref, mix1_ref, cot0_ref, cot1_ref,
    *rest,
):
    own_ref, other_ref, out_s = rest[-3:]
    c = c_ref[0]
    i = pl.program_id(0)

    @pl.when(i == 0)
    def _():
        out_s[...] = dot_tn(mix0_ref[0], cot0_ref[0]) + dot_tn(mix1_ref[0], cot1_ref[0])

    for part in range(3):
        both = dot_tn(n0_ref[0], dqkv0_ref[0, part]) + dot_tn(n1_ref[0], dqkv1_ref[0, part])
        put_halves(c, both, own_ref, other_ref, part * 256)
    rows = out_s[pl.ds(pl.multiple_of(i * 64, 64), 64), :]
    rows = [rows[d * 8 : d * 8 + 8, b * 256 : b * 256 + 256] for d in range(8) for b in range(4)]
    put_halves(c, jnp.concatenate(rows), own_ref, other_ref, 768)


def grads_att(c, normed, d_qkv, mixed, cot, after):
    tokens, width = normed[0].shape[1:]

    def whole(a):
        return pl.BlockSpec(a.shape, lambda i, c: (0,) * a.ndim, pipeline_mode=pl.Buffered(1))

    return pl.pallas_call(
        grads_att_kernel,
        grid_spec=pltpu.PrefetchScalarGridSpec(
            num_scalar_prefetch=1,
            grid=(4,),
            in_specs=[pl.BlockSpec((1, tokens, 256), lambda i, c: (0, 0, i))] * 2
            + [whole(a) for a in (*d_qkv, *mixed, *cot)]
            + [ANY] * len(after),
            out_specs=[pl.BlockSpec((128, 1024), lambda i, c: (i, 0))] * 2,
            scratch_shapes=[pltpu.VMEM((256, 1024), F32)],
        ),
        out_shape=[jax.ShapeDtypeStruct((512, 1024), BF)] * 2,
        compiler_params=pltpu.CompilerParams(vmem_limit_bytes=58 * MB),
        cost_estimate=QUICK,
        name="grads_att",
    )(c, *normed, *d_qkv, *mixed, *cot, *after)


def finish_kernel(x_ref, c_ref, vec_ref, part_ref, *rest):
    out_ref, dx_ref = rest[-2:]
    x = x_ref[0, 0].astype(F32)
    branch, g = part_ref[0].astype(F32), part_ref[1].astype(F32)
    out_ref[0] = (x + (branch + vec_ref[4:5, :])).astype(BF)
    centered = x - jnp.mean(x, axis=-1, keepdims=True)
    rs = lax.rsqrt(jnp.mean(centered * centered, axis=-1, keepdims=True) + 1e-05)
    xhat = centered * rs
    g = g * vec_ref[0:1, :]
    mean_g = jnp.mean(g, axis=-1, keepdims=True)
    mean_gx = jnp.mean(g * xhat, axis=-1, keepdims=True)
    dx_ref[0] = c_ref[0, 0].astype(F32) + rs * (g - mean_g - xhat * mean_gx)


def finish(micro, x, cot, part, vectors, others):
    n, d = x.shape[2:]
    tile = pl.BlockSpec((1, 1, 128, d), lambda i: (micro, 0, i, 0))
    out = pl.BlockSpec((1, 128, d), lambda i: (micro, i, 0))
    return pl.pallas_call(
        finish_kernel,
        grid=(n // 128,),
        in_specs=[tile] * 2
        + [
            pl.BlockSpec((8, d), lambda i: (0, 0)),
            pl.BlockSpec((2, 128, d), lambda i: (0, i, 0)),
        ]
        + [ANY] * len(others),
        out_specs=[out] * 2,
        out_shape=[jax.ShapeDtypeStruct((2, n, d), BF), jax.ShapeDtypeStruct((2, n, d), F32)],
        input_output_aliases={4 + k: k for k in range(len(others))},
        compiler_params=pltpu.CompilerParams(vmem_limit_bytes=58 * MB),
        cost_estimate=QUICK,
        name="finish",
    )(x, cot, vectors, part.reshape(2, n, d), *others)


def add_kernel(a_ref, b_ref, *rest):
    rest[-1][...] = (a_ref[...].astype(F32) + b_ref[...].astype(F32)).astype(BF)


def add_after(a, b, after):
    n, d = a.shape
    part = pl.BlockSpec((n // 4, d), lambda i: (i, 0))
    return pl.pallas_call(
        add_kernel,
        grid=(4,),
        in_specs=[part, part] + [ANY] * len(after),
        out_specs=part,
        out_shape=jax.ShapeDtypeStruct((n, d), BF),
        compiler_params=pltpu.CompilerParams(vmem_limit_bytes=32 * MB),
        cost_estimate=QUICK,
        name="add_after",
    )(a, b, *after)


def to_columns_kernel(z_ref, up_ref, qkv_ref, down_ref, out_ref, *rest):
    vectors, rows_ref, pieces = rest[:6], rest[6], rest[7:]
    lines = [v[...].astype(F32).reshape(1, -1) for v in vectors]
    lines = [jnp.concatenate([v, jnp.zeros((1, 128 - v.shape[1]), F32)], axis=1) for v in lines]
    block = jnp.concatenate(lines + [jnp.zeros((2, 128), F32)], axis=0).astype(BF)
    for k, piece in enumerate(pieces):
        to = lax.rem(z_ref[0] + k, NZ)
        piece[:, 0:1024] = up_ref[:, pl.ds(pl.multiple_of(to * 1024, 1024), 1024)]
        for part in range(3):
            first = pl.multiple_of(part * 1024 + to * 256, 256)
            at = 1024 + part * 256
            piece[:, at : at + 256] = qkv_ref[:, pl.ds(first, 256)]
        piece[:, 1792:1920] = block
    rows_ref[0:32, :] = down_ref[...].astype(F32).astype(BF)
    rows_ref[32:40, :] = out_ref[...].astype(F32).astype(BF)


def to_payload_kernel(z_ref, g0_ref, g1_ref, g2_ref, g3_ref, rows_ref, after_ref, out_ref):
    got = [g[...].astype(F32) for g in (g0_ref, g1_ref, g2_ref, g3_ref)]
    columns = []
    for source in range(NZ):
        k = lax.rem(z_ref[0] - source + NZ, NZ)
        value = got[3]
        for j in range(3):
            value = jnp.where(k == j, got[j], value)
        columns.append(value)
    columns = jnp.concatenate(columns, axis=0)
    rows = rows_ref[...].astype(F32)
    w_out = jnp.concatenate([rows[32:40, b * 256 : b * 256 + 256] for b in range(4)], axis=0)
    out_ref[:, 0:1792] = columns[:, 0:1792].astype(BF)
    out_ref[:, 1792:2816] = rows[0:32].astype(BF)
    out_ref[:, 2816:3072] = w_out.astype(BF)
    out_ref[:, 3072:3200] = columns[:, 1792:1920].astype(BF)


def total_of(refs, rows):
    return sum([r[rows, :].astype(F32) for r in refs[1:]], refs[0][rows, :].astype(F32))


def to_xy_kernel(c_ref, own_ref, got_ref, va_ref, vb_ref, out_ref):
    total = total_of((own_ref, got_ref), slice(None))
    out_ref[:, :, 0:1024] = total.astype(BF).reshape(16, 32, 1024)
    vec = (va_ref[...] + vb_ref[...]).reshape(16, 2, 32, 128)
    out_ref[:, :, 1024:1152] = jnp.where(c_ref[0] == 0, vec[:, 0], vec[:, 1]).astype(BF)


def to_y_kernel(at_ref, mlp_ref, *outs):
    for k, out in enumerate(outs):
        rows = pl.ds(pl.multiple_of(lax.rem(at_ref[0] + k, 4) * 32, 32), 32)
        out[...] = mlp_ref[rows, :]


def to_z_kernel(att_ref, a_ref, b_ref, c_ref, d_ref, home_ref, rows_ref):
    mlp = total_of((a_ref, b_ref, c_ref, d_ref), slice(0, 32))
    att = att_ref[0].astype(F32)
    for k in range(1, 16):
        att = att + att_ref[k].astype(F32)
    home = jnp.concatenate([mlp[:, :1024], att[:, :768], att[:, 1024:1152]], axis=1)
    home_ref[...] = home.reshape(4, 8, 1920)
    rows_ref[0:32, :] = mlp[:, 1024:2048]
    out = att[:, 768:1024].reshape(4, 8, 256)
    for b in range(4):
        rows_ref[32:40, b * 256 : b * 256 + 256] = out[b]


def home_kernel(home_ref, after_ref, up_ref, qkv_ref, *vectors):
    for k in range(NZ):
        up_ref[:, k * 1024 : k * 1024 + 1024] = home_ref[k, :, 0:1024]
        for part in range(3):
            at = part * 1024 + k * 256
            own = 1024 + part * 256
            qkv_ref[:, at : at + 256] = home_ref[k, :, own : own + 256]
    total = jnp.sum(home_ref[:, :, 1792:1920], axis=0)
    for k, ref in enumerate(vectors):
        ref[...] = total[k, : ref.shape[0]]


def in_vmem(kernel, name, operands, shapes, scalars=None, after=(), limit=58):
    def whole(shape):
        return pl.BlockSpec(shape, lambda i: (0,) * len(shape))

    specs = [whole(a.shape) for a in operands] + [ANY] * len(after)
    operands = (*operands, *after)
    if scalars is not None:
        specs = [pl.BlockSpec(memory_space=pltpu.SMEM)] + specs
        operands = (scalars, *operands)
    return pl.pallas_call(
        kernel,
        grid=(1,),
        in_specs=specs,
        out_specs=[whole(s[0]) for s in shapes],
        out_shape=[jax.ShapeDtypeStruct(*s) for s in shapes],
        compiler_params=pltpu.CompilerParams(vmem_limit_bytes=limit * MB),
        cost_estimate=QUICK,
        name=name,
    )(*operands)


def pack_kernel(a_ref, b_ref, *rest):
    rest[-1][0] = a_ref[0, 0]
    rest[-1][1] = b_ref[0, 0]


def pack(micro, a, b, after):
    n, d = a.shape[2:]
    part = pl.BlockSpec((1, 1, n // 2, d), lambda i: (micro, 0, i, 0))
    return pl.pallas_call(
        pack_kernel,
        grid=(2,),
        in_specs=[part, part] + [ANY] * len(after),
        out_specs=pl.BlockSpec((2, n // 2, d), lambda i: (0, i, 0)),
        out_shape=jax.ShapeDtypeStruct((2, n, d), BF),
        compiler_params=pltpu.CompilerParams(vmem_limit_bytes=58 * MB),
        cost_estimate=QUICK,
        name="pack",
    )(a, b, *after).reshape(2 * n, d)


def doc_positions(seg_row):
    length = seg_row.shape[-1]
    token_index = jnp.arange(length, dtype=jnp.int32)
    previous = jnp.concatenate([seg_row[..., :1], seg_row[..., :-1]], axis=-1)
    starts = jnp.where((token_index == 0) | (seg_row != previous), token_index, 0)
    doc_start = lax.cummax(starts, axis=seg_row.ndim - 1)
    return token_index - doc_start


def rotary_tables(positions):
    dim = jnp.arange(128, dtype=jnp.int32) % HEAD_DIM
    frequency = 10000.0 ** (-(dim % (ROT // 2)).astype(F32) * 2.0 / ROT)
    frequency = jnp.where(dim < ROT, frequency, 0.0)
    angles = positions.astype(F32)[..., None] * frequency
    return jnp.cos(angles), jnp.sin(angles) * jnp.where(dim < ROT // 2, -1.0, 1.0)


def send(value, axis, step):
    size = lax.axis_size(axis)
    return lax.ppermute(value, axis, [(i, (i + step) % size) for i in range(size)])


def exchange(parts, axis):
    return [parts[0]] + [send(parts[k], axis, k) for k in range(1, 4)]


def body(
    hidden_in,
    segments,
    valid_mask,
    w_qkv,
    w_out,
    w_up,
    w_down,
    b_qkv,
    b_out,
    b_up,
    b_down,
    ln_gain,
    ln_shift,
    cotangent,
):
    z = lax.axis_index("z")
    c = lax.axis_index("c").astype(jnp.int32).reshape(1)
    micro_count, _, group, width = hidden_in.shape
    row_len = group * NZ
    z_arr = z.astype(jnp.int32).reshape(1)

    w_rows, *columns = in_vmem(
        to_columns_kernel,
        "to_columns",
        (w_up, w_qkv, w_down, w_out, b_qkv, b_out, b_up, b_down, ln_gain, ln_shift),
        [((40, 1024), BF)] + [((8, 1920), BF)] * 4,
        z_arr,
    )
    there, back_home = [], []
    for d in range(32):
        for s in range(4):
            pair = (d * 4 + s, ((d % 8) * 4 + s) * 4 + d // 8)
            there.append(pair)
            back_home.append(pair[::-1])
    columns = exchange(columns, "z")
    w_rows = lax.ppermute(w_rows, ("x", "y", "c", "z"), there)
    mine0 = pack(0, hidden_in, cotangent, ())
    (payload,) = in_vmem(
        to_payload_kernel,
        "to_payload",
        (*columns, w_rows),
        [((32, 3200), BF)],
        z_arr,
        after=(mine0,),
    )
    weights = lax.all_gather(payload, ("x", "y", "c"), axis=0, tiled=True)

    pieces0 = [mine0] + [send(mine0, "z", -step) for step in range(1, NZ)]
    mine1 = pack(1, hidden_in, cotangent, (pieces0[2],))
    pieces1 = [mine1] + [send(mine1, "z", -step) for step in range(1, NZ)]

    seg = segments[:, 0]
    key_seg = jnp.where(valid_mask[:, 0] > 0, seg, -1)
    seg_row, seg_key = [
        jnp.broadcast_to(s.astype(F32)[:, None, :], (micro_count, 8, row_len)) for s in (seg, key_seg)
    ]
    tables = rotary_tables(doc_positions(seg))

    tables = [[t[m : m + 1] for t in tables] for m in range(micro_count)]

    lines = [[s[m : m + 1] for s in (seg_row, seg_key)] for m in range(micro_count)]

    def run_attend(m, heads, after):
        return attend(z_arr, *heads, *lines[m], *tables[m], after)

    hid0, cot0, n0, act0, dup0, *heads0, stat0, bup0, w_o, vecs = front(
        z_arr, pieces0, weights, (), *tables[0], (*lines[0], *lines[1])
    )
    mix0, dqkv0, bqkv0 = run_attend(0, heads0, ())
    first = grads_mlp0(n0, dup0, act0, cot0, (mix0,))
    cuts0, gain0, shift0 = back(
        z_arr, act0, mix0, dup0, dqkv0, hid0, stat0, weights, w_o, (first, *pieces1[1:])
    )
    sum0 = lax.psum_scatter(cuts0, "z", scatter_dimension=0, tiled=True)
    hid1, cot1, n1, act1, dup1, *heads1, stat1, bup1 = front(
        z_arr, pieces1, weights, (w_o, vecs), *tables[1], (cuts0,)
    )
    cot = (cot0, cot1)
    mlp = grads_mlp1(c, n1, dup1, act1, cot1, first)
    mix1, dqkv1, bqkv1 = run_attend(1, heads1, (mlp[0],))
    mlp = add_after(mlp[0], send(mlp[1], "c", 1), (mix1,))
    att = grads_att(c, (n0, n1), (dqkv0, dqkv1), (mix0, mix1), cot, (mlp,))
    mlp = lax.psum_scatter(mlp, "x", scatter_dimension=0, tiled=True)
    cuts1, gain1, shift1 = back(
        z_arr, act1, mix1, dup1, dqkv1, hid1, stat1, weights, w_o, (sum0, att[0])
    )
    sum1 = lax.psum_scatter(cuts1, "z", scatter_dimension=0, tiled=True)
    sums = ((bqkv0, gain0, shift0), (bqkv1, gain1, shift1))
    sum_bup = bup0 + bup1
    sum_bqkv, sum_gain, sum_shift = [jnp.sum(a + b, axis=-2) for a, b in zip(*sums)]

    mine = jnp.arange(NZ) == z
    sum_cot = jnp.sum(cotangent.astype(F32), axis=(0, 1, 2)).reshape(128, 8)
    sum_bqkv = jnp.where(mine[None, :, None], sum_bqkv.reshape(3, 1, 256), 0.0)
    sum_bup = jnp.where(mine[:, None], jnp.sum(sum_bup, axis=0)[None, :], 0.0)
    parts = (
        sum_bqkv.reshape(128, 24),
        sum_cot,
        sum_bup.reshape(128, 32),
        sum_cot,
        sum_gain.reshape(128, 8),
        sum_shift.reshape(128, 8),
    )
    vec_grads = jnp.stack(
        [jnp.pad(p, ((0, 0), (0, 128 - p.shape[1]))) for p in parts] + [jnp.zeros((128, 128), F32)] * 2,
        axis=1,
    ).reshape(1024, 128)
    mlp = in_vmem(
        to_y_kernel,
        "to_y",
        (mlp,),
        [((32, 2048), BF)] * 4,
        lax.axis_index("y").astype(jnp.int32).reshape(1),
    )
    mlp = exchange(mlp, "y")
    (att,) = in_vmem(
        to_xy_kernel,
        "to_xy",
        (att[0], send(att[1], "c", 1), vec_grads, send(vec_grads, "c", 1)),
        [((16, 32, 1152), BF)],
        c,
        limit=32,
    )
    att = lax.all_to_all(att, ("x", "y"), 0, 0, tiled=True)
    half = finish(0, hidden_in, cotangent, sum0, vecs, ())
    out_hidden, grad_input = finish(1, hidden_in, cotangent, sum1, vecs, half)
    out_hidden, grad_input = out_hidden[:, None], grad_input[:, None]
    home, rows_home = in_vmem(
        to_z_kernel,
        "to_z",
        (att, *mlp),
        [((4, 8, 1920), F32), ((40, 1024), F32)],
    )
    home = lax.all_to_all(home, "z", 0, 0, tiled=True)
    rows_home = lax.ppermute(rows_home, ("x", "y", "c", "z"), back_home)
    final_up, final_qkv, *final_vectors = in_vmem(
        home_kernel,
        "home",
        (home,),
        [((8, 4096), F32), ((8, 3072), F32)] + [((n,), F32) for n in (24, 8, 32, 8, 8, 8)],
        after=(out_hidden,),
    )
    return (
        out_hidden,
        grad_input,
        final_qkv,
        rows_home[32:],
        final_up,
        rows_home[:32],
        *final_vectors,
    )


def solution(mesh):
    parts = jax.sharding.Mesh(mesh.devices.reshape(4, 4, 2, NZ), ("x", "y", "c", "z"))
    dp = ("x", "y", "c")
    rows = P(None, dp, "z", None)
    tokens = P(None, dp, None)
    matrix = P(dp + ("z",), None)
    vector = P(dp + ("z",))
    in_specs = (rows, tokens, tokens) + (matrix,) * 4 + (vector,) * 6 + (rows,)
    out_specs = (rows, rows) + (matrix,) * 4 + (vector,) * 6
    return jax.shard_map(body, mesh=parts, in_specs=in_specs, out_specs=out_specs, check_vma=False)
```

```python
import functools

import jax
import jax.numpy as jnp
from jax import lax
from jax.experimental import pallas as pl
from jax.experimental.pallas import tpu as pltpu
from jax.sharding import PartitionSpec as P

BF = jnp.bfloat16
F32 = jnp.float32
MB = 1 << 20
HEAD_DIM = 64
ROT = 32
NZ = 4


def dot(left, right):
    return jnp.dot(left, right, preferred_element_type=F32)


def dot_nt(left, right):
    return lax.dot_general(left, right, (((1,), (1,)), ((), ())), preferred_element_type=F32)


def dot_tn(left, right):
    return lax.dot_general(left, right, (((0,), (0,)), ((), ())), preferred_element_type=F32)


def turn(value, cos, sin, sign):
    right, left = pltpu.roll(value, 16, 1), pltpu.roll(value, 112, 1)
    first = lax.broadcasted_iota(jnp.int32, value.shape, 1) % 32 < 16
    return value * cos + jnp.where(first, left, right) * (sign * sin)


def spread(value, period):
    while period < 128:
        value = value + pltpu.roll(value, period, 1)
        period *= 2
    return value


def lay_out(value, period):
    fold = 128 // period
    lane = lax.broadcasted_iota(jnp.int32, value.shape, 1) // period
    row = lax.broadcasted_iota(jnp.int32, value.shape, 0) % fold
    value = jnp.where(lane == row, spread(value, period), 0.0)
    value = jnp.sum(value.reshape(8, fold, 128), axis=1)
    return jnp.concatenate([value[t : t + 1] for t in range(8)], axis=1)


def unpack_parameters(z, w_ref, wo_ref, vec_ref, block_s):
    rows = w_ref[:, 2816:3072].astype(F32).reshape(32, 4, 8, 256)
    for b in range(4):
        wo_ref[:, b * 256 : b * 256 + 256] = rows[:, b].reshape(256, 256).astype(BF)
    block_s[...] = w_ref[:, 3072:3200].astype(F32)

    def kind(k, first=0, count=128):
        return block_s[pl.ds(first * 8 + k, count, stride=8), :]

    vec_ref[0:1, :] = lay_out(kind(4), 8)
    vec_ref[1:2, :] = lay_out(kind(5), 8)
    vec_ref[2:3, :] = lay_out(kind(2, z * 32, 32), 32)
    vec_ref[4:5, :] = lay_out(kind(1) + kind(3), 8)
    lane = lax.broadcasted_iota(jnp.int32, (128, 128), 1)
    row = lax.broadcasted_iota(jnp.int32, (128, 128), 0)
    qkv = kind(0)
    groups = []
    for g in range(3):
        here = jnp.where(lane < 8, pltpu.roll(qkv, 128 - 8 * g, 1) if g else qkv, 0.0)
        groups.append(spread(here, 8))
    for part in range(3):
        for half in range(2):
            want = (part * 8 + z * 2 + half) * 16 + lane // 8
            total = jnp.zeros((128, 128), F32)
            for g in range(3):
                total = total + jnp.where(3 * row + g == want, groups[g], 0.0)
            at = part * 256 + half * 128
            vec_ref[3:4, at : at + 128] = jnp.sum(total, axis=0, keepdims=True)


def front_kernel(known, z_ref, *rest):
    z = z_ref[0]
    step = pl.program_id(0)
    if not known:
        rest, (wo_ref, vec_ref, block_s) = rest[:-3], rest[-3:]
    x_ref, c_ref, n_ref, act_ref, dup_ref, q_ref, k_ref, v_ref, dm_ref, stat_ref, sum_ref = rest[
        -11:
    ]
    tile = x_ref.shape[1]
    for at, piece in enumerate(rest[:NZ]):

        @pl.when(step == at)
        def _(piece=piece):
            x_ref[0], c_ref[0] = piece[:tile], piece[tile:]

    w_ref = rest[NZ]
    if known:
        wo_ref, vec_ref, cos_ref, sin_ref = rest[NZ + 1 : NZ + 5]
    else:
        cos_ref, sin_ref = rest[NZ + 1 : NZ + 3]

        @pl.when(step == 0)
        def _():
            unpack_parameters(z, w_ref, wo_ref, vec_ref, block_s)

    gain_ref, shift_ref, bu_ref, bq_ref = [vec_ref.at[k : k + 1] for k in range(4)]

    @pl.when(step == 0)
    def _():
        sum_ref[...] = jnp.zeros_like(sum_ref)

    def put(ref, value):
        for r in range(tile // 256):
            row = lax.rem(pl.program_id(0) * (tile // 256) + r + z, 4) * 256
            ref[0, pl.ds(pl.multiple_of(row, 256), 256), :] = value[r * 256 : r * 256 + 256]

    def d_act_of(j):
        return dot_nt(c_ref[0], w_ref[j * 256 : j * 256 + 256, 1792:2816])

    def in_of(j):
        return dot(n_ref[0], w_ref[:, j * 256 : j * 256 + 256])

    d_act = d_act_of(0)
    d_mixed = dot_nt(c_ref[0], wo_ref[...])
    x = x_ref[0].astype(F32)
    average = jnp.mean(x, axis=-1, keepdims=True)
    centered = x - average
    spread = jnp.mean(centered * centered, axis=-1, keepdims=True)
    rs = lax.rsqrt(spread + 1e-05)
    stat_ref[0, :, 0:1] = average
    stat_ref[0, :, 1:2] = rs
    n_ref[0] = (centered * rs * gain_ref[...] + shift_ref[...]).astype(BF)
    put(dm_ref, d_mixed.astype(BF))
    up = in_of(0)
    k0 = 0.7978845608028654
    k1 = k0 * 0.044715
    for j in range(4):
        cols = slice(j * 256, j * 256 + 256)
        if j < 3:
            next_up, next_act = in_of(j + 1), d_act_of(j + 1)
        else:
            q, k, v = in_of(4), in_of(5), in_of(6)
        up = up + bu_ref[:, cols]
        square = up * up
        half = 0.5 + 0.5 * jnp.tanh(up * (k0 + k1 * square))
        act = up * half
        slope = half + 2.0 * act * (1.0 - half) * (k0 + 3.0 * k1 * square)
        d_up = (slope * d_act).astype(BF)
        act_ref[0, :, cols] = act.astype(BF)
        dup_ref[0, :, cols] = d_up
        back = d_up.astype(F32)
        sum_ref[:, cols] += jnp.sum(back.reshape(back.shape[0] // 8, 8, 256), axis=0)
        up, d_act = next_up, next_act
    tabs = (cos_ref[0], sin_ref[0])
    def turn_both(value):
        return jnp.concatenate(
            [turn(value[:, h : h + 128], *tabs, 1.0) for h in (0, 128)], axis=1
        ).astype(BF)

    q = turn_both(q + bq_ref[:, 0:256]) * BF(0.125)
    put(q_ref, q)
    put(k_ref, turn_both(k + bq_ref[:, 256:512]))
    put(v_ref, (v + bq_ref[:, 512:768]).astype(BF))


ANY = pl.BlockSpec(memory_space=pl.ANY)
QUICK = pl.CostEstimate(flops=1024, bytes_accessed=1024, transcendentals=0)


def front(z, pieces, weights, known, cos, sin, after, limit):
    tile, d = pieces[0].shape[-2] // 2, pieces[0].shape[-1]
    n = tile * NZ

    def tok(width):
        return pl.BlockSpec((1, tile, width), lambda j, z: (0, j, 0))

    def turned(width):
        return pl.BlockSpec((1, tile, width), lambda j, z: (0, lax.rem(j + z[0], NZ), 0))

    def row(width):
        return pl.BlockSpec((1, n, width), lambda j, z: (0, 0, 0))

    def whole(a):
        return pl.BlockSpec(a.shape, lambda j, z: (0, 0), pipeline_mode=pl.Buffered(1))

    def keep(*shape):
        return pl.BlockSpec(shape, lambda j, z: (0, 0))

    first = [whole(a) for a in pieces]
    fixed = (weights, *known)
    out_specs = [tok(d)] * 5 + [row(256)] * 4 + [tok(128), keep(8, 1024)]
    out_shape = [jax.ShapeDtypeStruct((1, n, w), BF) for w in [d] * 5 + [256] * 4]
    out_shape += [jax.ShapeDtypeStruct((1, n, 128), F32), jax.ShapeDtypeStruct((8, 1024), F32)]
    scratch = []
    if not known:
        out_specs += [keep(256, d), keep(8, d)]
        out_shape += [jax.ShapeDtypeStruct((256, d), BF), jax.ShapeDtypeStruct((8, d), F32)]
        scratch = [pltpu.VMEM((1024, 128), F32)]
    return pl.pallas_call(
        functools.partial(front_kernel, bool(known)),
        grid_spec=pltpu.PrefetchScalarGridSpec(
            num_scalar_prefetch=1,
            grid=(NZ,),
            in_specs=first + [whole(a) for a in fixed] + [turned(128)] * 2 + [ANY] * len(after),
            out_specs=out_specs,
            scratch_shapes=scratch,
        ),
        out_shape=out_shape,
        compiler_params=pltpu.CompilerParams(vmem_limit_bytes=limit * MB),
        cost_estimate=QUICK,
        name="front",
    )(z, *pieces, *fixed, cos, sin, *after)


def attend_kernel(
    z_ref, q_ref, k_ref, v_ref, dm_ref, row_ref, key_ref, cos_ref, sin_ref, *rest,
):
    mixed_ref, dqkv_ref, sum_ref, bias_s, s_s, dp_s, p_s, ds_s, qm_s, dmm_s, dk_s, dv_s = rest[-12:]
    B = 256
    z = z_ref[0]
    sum_ref[...] = jnp.zeros_like(sum_ref)

    def put(part, a, value):
        rows = pl.ds(pl.multiple_of(lax.rem(a - z + 4, 4) * B, B), B)
        if part is None:
            mixed_ref[0, rows, :] = value
        else:
            dqkv_ref[0, part, rows, :] = value
            sum_ref[part, 0:1, :] += jnp.sum(value.astype(F32), axis=0, keepdims=True)

    key_col = key_ref[0].T
    lane_head = lax.broadcasted_iota(jnp.int32, (B, 128), 1) // 64
    diff = lax.broadcasted_iota(jnp.int32, (B, B), 0) - lax.broadcasted_iota(jnp.int32, (B, B), 1)

    def prepare(aq):
        par, n, here = aq % 2, (aq + 1) * B, slice(aq * B, aq * B + B)
        bias = jnp.where(key_col[0:n, 0:1] == row_ref[0, 0:1, here], 0.0, -1e30)
        if aq:
            bias_s[par, 0 : aq * B, :] = bias[: aq * B]
        edge = jnp.where(diff <= 0, bias[aq * B :], -1e30)
        bias_s[par, here, :] = jnp.where(diff == 0, 0.0, edge)
        q_all, d_all = q_ref[0, here, :], dm_ref[0, here, :]
        for h in range(2):
            cols = slice(h * B, h * B + B)
            qm_s[par, cols, :] = jnp.where(lane_head == h, q_all, jnp.zeros_like(q_all))
            dmm_s[par, cols, :] = jnp.where(lane_head == h, d_all, jnp.zeros_like(d_all))

    def products(aq, h):
        par, n, cols = aq % 2, (aq + 1) * B, slice(h * B, h * B + B)
        s = dot_nt(k_ref[0, 0:n, :], qm_s[par, cols, :]) + bias_s[par, 0:n, :]
        s_s[h, 0:n] = s
        dp_s[h, 0:n] = dot_nt(v_ref[0, 0:n, :], dmm_s[par, cols, :])
        return jnp.max(s, axis=0, keepdims=True)

    def soften(aq, h, top):
        par, n, cols = aq % 2, (aq + 1) * B, slice(h * B, h * B + B)
        e = jnp.exp(s_s[h, 0:n] - top)
        s_s[h, 0:n] = e
        inv = 1.0 / jnp.sum(e, axis=0, keepdims=True)
        mean = jnp.sum(e * dp_s[h, 0:n], axis=0, keepdims=True) * inv
        p = s_s[h, 0:n] * inv
        p_s[par, 0:n, cols] = p.astype(BF)
        ds_s[par, 0:n, cols] = (p * (dp_s[h, 0:n] - mean)).astype(BF)

    def pick(value):
        return jnp.where(lane_head == 0, value[0:B], value[B:])

    def gather(aq, part):
        par, n, here = aq % 2, (aq + 1) * B, slice(aq * B, aq * B + B)
        if part == 0:
            put(None, aq, pick(dot_tn(p_s[par, 0:n, :], v_ref[0, 0:n, :])).astype(BF))
        elif part == 1:
            dq = pick(dot_tn(ds_s[par, 0:n, :], k_ref[0, 0:n, :])) * 0.125
            put(0, aq, turn(dq, cos_ref[0, here, :], sin_ref[0, here, :], -1.0).astype(BF))
        else:
            left, right, to = (p_s, dmm_s, dv_s) if part == 2 else (ds_s, qm_s, dk_s)
            value = dot(left[par, 0:n, :], right[par])
            if aq:
                to[0 : aq * B, :] += value[: aq * B]
            to[here, :] = value[aq * B :]

    prepare(0)
    top = products(0, 0)
    for aq in range(4):
        ahead = products(aq, 1)
        if aq:
            gather(aq - 1, 0)
            gather(aq - 1, 1)
        soften(aq, 0, top)
        if aq:
            gather(aq - 1, 2)
            gather(aq - 1, 3)
        if aq < 3:
            prepare(aq + 1)
            top = products(aq + 1, 0)
        soften(aq, 1, ahead)
    for part in range(4):
        gather(3, part)
    for a in range(4):
        here = slice(a * B, a * B + B)
        put(1, a, turn(dk_s[here, :], cos_ref[0, here, :], sin_ref[0, here, :], -1.0).astype(BF))
        put(2, a, dv_s[here, :].astype(BF))


def attend(z, q, k, v, dm, seg_row, seg_key, cos, sin, after, limit):
    n = q.shape[1]
    half = pl.BlockSpec((1, n, 128), lambda g, z: (0, 0, g))
    table = pl.BlockSpec((1, n, 128), lambda g, z: (0, 0, 0))
    line = pl.BlockSpec((1, 8, n), lambda g, z: (0, 0, 0))
    S = pltpu.VMEM
    return pl.pallas_call(
        attend_kernel,
        grid_spec=pltpu.PrefetchScalarGridSpec(
            num_scalar_prefetch=1,
            grid=(2,),
            in_specs=[half] * 4 + [line] * 2 + [table] * 2 + [ANY] * len(after),
            out_specs=[
                half,
                pl.BlockSpec((1, 3, n, 128), lambda g, z: (0, 0, 0, g)),
                pl.BlockSpec((3, 8, 128), lambda g, z: (0, 0, g)),
            ],
            scratch_shapes=[
                S((2, n, 256), F32), S((2, n, 256), F32), S((2, n, 256), F32),
                S((2, n, 512), BF), S((2, n, 512), BF),
                S((2, 512, 128), BF), S((2, 512, 128), BF),
                S((n, 128), F32), S((n, 128), F32),
            ],
        ),
        out_shape=[
            jax.ShapeDtypeStruct((1, n, 256), BF),
            jax.ShapeDtypeStruct((1, 3, n, 256), BF),
            jax.ShapeDtypeStruct((3, 8, 256), F32),
        ],
        compiler_params=pltpu.CompilerParams(vmem_limit_bytes=limit * MB),
        cost_estimate=QUICK,
        name="attend",
    )(z, q, k, v, dm, seg_row, seg_key, cos, sin, *after)


def back_kernel(
    z_ref, act_ref, mix_ref, dup_ref, dqkv_ref, x_ref, stat_ref, wd_ref, wo_ref, wi_ref, *rest,
):
    cut, gain_ref, shift_ref = rest[-3:]
    z = z_ref[0]
    out = dot(act_ref[0], wd_ref[...]) + dot(mix_ref[0], wo_ref[...])
    dn = dot_nt(dup_ref[0], wi_ref[:, 0:1024])
    for part in range(3):
        at = 1024 + part * 256
        dn = dn + dot_nt(dqkv_ref[0, part], wi_ref[:, at : at + 256])
    xhat = (x_ref[0].astype(F32) - stat_ref[0, :, 0:1]) * stat_ref[0, :, 1:2]
    gain_ref[...] = jnp.sum((dn * xhat).reshape(-1, 8, 256), axis=0)
    shift_ref[...] = jnp.sum(dn.reshape(-1, 8, 256), axis=0)
    for r in range(NZ):
        rows = slice(r * 256, r * 256 + 256)
        first = pl.multiple_of(lax.rem(r + z, NZ) * 512, 512)
        cut[pl.ds(first, 256), :] = out[rows].astype(BF)
        cut[pl.ds(first + 256, 256), :] = dn[rows].astype(BF)


def back(z, act, mixed, d_up, d_qkv, x, stat, weights, w_o, after, limit):
    def rows(a):
        return pl.BlockSpec(a.shape, lambda j, z: (0,) * a.ndim, pipeline_mode=pl.Buffered(1))

    def cols(n, first=0):
        return pl.BlockSpec((n, 256), lambda j, z: (0, first + j))

    return pl.pallas_call(
        back_kernel,
        grid_spec=pltpu.PrefetchScalarGridSpec(
            num_scalar_prefetch=1,
            grid=(4,),
            in_specs=[rows(a) for a in (act, mixed, d_up, d_qkv)]
            + [
                pl.BlockSpec((1, 1024, 256), lambda j, z: (0, 0, j)),
                rows(stat),
                cols(1024, 7),
                cols(256),
                pl.BlockSpec((256, 1792), lambda j, z: (j, 0)),
            ]
            + [ANY] * len(after),
            out_specs=[cols(2048)] + [cols(8)] * 2,
        ),
        out_shape=[jax.ShapeDtypeStruct((2048, 1024), BF)]
        + [jax.ShapeDtypeStruct((8, 1024), F32)] * 2,
        compiler_params=pltpu.CompilerParams(vmem_limit_bytes=limit * MB),
        cost_estimate=QUICK,
        name="back",
    )(z, act, mixed, d_up, d_qkv, x, stat, weights, w_o, weights, *after)


def put_halves(c, value, own_ref, other_ref, lo):
    value = value.reshape(4, 2, 32, value.shape[1])
    first, second = [value[:, k].reshape(128, value.shape[3]) for k in range(2)]
    hi = lo + value.shape[3]
    own_ref[:, lo:hi] = jnp.where(c == 0, first, second).astype(BF)
    other_ref[:, lo:hi] = jnp.where(c == 0, second, first).astype(BF)


def grads_mlp0_kernel(n_ref, dup_ref, act_ref, cot_ref, *rest):
    rest[-1][:, 0:1024] = dot_tn(n_ref[0], dup_ref[0]).astype(BF)
    rest[-1][:, 1024:2048] = dot_tn(act_ref[0], cot_ref[0]).astype(BF)


def grads_mlp1_kernel(c_ref, n_ref, dup_ref, act_ref, cot_ref, sum_ref, own_ref, other_ref):
    c = c_ref[0]
    up = sum_ref[:, 0:1024].astype(F32) + dot_tn(n_ref[0], dup_ref[0])
    put_halves(c, up, own_ref, other_ref, 0)
    down = sum_ref[:, 1024:2048].astype(F32) + dot_tn(act_ref[0], cot_ref[0])
    put_halves(c, down, own_ref, other_ref, 1024)


def grads_mlp0(normed, d_up, act, cot, after):
    tokens, width = normed.shape[1:]
    part = pl.BlockSpec((1, tokens, 256), lambda i: (0, 0, i))
    whole = pl.BlockSpec(d_up.shape, lambda i: (0, 0, 0), pipeline_mode=pl.Buffered(1))
    return pl.pallas_call(
        grads_mlp0_kernel,
        grid=(width // 256,),
        in_specs=[part, whole, part, whole] + [ANY] * len(after),
        out_specs=pl.BlockSpec((256, 2048), lambda i: (i, 0)),
        out_shape=jax.ShapeDtypeStruct((width, 2048), BF),
        compiler_params=pltpu.CompilerParams(vmem_limit_bytes=24 * MB),
        cost_estimate=QUICK,
        name="grads_mlp0",
    )(normed, d_up, act, cot, *after)


def grads_mlp1(c, normed, d_up, act, cot, first):
    tokens, width = normed.shape[1:]
    part = pl.BlockSpec((1, tokens, 256), lambda i, c: (0, 0, i))
    whole = pl.BlockSpec(d_up.shape, lambda i, c: (0, 0, 0), pipeline_mode=pl.Buffered(1))
    return pl.pallas_call(
        grads_mlp1_kernel,
        grid_spec=pltpu.PrefetchScalarGridSpec(
            num_scalar_prefetch=1,
            grid=(width // 256,),
            in_specs=[part, whole, part, whole, pl.BlockSpec((256, 2048), lambda i, c: (i, 0))],
            out_specs=[pl.BlockSpec((128, 2048), lambda i, c: (i, 0))] * 2,
        ),
        out_shape=[jax.ShapeDtypeStruct((width // 2, 2048), BF)] * 2,
        compiler_params=pltpu.CompilerParams(vmem_limit_bytes=46 * MB),
        cost_estimate=QUICK,
        name="grads_mlp1",
    )(c, normed, d_up, act, cot, first)


def grads_att_kernel(
    c_ref, n0_ref, n1_ref, dqkv0_ref, dqkv1_ref, mix0_ref, mix1_ref, cot0_ref, cot1_ref,
    *rest,
):
    own_ref, other_ref, out_s = rest[-3:]
    c = c_ref[0]
    i = pl.program_id(0)

    @pl.when(i == 0)
    def _():
        out_s[...] = dot_tn(mix0_ref[0], cot0_ref[0]) + dot_tn(mix1_ref[0], cot1_ref[0])

    for part in range(3):
        both = dot_tn(n0_ref[0], dqkv0_ref[0, part]) + dot_tn(n1_ref[0], dqkv1_ref[0, part])
        put_halves(c, both, own_ref, other_ref, part * 256)
    rows = out_s[pl.ds(pl.multiple_of(i * 64, 64), 64), :]
    rows = [rows[d * 8 : d * 8 + 8, b * 256 : b * 256 + 256] for d in range(8) for b in range(4)]
    put_halves(c, jnp.concatenate(rows), own_ref, other_ref, 768)


def grads_att(c, normed, d_qkv, mixed, cot, after):
    tokens, width = normed[0].shape[1:]

    def whole(a):
        return pl.BlockSpec(a.shape, lambda i, c: (0,) * a.ndim, pipeline_mode=pl.Buffered(1))

    return pl.pallas_call(
        grads_att_kernel,
        grid_spec=pltpu.PrefetchScalarGridSpec(
            num_scalar_prefetch=1,
            grid=(4,),
            in_specs=[pl.BlockSpec((1, tokens, 256), lambda i, c: (0, 0, i))] * 2
            + [whole(a) for a in (*d_qkv, *mixed, *cot)]
            + [ANY] * len(after),
            out_specs=[pl.BlockSpec((128, 1024), lambda i, c: (i, 0))] * 2,
            scratch_shapes=[pltpu.VMEM((256, 1024), F32)],
        ),
        out_shape=[jax.ShapeDtypeStruct((512, 1024), BF)] * 2,
        compiler_params=pltpu.CompilerParams(vmem_limit_bytes=58 * MB),
        cost_estimate=QUICK,
        name="grads_att",
    )(c, *normed, *d_qkv, *mixed, *cot, *after)


def finish_kernel(x_ref, c_ref, vec_ref, part_ref, *rest):
    out_ref, dx_ref = rest[-2:]
    x = x_ref[0, 0].astype(F32)
    branch, g = part_ref[0].astype(F32), part_ref[1].astype(F32)
    out_ref[0] = (x + (branch + vec_ref[4:5, :])).astype(BF)
    centered = x - jnp.mean(x, axis=-1, keepdims=True)
    rs = lax.rsqrt(jnp.mean(centered * centered, axis=-1, keepdims=True) + 1e-05)
    xhat = centered * rs
    g = g * vec_ref[0:1, :]
    mean_g = jnp.mean(g, axis=-1, keepdims=True)
    mean_gx = jnp.mean(g * xhat, axis=-1, keepdims=True)
    dx_ref[0] = c_ref[0, 0].astype(F32) + rs * (g - mean_g - xhat * mean_gx)


def finish(micro, x, cot, part, vectors, others, after=()):
    n, d = x.shape[2:]
    tile = pl.BlockSpec((1, 1, 128, d), lambda i: (micro, 0, i, 0))
    out = pl.BlockSpec((1, 128, d), lambda i: (micro, i, 0))
    return pl.pallas_call(
        finish_kernel,
        grid=(n // 128,),
        in_specs=[tile] * 2
        + [
            pl.BlockSpec((8, d), lambda i: (0, 0)),
            pl.BlockSpec((2, 128, d), lambda i: (0, i, 0)),
        ]
        + [ANY] * (len(others) + len(after)),
        out_specs=[out] * 2,
        out_shape=[jax.ShapeDtypeStruct((2, n, d), BF), jax.ShapeDtypeStruct((2, n, d), F32)],
        input_output_aliases={4 + k: k for k in range(len(others))},
        compiler_params=pltpu.CompilerParams(vmem_limit_bytes=58 * MB),
        cost_estimate=QUICK,
        name="finish",
    )(x, cot, vectors, part.reshape(2, n, d), *others, *after)


def add_kernel(a_ref, b_ref, *rest):
    rest[-1][...] = (a_ref[...].astype(F32) + b_ref[...].astype(F32)).astype(BF)


def add_after(a, b, after):
    n, d = a.shape
    part = pl.BlockSpec((n // 4, d), lambda i: (i, 0))
    return pl.pallas_call(
        add_kernel,
        grid=(4,),
        in_specs=[part, part] + [ANY] * len(after),
        out_specs=part,
        out_shape=jax.ShapeDtypeStruct((n, d), BF),
        compiler_params=pltpu.CompilerParams(vmem_limit_bytes=32 * MB),
        cost_estimate=QUICK,
        name="add_after",
    )(a, b, *after)


def to_columns_kernel(z_ref, up_ref, qkv_ref, down_ref, out_ref, *rest):
    vectors, rows_ref, pieces = rest[:6], rest[6], rest[7:]
    lines = [v[...].astype(F32).reshape(1, -1) for v in vectors]
    lines = [jnp.concatenate([v, jnp.zeros((1, 128 - v.shape[1]), F32)], axis=1) for v in lines]
    block = jnp.concatenate(lines + [jnp.zeros((2, 128), F32)], axis=0).astype(BF)
    for k, piece in enumerate(pieces):
        to = lax.rem(z_ref[0] + k, NZ)
        piece[:, 0:1024] = up_ref[:, pl.ds(pl.multiple_of(to * 1024, 1024), 1024)]
        for part in range(3):
            first = pl.multiple_of(part * 1024 + to * 256, 256)
            at = 1024 + part * 256
            piece[:, at : at + 256] = qkv_ref[:, pl.ds(first, 256)]
        piece[:, 1792:1920] = block
    rows_ref[0:32, :] = down_ref[...].astype(F32).astype(BF)
    rows_ref[32:40, :] = out_ref[...].astype(F32).astype(BF)


def to_payload_kernel(z_ref, g0_ref, g1_ref, g2_ref, g3_ref, rows_ref, after_ref, out_ref):
    got = [g[...].astype(F32) for g in (g0_ref, g1_ref, g2_ref, g3_ref)]
    columns = []
    for source in range(NZ):
        k = lax.rem(z_ref[0] - source + NZ, NZ)
        value = got[3]
        for j in range(3):
            value = jnp.where(k == j, got[j], value)
        columns.append(value)
    columns = jnp.concatenate(columns, axis=0)
    rows = rows_ref[...].astype(F32)
    w_out = jnp.concatenate([rows[32:40, b * 256 : b * 256 + 256] for b in range(4)], axis=0)
    out_ref[:, 0:1792] = columns[:, 0:1792].astype(BF)
    out_ref[:, 1792:2816] = rows[0:32].astype(BF)
    out_ref[:, 2816:3072] = w_out.astype(BF)
    out_ref[:, 3072:3200] = columns[:, 1792:1920].astype(BF)


def total_of(refs, rows):
    return sum([r[rows, :].astype(F32) for r in refs[1:]], refs[0][rows, :].astype(F32))


def to_xy_kernel(c_ref, own_ref, got_ref, va_ref, vb_ref, out_ref):
    total = total_of((own_ref, got_ref), slice(None))
    out_ref[:, :, 0:1024] = total.astype(BF).reshape(16, 32, 1024)
    vec = (va_ref[...] + vb_ref[...]).reshape(16, 2, 32, 128)
    out_ref[:, :, 1024:1152] = jnp.where(c_ref[0] == 0, vec[:, 0], vec[:, 1]).astype(BF)


def to_y_kernel(at_ref, mlp_ref, *outs):
    for k, out in enumerate(outs):
        rows = pl.ds(pl.multiple_of(lax.rem(at_ref[0] + k, 4) * 32, 32), 32)
        out[...] = mlp_ref[rows, :]


def to_z_kernel(att_ref, a_ref, b_ref, c_ref, d_ref, home_ref, rows_ref):
    mlp = total_of((a_ref, b_ref, c_ref, d_ref), slice(0, 32))
    att = att_ref[0].astype(F32)
    for k in range(1, 16):
        att = att + att_ref[k].astype(F32)
    home = jnp.concatenate([mlp[:, :1024], att[:, :768], att[:, 1024:1152]], axis=1)
    home_ref[...] = home.reshape(4, 8, 1920).astype(BF)
    rows_ref[0:32, :] = mlp[:, 1024:2048]
    out = att[:, 768:1024].reshape(4, 8, 256)
    for b in range(4):
        rows_ref[32:40, b * 256 : b * 256 + 256] = out[b]


def home_kernel(home_ref, up_ref, qkv_ref, *vectors):
    for k in range(NZ):
        up_ref[:, k * 1024 : k * 1024 + 1024] = home_ref[k, :, 0:1024].astype(F32)
        for part in range(3):
            at = part * 1024 + k * 256
            own = 1024 + part * 256
            qkv_ref[:, at : at + 256] = home_ref[k, :, own : own + 256].astype(F32)
    total = jnp.sum(home_ref[:, :, 1792:1920].astype(F32), axis=0)
    for k, ref in enumerate(vectors):
        ref[...] = total[k, : ref.shape[0]]


def in_vmem(kernel, name, operands, shapes, scalars=None, after=(), limit=58):
    def whole(shape):
        return pl.BlockSpec(shape, lambda i: (0,) * len(shape))

    specs = [whole(a.shape) for a in operands] + [ANY] * len(after)
    operands = (*operands, *after)
    if scalars is not None:
        specs = [pl.BlockSpec(memory_space=pltpu.SMEM)] + specs
        operands = (scalars, *operands)
    return pl.pallas_call(
        kernel,
        grid=(1,),
        in_specs=specs,
        out_specs=[whole(s[0]) for s in shapes],
        out_shape=[jax.ShapeDtypeStruct(*s) for s in shapes],
        compiler_params=pltpu.CompilerParams(vmem_limit_bytes=limit * MB),
        cost_estimate=QUICK,
        name=name,
    )(*operands)


def pack_kernel(a_ref, b_ref, *rest):
    rest[-1][0] = a_ref[0, 0]
    rest[-1][1] = b_ref[0, 0]


def pack(micro, a, b, after):
    n, d = a.shape[2:]
    part = pl.BlockSpec((1, 1, n // 2, d), lambda i: (micro, 0, i, 0))
    return pl.pallas_call(
        pack_kernel,
        grid=(2,),
        in_specs=[part, part] + [ANY] * len(after),
        out_specs=pl.BlockSpec((2, n // 2, d), lambda i: (0, i, 0)),
        out_shape=jax.ShapeDtypeStruct((2, n, d), BF),
        compiler_params=pltpu.CompilerParams(vmem_limit_bytes=58 * MB),
        cost_estimate=QUICK,
        name="pack",
    )(a, b, *after).reshape(2 * n, d)


def doc_positions(seg_row):
    length = seg_row.shape[-1]
    token_index = jnp.arange(length, dtype=jnp.int32)
    previous = jnp.concatenate([seg_row[..., :1], seg_row[..., :-1]], axis=-1)
    starts = jnp.where((token_index == 0) | (seg_row != previous), token_index, 0)
    doc_start = lax.cummax(starts, axis=seg_row.ndim - 1)
    return token_index - doc_start


def rotary_tables(positions):
    dim = jnp.arange(128, dtype=jnp.int32) % HEAD_DIM
    frequency = 10000.0 ** (-(dim % (ROT // 2)).astype(F32) * 2.0 / ROT)
    frequency = jnp.where(dim < ROT, frequency, 0.0)
    angles = positions.astype(F32)[..., None] * frequency
    return jnp.cos(angles), jnp.sin(angles) * jnp.where(dim < ROT // 2, -1.0, 1.0)


def send(value, axis, step):
    size = lax.axis_size(axis)
    return lax.ppermute(value, axis, [(i, (i + step) % size) for i in range(size)])


def exchange(parts, axis):
    return [parts[0]] + [send(parts[k], axis, k) for k in range(1, 4)]


def body(
    hidden_in,
    segments,
    valid_mask,
    w_qkv,
    w_out,
    w_up,
    w_down,
    b_qkv,
    b_out,
    b_up,
    b_down,
    ln_gain,
    ln_shift,
    cotangent,
):
    z = lax.axis_index("z")
    c = lax.axis_index("c").astype(jnp.int32).reshape(1)
    micro_count, _, group, width = hidden_in.shape
    row_len = group * NZ
    z_arr = z.astype(jnp.int32).reshape(1)

    w_rows, *columns = in_vmem(
        to_columns_kernel,
        "to_columns",
        (w_up, w_qkv, w_down, w_out, b_qkv, b_out, b_up, b_down, ln_gain, ln_shift),
        [((40, 1024), BF)] + [((8, 1920), BF)] * 4,
        z_arr,
    )
    there, back_home = [], []
    for d in range(32):
        for s in range(4):
            pair = (d * 4 + s, ((d % 8) * 4 + s) * 4 + d // 8)
            there.append(pair)
            back_home.append(pair[::-1])
    columns = exchange(columns, "z")
    w_rows = lax.ppermute(w_rows, ("x", "y", "c", "z"), there)
    mine0 = pack(0, hidden_in, cotangent, ())
    (payload,) = in_vmem(
        to_payload_kernel,
        "to_payload",
        (*columns, w_rows),
        [((32, 3200), BF)],
        z_arr,
        after=(mine0,),
    )
    weights = lax.all_gather(payload, ("x", "y", "c"), axis=0, tiled=True)

    pieces0 = [mine0] + [send(mine0, "z", -step) for step in range(1, NZ)]
    mine1 = pack(1, hidden_in, cotangent, (pieces0[2],))
    pieces1 = [mine1] + [send(mine1, "z", -step) for step in range(1, NZ)]

    seg = segments[:, 0]
    key_seg = jnp.where(valid_mask[:, 0] > 0, seg, -1)
    seg_row, seg_key = [
        jnp.broadcast_to(s.astype(F32)[:, None, :], (micro_count, 8, row_len)) for s in (seg, key_seg)
    ]
    tables = rotary_tables(doc_positions(seg))

    tables = [[t[m : m + 1] for t in tables] for m in range(micro_count)]

    lines = [[s[m : m + 1] for s in (seg_row, seg_key)] for m in range(micro_count)]

    def run_attend(m, heads, after, limit):
        return attend(z_arr, *heads, *lines[m], *tables[m], after, limit)

    hid0, cot0, n0, act0, dup0, *heads0, stat0, bup0, w_o, vecs = front(
        z_arr, pieces0, weights, (), *tables[0], (*lines[0], *lines[1]), 34
    )
    mix0, dqkv0, bqkv0 = run_attend(0, heads0, (), 30)
    first = grads_mlp0(n0, dup0, act0, cot0, (mix0,))
    cuts0, gain0, shift0 = back(
        z_arr, act0, mix0, dup0, dqkv0, hid0, stat0, weights, w_o, (first, *pieces1[1:]), 46
    )
    sum0 = lax.psum_scatter(cuts0, "z", scatter_dimension=0, tiled=True)
    hid1, cot1, n1, act1, dup1, *heads1, stat1, bup1 = front(
        z_arr, pieces1, weights, (w_o, vecs), *tables[1], (cuts0,), 48
    )
    cot = (cot0, cot1)
    mlp = grads_mlp1(c, n1, dup1, act1, cot1, first)
    mix1, dqkv1, bqkv1 = run_attend(1, heads1, (mlp[0],), 46)
    mlp = add_after(mlp[0], send(mlp[1], "c", 1), (mix1,))
    att = grads_att(c, (n0, n1), (dqkv0, dqkv1), (mix0, mix1), cot, (mlp,))
    mlp = lax.psum_scatter(mlp, "x", scatter_dimension=0, tiled=True)
    cuts1, gain1, shift1 = back(
        z_arr, act1, mix1, dup1, dqkv1, hid1, stat1, weights, w_o, (sum0, att[0]), 58
    )
    sum1 = lax.psum_scatter(cuts1, "z", scatter_dimension=0, tiled=True)
    sums = ((bqkv0, gain0, shift0), (bqkv1, gain1, shift1))
    sum_bup = bup0 + bup1
    sum_bqkv, sum_gain, sum_shift = [jnp.sum(a + b, axis=-2) for a, b in zip(*sums)]

    mine = jnp.arange(NZ) == z
    sum_cot = jnp.sum(cotangent.astype(F32), axis=(0, 1, 2)).reshape(128, 8)
    sum_bqkv = jnp.where(mine[None, :, None], sum_bqkv.reshape(3, 1, 256), 0.0)
    sum_bup = jnp.where(mine[:, None], jnp.sum(sum_bup, axis=0)[None, :], 0.0)
    parts = (
        sum_bqkv.reshape(128, 24),
        sum_cot,
        sum_bup.reshape(128, 32),
        sum_cot,
        sum_gain.reshape(128, 8),
        sum_shift.reshape(128, 8),
    )
    vec_grads = jnp.stack(
        [jnp.pad(p, ((0, 0), (0, 128 - p.shape[1]))) for p in parts] + [jnp.zeros((128, 128), F32)] * 2,
        axis=1,
    ).reshape(1024, 128)
    mlp = in_vmem(
        to_y_kernel,
        "to_y",
        (mlp,),
        [((32, 2048), BF)] * 4,
        lax.axis_index("y").astype(jnp.int32).reshape(1),
    )
    mlp = exchange(mlp, "y")
    (att,) = in_vmem(
        to_xy_kernel,
        "to_xy",
        (att[0], send(att[1], "c", 1), vec_grads, send(vec_grads, "c", 1)),
        [((16, 32, 1152), BF)],
        c,
        limit=32,
    )
    att = lax.all_to_all(att, ("x", "y"), 0, 0, tiled=True)
    home, rows_home = in_vmem(
        to_z_kernel,
        "to_z",
        (att, *mlp),
        [((4, 8, 1920), BF), ((40, 1024), F32)],
    )
    home = lax.all_to_all(home, "z", 0, 0, tiled=True)
    rows_home = lax.ppermute(rows_home, ("x", "y", "c", "z"), back_home)
    final_up, final_qkv, *final_vectors = in_vmem(
        home_kernel,
        "home",
        (home,),
        [((8, 4096), F32), ((8, 3072), F32)] + [((n,), F32) for n in (24, 8, 32, 8, 8, 8)],
    )
    half = finish(0, hidden_in, cotangent, sum0, vecs, ())
    out_hidden, grad_input = finish(1, hidden_in, cotangent, sum1, vecs, half, (final_up,))
    out_hidden, grad_input = out_hidden[:, None], grad_input[:, None]
    return (
        out_hidden,
        grad_input,
        final_qkv,
        rows_home[32:],
        final_up,
        rows_home[:32],
        *final_vectors,
    )


def solution(mesh):
    parts = jax.sharding.Mesh(mesh.devices.reshape(4, 4, 2, NZ), ("x", "y", "c", "z"))
    dp = ("x", "y", "c")
    rows = P(None, dp, "z", None)
    tokens = P(None, dp, None)
    matrix = P(dp + ("z",), None)
    vector = P(dp + ("z",))
    in_specs = (rows, tokens, tokens) + (matrix,) * 4 + (vector,) * 6 + (rows,)
    out_specs = (rows, rows) + (matrix,) * 4 + (vector,) * 6
    return jax.shard_map(body, mesh=parts, in_specs=in_specs, out_specs=out_specs, check_vma=False)
```

```python
import functools

import jax
import jax.numpy as jnp
from jax import lax
from jax.experimental import pallas as pl
from jax.experimental.pallas import tpu as pltpu
from jax.sharding import PartitionSpec as P

BF = jnp.bfloat16
F32 = jnp.float32
MB = 1 << 20
HEAD_DIM = 64
ROT = 32
NZ = 4


def dot(left, right):
    return jnp.dot(left, right, preferred_element_type=F32)


def dot_nt(left, right):
    return lax.dot_general(left, right, (((1,), (1,)), ((), ())), preferred_element_type=F32)


def dot_tn(left, right):
    return lax.dot_general(left, right, (((0,), (0,)), ((), ())), preferred_element_type=F32)


def turn(value, cos, sin, sign):
    right, left = pltpu.roll(value, 16, 1), pltpu.roll(value, 112, 1)
    first = lax.broadcasted_iota(jnp.int32, value.shape, 1) % 32 < 16
    return value * cos + jnp.where(first, left, right) * (sign * sin)


def spread(value, period):
    while period < 128:
        value = value + pltpu.roll(value, period, 1)
        period *= 2
    return value


def lay_out(value, period):
    fold = 128 // period
    lane = lax.broadcasted_iota(jnp.int32, value.shape, 1) // period
    row = lax.broadcasted_iota(jnp.int32, value.shape, 0) % fold
    value = jnp.where(lane == row, spread(value, period), 0.0)
    value = jnp.sum(value.reshape(8, fold, 128), axis=1)
    return jnp.concatenate([value[t : t + 1] for t in range(8)], axis=1)


def unpack_parameters(z, w_ref, wo_ref, vec_ref, block_s):
    rows = w_ref[:, 2816:3072].astype(F32).reshape(32, 4, 8, 256)
    for b in range(4):
        wo_ref[:, b * 256 : b * 256 + 256] = rows[:, b].reshape(256, 256).astype(BF)
    block_s[...] = w_ref[:, 3072:3200].astype(F32)

    def kind(k, first=0, count=128):
        return block_s[pl.ds(first * 8 + k, count, stride=8), :]

    vec_ref[0:1, :] = lay_out(kind(4), 8)
    vec_ref[1:2, :] = lay_out(kind(5), 8)
    vec_ref[2:3, :] = lay_out(kind(2, z * 32, 32), 32)
    vec_ref[4:5, :] = lay_out(kind(1) + kind(3), 8)
    lane = lax.broadcasted_iota(jnp.int32, (128, 128), 1)
    row = lax.broadcasted_iota(jnp.int32, (128, 128), 0)
    qkv = kind(0)
    groups = []
    for g in range(3):
        here = jnp.where(lane < 8, pltpu.roll(qkv, 128 - 8 * g, 1) if g else qkv, 0.0)
        groups.append(spread(here, 8))
    for part in range(3):
        for half in range(2):
            want = (part * 8 + z * 2 + half) * 16 + lane // 8
            total = jnp.zeros((128, 128), F32)
            for g in range(3):
                total = total + jnp.where(3 * row + g == want, groups[g], 0.0)
            at = part * 256 + half * 128
            vec_ref[3:4, at : at + 128] = jnp.sum(total, axis=0, keepdims=True)


def front_kernel(known, z_ref, *rest):
    z = z_ref[0]
    step = pl.program_id(0)
    if not known:
        rest, (wo_ref, vec_ref, block_s) = rest[:-3], rest[-3:]
    x_ref, c_ref, n_ref, act_ref, dup_ref, q_ref, k_ref, v_ref, dm_ref, stat_ref, sum_ref = rest[
        -11:
    ]
    tile = x_ref.shape[1]
    for at, piece in enumerate(rest[:NZ]):

        @pl.when(step == at)
        def _(piece=piece):
            x_ref[0], c_ref[0] = piece[:tile], piece[tile:]

    w_ref = rest[NZ]
    if known:
        wo_ref, vec_ref, cos_ref, sin_ref = rest[NZ + 1 : NZ + 5]
    else:
        cos_ref, sin_ref = rest[NZ + 1 : NZ + 3]

        @pl.when(step == 0)
        def _():
            unpack_parameters(z, w_ref, wo_ref, vec_ref, block_s)

    gain_ref, shift_ref, bu_ref, bq_ref = [vec_ref.at[k : k + 1] for k in range(4)]

    @pl.when(step == 0)
    def _():
        sum_ref[...] = jnp.zeros_like(sum_ref)

    def put(ref, value):
        for r in range(tile // 256):
            row = lax.rem(pl.program_id(0) * (tile // 256) + r + z, 4) * 256
            ref[0, pl.ds(pl.multiple_of(row, 256), 256), :] = value[r * 256 : r * 256 + 256]

    def d_act_of(j):
        return dot_nt(c_ref[0], w_ref[j * 256 : j * 256 + 256, 1792:2816])

    def in_of(j):
        return dot(n_ref[0], w_ref[:, j * 256 : j * 256 + 256])

    d_act = d_act_of(0)
    d_mixed = dot_nt(c_ref[0], wo_ref[...])
    x = x_ref[0].astype(F32)
    average = jnp.mean(x, axis=-1, keepdims=True)
    centered = x - average
    spread = jnp.mean(centered * centered, axis=-1, keepdims=True)
    rs = lax.rsqrt(spread + 1e-05)
    stat_ref[0, :, 0:1] = average
    stat_ref[0, :, 1:2] = rs
    n_ref[0] = (centered * rs * gain_ref[...] + shift_ref[...]).astype(BF)
    put(dm_ref, d_mixed.astype(BF))
    up = in_of(0)
    k0 = 0.7978845608028654
    k1 = k0 * 0.044715
    for j in range(4):
        cols = slice(j * 256, j * 256 + 256)
        if j < 3:
            next_up, next_act = in_of(j + 1), d_act_of(j + 1)
        else:
            q, k, v = in_of(4), in_of(5), in_of(6)
        up = up + bu_ref[:, cols]
        square = up * up
        half = 0.5 + 0.5 * jnp.tanh(up * (k0 + k1 * square))
        act = up * half
        slope = half + 2.0 * act * (1.0 - half) * (k0 + 3.0 * k1 * square)
        d_up = (slope * d_act).astype(BF)
        act_ref[0, :, cols] = act.astype(BF)
        dup_ref[0, :, cols] = d_up
        back = d_up.astype(F32)
        sum_ref[:, cols] += jnp.sum(back.reshape(back.shape[0] // 8, 8, 256), axis=0)
        up, d_act = next_up, next_act
    tabs = (cos_ref[0], sin_ref[0])
    def turn_both(value):
        return jnp.concatenate(
            [turn(value[:, h : h + 128], *tabs, 1.0) for h in (0, 128)], axis=1
        ).astype(BF)

    q = turn_both(q + bq_ref[:, 0:256]) * BF(0.125)
    put(q_ref, q)
    put(k_ref, turn_both(k + bq_ref[:, 256:512]))
    put(v_ref, (v + bq_ref[:, 512:768]).astype(BF))


ANY = pl.BlockSpec(memory_space=pl.ANY)
QUICK = pl.CostEstimate(flops=1024, bytes_accessed=1024, transcendentals=0)


def front(z, pieces, weights, known, cos, sin, after, limit):
    tile, d = pieces[0].shape[-2] // 2, pieces[0].shape[-1]
    n = tile * NZ

    def tok(width):
        return pl.BlockSpec((1, tile, width), lambda j, z: (0, j, 0))

    def turned(width):
        return pl.BlockSpec((1, tile, width), lambda j, z: (0, lax.rem(j + z[0], NZ), 0))

    def row(width):
        return pl.BlockSpec((1, n, width), lambda j, z: (0, 0, 0))

    def whole(a):
        return pl.BlockSpec(a.shape, lambda j, z: (0, 0), pipeline_mode=pl.Buffered(1))

    def keep(*shape):
        return pl.BlockSpec(shape, lambda j, z: (0, 0))

    first = [whole(a) for a in pieces]
    fixed = (weights, *known)
    out_specs = [tok(d)] * 5 + [row(256)] * 4 + [tok(128), keep(8, 1024)]
    out_shape = [jax.ShapeDtypeStruct((1, n, w), BF) for w in [d] * 5 + [256] * 4]
    out_shape += [jax.ShapeDtypeStruct((1, n, 128), F32), jax.ShapeDtypeStruct((8, 1024), F32)]
    scratch = []
    if not known:
        out_specs += [keep(256, d), keep(8, d)]
        out_shape += [jax.ShapeDtypeStruct((256, d), BF), jax.ShapeDtypeStruct((8, d), F32)]
        scratch = [pltpu.VMEM((1024, 128), F32)]
    return pl.pallas_call(
        functools.partial(front_kernel, bool(known)),
        grid_spec=pltpu.PrefetchScalarGridSpec(
            num_scalar_prefetch=1,
            grid=(NZ,),
            in_specs=first + [whole(a) for a in fixed] + [turned(128)] * 2 + [ANY] * len(after),
            out_specs=out_specs,
            scratch_shapes=scratch,
        ),
        out_shape=out_shape,
        compiler_params=pltpu.CompilerParams(vmem_limit_bytes=limit * MB),
        cost_estimate=QUICK,
        name="front",
    )(z, *pieces, *fixed, cos, sin, *after)


def attend_kernel(
    z_ref, q_ref, k_ref, v_ref, dm_ref, row_ref, key_ref, cos_ref, sin_ref, *rest,
):
    mixed_ref, dqkv_ref, sum_ref, bias_s, s_s, dp_s, p_s, ds_s, qm_s, dmm_s, dk_s, dv_s = rest[-12:]
    B = 256
    z = z_ref[0]
    sum_ref[...] = jnp.zeros_like(sum_ref)

    def put(part, a, value):
        rows = pl.ds(pl.multiple_of(lax.rem(a - z + 4, 4) * B, B), B)
        if part is None:
            mixed_ref[0, rows, :] = value
        else:
            dqkv_ref[0, part, rows, :] = value
            sum_ref[part, 0:1, :] += jnp.sum(value.astype(F32), axis=0, keepdims=True)

    key_col = key_ref[0].T
    lane_head = lax.broadcasted_iota(jnp.int32, (B, 128), 1) // 64
    diff = lax.broadcasted_iota(jnp.int32, (B, B), 0) - lax.broadcasted_iota(jnp.int32, (B, B), 1)

    def prepare(aq):
        par, n, here = aq % 2, (aq + 1) * B, slice(aq * B, aq * B + B)
        bias = jnp.where(key_col[0:n, 0:1] == row_ref[0, 0:1, here], 0.0, -1e30)
        if aq:
            bias_s[par, 0 : aq * B, :] = bias[: aq * B]
        edge = jnp.where(diff <= 0, bias[aq * B :], -1e30)
        bias_s[par, here, :] = jnp.where(diff == 0, 0.0, edge)
        q_all, d_all = q_ref[0, here, :], dm_ref[0, here, :]
        for h in range(2):
            cols = slice(h * B, h * B + B)
            qm_s[par, cols, :] = jnp.where(lane_head == h, q_all, jnp.zeros_like(q_all))
            dmm_s[par, cols, :] = jnp.where(lane_head == h, d_all, jnp.zeros_like(d_all))

    def products(aq, h):
        par, n, cols = aq % 2, (aq + 1) * B, slice(h * B, h * B + B)
        s = dot_nt(k_ref[0, 0:n, :], qm_s[par, cols, :]) + bias_s[par, 0:n, :]
        s_s[h, 0:n] = s
        dp_s[h, 0:n] = dot_nt(v_ref[0, 0:n, :], dmm_s[par, cols, :])
        return jnp.max(s, axis=0, keepdims=True)

    def soften(aq, h, top):
        par, n, cols = aq % 2, (aq + 1) * B, slice(h * B, h * B + B)
        e = jnp.exp(s_s[h, 0:n] - top)
        s_s[h, 0:n] = e
        inv = 1.0 / jnp.sum(e, axis=0, keepdims=True)
        mean = jnp.sum(e * dp_s[h, 0:n], axis=0, keepdims=True) * inv
        p = s_s[h, 0:n] * inv
        p_s[par, 0:n, cols] = p.astype(BF)
        ds_s[par, 0:n, cols] = (p * (dp_s[h, 0:n] - mean)).astype(BF)

    def pick(value):
        return jnp.where(lane_head == 0, value[0:B], value[B:])

    def gather(aq, part):
        par, n, here = aq % 2, (aq + 1) * B, slice(aq * B, aq * B + B)
        if part == 0:
            put(None, aq, pick(dot_tn(p_s[par, 0:n, :], v_ref[0, 0:n, :])).astype(BF))
        elif part == 1:
            dq = pick(dot_tn(ds_s[par, 0:n, :], k_ref[0, 0:n, :])) * 0.125
            put(0, aq, turn(dq, cos_ref[0, here, :], sin_ref[0, here, :], -1.0).astype(BF))
        else:
            left, right, to = (p_s, dmm_s, dv_s) if part == 2 else (ds_s, qm_s, dk_s)
            value = dot(left[par, 0:n, :], right[par])
            if aq:
                to[0 : aq * B, :] += value[: aq * B]
            to[here, :] = value[aq * B :]

    prepare(0)
    top = products(0, 0)
    for aq in range(4):
        ahead = products(aq, 1)
        if aq:
            gather(aq - 1, 0)
            gather(aq - 1, 1)
        soften(aq, 0, top)
        if aq:
            gather(aq - 1, 2)
            gather(aq - 1, 3)
        if aq < 3:
            prepare(aq + 1)
            top = products(aq + 1, 0)
        soften(aq, 1, ahead)
    for part in range(4):
        gather(3, part)
    for a in range(4):
        here = slice(a * B, a * B + B)
        put(1, a, turn(dk_s[here, :], cos_ref[0, here, :], sin_ref[0, here, :], -1.0).astype(BF))
        put(2, a, dv_s[here, :].astype(BF))


def attend(z, q, k, v, dm, seg_row, seg_key, cos, sin, after, limit):
    n = q.shape[1]
    half = pl.BlockSpec((1, n, 128), lambda g, z: (0, 0, g))
    table = pl.BlockSpec((1, n, 128), lambda g, z: (0, 0, 0))
    line = pl.BlockSpec((1, 8, n), lambda g, z: (0, 0, 0))
    S = pltpu.VMEM
    return pl.pallas_call(
        attend_kernel,
        grid_spec=pltpu.PrefetchScalarGridSpec(
            num_scalar_prefetch=1,
            grid=(2,),
            in_specs=[half] * 4 + [line] * 2 + [table] * 2 + [ANY] * len(after),
            out_specs=[
                half,
                pl.BlockSpec((1, 3, n, 128), lambda g, z: (0, 0, 0, g)),
                pl.BlockSpec((3, 8, 128), lambda g, z: (0, 0, g)),
            ],
            scratch_shapes=[
                S((2, n, 256), F32), S((2, n, 256), F32), S((2, n, 256), F32),
                S((2, n, 512), BF), S((2, n, 512), BF),
                S((2, 512, 128), BF), S((2, 512, 128), BF),
                S((n, 128), F32), S((n, 128), F32),
            ],
        ),
        out_shape=[
            jax.ShapeDtypeStruct((1, n, 256), BF),
            jax.ShapeDtypeStruct((1, 3, n, 256), BF),
            jax.ShapeDtypeStruct((3, 8, 256), F32),
        ],
        compiler_params=pltpu.CompilerParams(vmem_limit_bytes=limit * MB),
        cost_estimate=QUICK,
        name="attend",
    )(z, q, k, v, dm, seg_row, seg_key, cos, sin, *after)


def back_kernel(
    z_ref, act_ref, mix_ref, dup_ref, dqkv_ref, x_ref, stat_ref, wd_ref, wo_ref, wi_ref, *rest,
):
    cut, gain_ref, shift_ref = rest[-3:]
    z = z_ref[0]
    out = dot(act_ref[0], wd_ref[...]) + dot(mix_ref[0], wo_ref[...])
    dn = dot_nt(dup_ref[0], wi_ref[:, 0:1024])
    for part in range(3):
        at = 1024 + part * 256
        dn = dn + dot_nt(dqkv_ref[0, part], wi_ref[:, at : at + 256])
    xhat = (x_ref[0].astype(F32) - stat_ref[0, :, 0:1]) * stat_ref[0, :, 1:2]
    gain_ref[...] = jnp.sum((dn * xhat).reshape(-1, 8, 256), axis=0)
    shift_ref[...] = jnp.sum(dn.reshape(-1, 8, 256), axis=0)
    for r in range(NZ):
        rows = slice(r * 256, r * 256 + 256)
        first = pl.multiple_of(lax.rem(r + z, NZ) * 512, 512)
        cut[pl.ds(first, 256), :] = out[rows].astype(BF)
        cut[pl.ds(first + 256, 256), :] = dn[rows].astype(BF)


def back(z, act, mixed, d_up, d_qkv, x, stat, weights, w_o, after, limit):
    def rows(a):
        return pl.BlockSpec(a.shape, lambda j, z: (0,) * a.ndim, pipeline_mode=pl.Buffered(1))

    def cols(n, first=0):
        return pl.BlockSpec((n, 256), lambda j, z: (0, first + j))

    return pl.pallas_call(
        back_kernel,
        grid_spec=pltpu.PrefetchScalarGridSpec(
            num_scalar_prefetch=1,
            grid=(4,),
            in_specs=[rows(a) for a in (act, mixed, d_up, d_qkv)]
            + [
                pl.BlockSpec((1, 1024, 256), lambda j, z: (0, 0, j)),
                rows(stat),
                cols(1024, 7),
                cols(256),
                pl.BlockSpec((256, 1792), lambda j, z: (j, 0)),
            ]
            + [ANY] * len(after),
            out_specs=[cols(2048)] + [cols(8)] * 2,
        ),
        out_shape=[jax.ShapeDtypeStruct((2048, 1024), BF)]
        + [jax.ShapeDtypeStruct((8, 1024), F32)] * 2,
        compiler_params=pltpu.CompilerParams(vmem_limit_bytes=limit * MB),
        cost_estimate=QUICK,
        name="back",
    )(z, act, mixed, d_up, d_qkv, x, stat, weights, w_o, weights, *after)


def put_halves(c, value, own_ref, other_ref, lo):
    value = value.reshape(4, 2, 32, value.shape[1])
    first, second = [value[:, k].reshape(128, value.shape[3]) for k in range(2)]
    hi = lo + value.shape[3]
    own_ref[:, lo:hi] = jnp.where(c == 0, first, second).astype(BF)
    other_ref[:, lo:hi] = jnp.where(c == 0, second, first).astype(BF)


def grads_mlp0_kernel(n_ref, dup_ref, act_ref, cot_ref, *rest):
    rest[-1][:, 0:1024] = dot_tn(n_ref[0], dup_ref[0]).astype(BF)
    rest[-1][:, 1024:2048] = dot_tn(act_ref[0], cot_ref[0]).astype(BF)


def grads_mlp1_kernel(c_ref, n_ref, dup_ref, act_ref, cot_ref, sum_ref, own_ref, other_ref):
    c = c_ref[0]
    up = sum_ref[:, 0:1024].astype(F32) + dot_tn(n_ref[0], dup_ref[0])
    put_halves(c, up, own_ref, other_ref, 0)
    down = sum_ref[:, 1024:2048].astype(F32) + dot_tn(act_ref[0], cot_ref[0])
    put_halves(c, down, own_ref, other_ref, 1024)


def grads_mlp0(normed, d_up, act, cot, after):
    tokens, width = normed.shape[1:]
    part = pl.BlockSpec((1, tokens, 256), lambda i: (0, 0, i))
    whole = pl.BlockSpec(d_up.shape, lambda i: (0, 0, 0), pipeline_mode=pl.Buffered(1))
    return pl.pallas_call(
        grads_mlp0_kernel,
        grid=(width // 256,),
        in_specs=[part, whole, part, whole] + [ANY] * len(after),
        out_specs=pl.BlockSpec((256, 2048), lambda i: (i, 0)),
        out_shape=jax.ShapeDtypeStruct((width, 2048), BF),
        compiler_params=pltpu.CompilerParams(vmem_limit_bytes=24 * MB),
        cost_estimate=QUICK,
        name="grads_mlp0",
    )(normed, d_up, act, cot, *after)


def grads_mlp1(c, normed, d_up, act, cot, first):
    tokens, width = normed.shape[1:]
    part = pl.BlockSpec((1, tokens, 256), lambda i, c: (0, 0, i))
    whole = pl.BlockSpec(d_up.shape, lambda i, c: (0, 0, 0), pipeline_mode=pl.Buffered(1))
    return pl.pallas_call(
        grads_mlp1_kernel,
        grid_spec=pltpu.PrefetchScalarGridSpec(
            num_scalar_prefetch=1,
            grid=(width // 256,),
            in_specs=[part, whole, part, whole, pl.BlockSpec((256, 2048), lambda i, c: (i, 0))],
            out_specs=[pl.BlockSpec((128, 2048), lambda i, c: (i, 0))] * 2,
        ),
        out_shape=[jax.ShapeDtypeStruct((width // 2, 2048), BF)] * 2,
        compiler_params=pltpu.CompilerParams(vmem_limit_bytes=46 * MB),
        cost_estimate=QUICK,
        name="grads_mlp1",
    )(c, normed, d_up, act, cot, first)


def grads_att_kernel(
    c_ref, n0_ref, n1_ref, dqkv0_ref, dqkv1_ref, mix0_ref, mix1_ref, cot0_ref, cot1_ref,
    *rest,
):
    own_ref, other_ref, out_s = rest[-3:]
    c = c_ref[0]
    i = pl.program_id(0)

    @pl.when(i == 0)
    def _():
        out_s[...] = dot_tn(mix0_ref[0], cot0_ref[0]) + dot_tn(mix1_ref[0], cot1_ref[0])

    for part in range(3):
        both = dot_tn(n0_ref[0], dqkv0_ref[0, part]) + dot_tn(n1_ref[0], dqkv1_ref[0, part])
        put_halves(c, both, own_ref, other_ref, part * 256)
    rows = out_s[pl.ds(pl.multiple_of(i * 64, 64), 64), :]
    rows = [rows[d * 8 : d * 8 + 8, b * 256 : b * 256 + 256] for d in range(8) for b in range(4)]
    put_halves(c, jnp.concatenate(rows), own_ref, other_ref, 768)


def grads_att(c, normed, d_qkv, mixed, cot, after):
    tokens, width = normed[0].shape[1:]

    def whole(a):
        return pl.BlockSpec(a.shape, lambda i, c: (0,) * a.ndim, pipeline_mode=pl.Buffered(1))

    return pl.pallas_call(
        grads_att_kernel,
        grid_spec=pltpu.PrefetchScalarGridSpec(
            num_scalar_prefetch=1,
            grid=(4,),
            in_specs=[pl.BlockSpec((1, tokens, 256), lambda i, c: (0, 0, i))] * 2
            + [whole(a) for a in (*d_qkv, *mixed, *cot)]
            + [ANY] * len(after),
            out_specs=[pl.BlockSpec((128, 1024), lambda i, c: (i, 0))] * 2,
            scratch_shapes=[pltpu.VMEM((256, 1024), F32)],
        ),
        out_shape=[jax.ShapeDtypeStruct((512, 1024), BF)] * 2,
        compiler_params=pltpu.CompilerParams(vmem_limit_bytes=58 * MB),
        cost_estimate=QUICK,
        name="grads_att",
    )(c, *normed, *d_qkv, *mixed, *cot, *after)


def finish_kernel(x_ref, c_ref, vec_ref, part_ref, *rest):
    out_ref, dx_ref = rest[-2:]
    x = x_ref[0, 0].astype(F32)
    branch, g = part_ref[0].astype(F32), part_ref[1].astype(F32)
    out_ref[0] = (x + (branch + vec_ref[4:5, :])).astype(BF)
    centered = x - jnp.mean(x, axis=-1, keepdims=True)
    rs = lax.rsqrt(jnp.mean(centered * centered, axis=-1, keepdims=True) + 1e-05)
    xhat = centered * rs
    g = g * vec_ref[0:1, :]
    mean_g = jnp.mean(g, axis=-1, keepdims=True)
    mean_gx = jnp.mean(g * xhat, axis=-1, keepdims=True)
    dx_ref[0] = c_ref[0, 0].astype(F32) + rs * (g - mean_g - xhat * mean_gx)


def finish(micro, x, cot, part, vectors, others, after=()):
    n, d = x.shape[2:]
    tile = pl.BlockSpec((1, 1, 256, d), lambda i: (micro, 0, i, 0))
    out = pl.BlockSpec((1, 256, d), lambda i: (micro, i, 0))
    return pl.pallas_call(
        finish_kernel,
        grid=(n // 256,),
        in_specs=[tile] * 2
        + [
            pl.BlockSpec((8, d), lambda i: (0, 0)),
            pl.BlockSpec((2, 256, d), lambda i: (0, i, 0)),
        ]
        + [ANY] * (len(others) + len(after)),
        out_specs=[out] * 2,
        out_shape=[jax.ShapeDtypeStruct((2, n, d), BF), jax.ShapeDtypeStruct((2, n, d), F32)],
        input_output_aliases={4 + k: k for k in range(len(others))},
        compiler_params=pltpu.CompilerParams(vmem_limit_bytes=58 * MB),
        cost_estimate=QUICK,
        name="finish",
    )(x, cot, vectors, part.reshape(2, n, d), *others, *after)


def add_kernel(a_ref, b_ref, *rest):
    rest[-1][...] = (a_ref[...].astype(F32) + b_ref[...].astype(F32)).astype(BF)


def add_after(a, b, after):
    n, d = a.shape
    part = pl.BlockSpec((n // 4, d), lambda i: (i, 0))
    return pl.pallas_call(
        add_kernel,
        grid=(4,),
        in_specs=[part, part] + [ANY] * len(after),
        out_specs=part,
        out_shape=jax.ShapeDtypeStruct((n, d), BF),
        compiler_params=pltpu.CompilerParams(vmem_limit_bytes=32 * MB),
        cost_estimate=QUICK,
        name="add_after",
    )(a, b, *after)


def to_columns_kernel(z_ref, up_ref, qkv_ref, down_ref, out_ref, *rest):
    vectors, rows_ref, pieces = rest[:6], rest[6], rest[7:]
    lines = [v[...].astype(F32).reshape(1, -1) for v in vectors]
    lines = [jnp.concatenate([v, jnp.zeros((1, 128 - v.shape[1]), F32)], axis=1) for v in lines]
    block = jnp.concatenate(lines + [jnp.zeros((2, 128), F32)], axis=0).astype(BF)
    for k, piece in enumerate(pieces):
        to = lax.rem(z_ref[0] + k, NZ)
        piece[:, 0:1024] = up_ref[:, pl.ds(pl.multiple_of(to * 1024, 1024), 1024)]
        for part in range(3):
            first = pl.multiple_of(part * 1024 + to * 256, 256)
            at = 1024 + part * 256
            piece[:, at : at + 256] = qkv_ref[:, pl.ds(first, 256)]
        piece[:, 1792:1920] = block
    rows = jnp.concatenate([down_ref[...].astype(F32), out_ref[...].astype(F32)], axis=0)
    rows_ref[...] = rows.astype(BF)


def to_payload_kernel(z_ref, g0_ref, g1_ref, g2_ref, g3_ref, rows_ref, after_ref, out_ref):
    got = [g[...].astype(F32) for g in (g0_ref, g1_ref, g2_ref, g3_ref)]
    columns = []
    for source in range(NZ):
        k = lax.rem(z_ref[0] - source + NZ, NZ)
        value = got[3]
        for j in range(3):
            value = jnp.where(k == j, got[j], value)
        columns.append(value)
    columns = jnp.concatenate(columns, axis=0)
    rows = rows_ref[...].astype(F32)
    w_out = jnp.concatenate([rows[32:40, b * 256 : b * 256 + 256] for b in range(4)], axis=0)
    out_ref[:, 0:1792] = columns[:, 0:1792].astype(BF)
    out_ref[:, 1792:2816] = rows[0:32].astype(BF)
    out_ref[:, 2816:3072] = w_out.astype(BF)
    out_ref[:, 3072:3200] = columns[:, 1792:1920].astype(BF)


def total_of(refs, rows):
    return sum([r[rows, :].astype(F32) for r in refs[1:]], refs[0][rows, :].astype(F32))


def to_xy_kernel(c_ref, own_ref, got_ref, va_ref, vb_ref, out_ref):
    total = total_of((own_ref, got_ref), slice(None))
    out_ref[:, :, 0:1024] = total.astype(BF).reshape(16, 32, 1024)
    vec = (va_ref[...] + vb_ref[...]).reshape(16, 2, 32, 128)
    out_ref[:, :, 1024:1152] = jnp.where(c_ref[0] == 0, vec[:, 0], vec[:, 1]).astype(BF)


def to_y_kernel(at_ref, mlp_ref, *outs):
    for k, out in enumerate(outs):
        rows = pl.ds(pl.multiple_of(lax.rem(at_ref[0] + k, 4) * 32, 32), 32)
        out[...] = mlp_ref[rows, :]


def to_z_kernel(att_ref, a_ref, b_ref, c_ref, d_ref, home_ref, rows_ref):
    mlp = total_of((a_ref, b_ref, c_ref, d_ref), slice(0, 32))
    att = att_ref[0].astype(F32)
    for k in range(1, 16):
        att = att + att_ref[k].astype(F32)
    home = jnp.concatenate([mlp[:, :1024], att[:, :768], att[:, 1024:1152]], axis=1)
    home_ref[...] = home.reshape(4, 8, 1920).astype(BF)
    rows_ref[0:32, :] = mlp[:, 1024:2048]
    out = att[:, 768:1024].reshape(4, 8, 256)
    for b in range(4):
        rows_ref[32:40, b * 256 : b * 256 + 256] = out[b]


def home_kernel(home_ref, up_ref, qkv_ref, *vectors):
    for k in range(NZ):
        up_ref[:, k * 1024 : k * 1024 + 1024] = home_ref[k, :, 0:1024].astype(F32)
        for part in range(3):
            at = part * 1024 + k * 256
            own = 1024 + part * 256
            qkv_ref[:, at : at + 256] = home_ref[k, :, own : own + 256].astype(F32)
    total = jnp.sum(home_ref[:, :, 1792:1920].astype(F32), axis=0)
    for k, ref in enumerate(vectors):
        ref[...] = total[k, : ref.shape[0]]


def in_vmem(kernel, name, operands, shapes, scalars=None, after=(), limit=58):
    def whole(shape):
        return pl.BlockSpec(shape, lambda i: (0,) * len(shape))

    specs = [whole(a.shape) for a in operands] + [ANY] * len(after)
    operands = (*operands, *after)
    if scalars is not None:
        specs = [pl.BlockSpec(memory_space=pltpu.SMEM)] + specs
        operands = (scalars, *operands)
    return pl.pallas_call(
        kernel,
        grid=(1,),
        in_specs=specs,
        out_specs=[whole(s[0]) for s in shapes],
        out_shape=[jax.ShapeDtypeStruct(*s) for s in shapes],
        compiler_params=pltpu.CompilerParams(vmem_limit_bytes=limit * MB),
        cost_estimate=QUICK,
        name=name,
    )(*operands)


def pack_kernel(a_ref, b_ref, *rest):
    rest[-1][0] = a_ref[0, 0]
    rest[-1][1] = b_ref[0, 0]


def pack(micro, a, b, after):
    n, d = a.shape[2:]
    part = pl.BlockSpec((1, 1, n // 2, d), lambda i: (micro, 0, i, 0))
    return pl.pallas_call(
        pack_kernel,
        grid=(2,),
        in_specs=[part, part] + [ANY] * len(after),
        out_specs=pl.BlockSpec((2, n // 2, d), lambda i: (0, i, 0)),
        out_shape=jax.ShapeDtypeStruct((2, n, d), BF),
        compiler_params=pltpu.CompilerParams(vmem_limit_bytes=58 * MB),
        cost_estimate=QUICK,
        name="pack",
    )(a, b, *after).reshape(2 * n, d)


def doc_positions(seg_row):
    length = seg_row.shape[-1]
    token_index = jnp.arange(length, dtype=jnp.int32)
    previous = jnp.concatenate([seg_row[..., :1], seg_row[..., :-1]], axis=-1)
    starts = jnp.where((token_index == 0) | (seg_row != previous), token_index, 0)
    doc_start = lax.cummax(starts, axis=seg_row.ndim - 1)
    return token_index - doc_start


def rotary_tables(positions):
    dim = jnp.arange(128, dtype=jnp.int32) % HEAD_DIM
    frequency = 10000.0 ** (-(dim % (ROT // 2)).astype(F32) * 2.0 / ROT)
    frequency = jnp.where(dim < ROT, frequency, 0.0)
    angles = positions.astype(F32)[..., None] * frequency
    return jnp.cos(angles), jnp.sin(angles) * jnp.where(dim < ROT // 2, -1.0, 1.0)


def send(value, axis, step):
    size = lax.axis_size(axis)
    return lax.ppermute(value, axis, [(i, (i + step) % size) for i in range(size)])


def exchange(parts, axis):
    return [parts[0]] + [send(parts[k], axis, k) for k in range(1, 4)]


def body(
    hidden_in,
    segments,
    valid_mask,
    w_qkv,
    w_out,
    w_up,
    w_down,
    b_qkv,
    b_out,
    b_up,
    b_down,
    ln_gain,
    ln_shift,
    cotangent,
):
    z = lax.axis_index("z")
    c = lax.axis_index("c").astype(jnp.int32).reshape(1)
    micro_count, _, group, width = hidden_in.shape
    row_len = group * NZ
    z_arr = z.astype(jnp.int32).reshape(1)

    w_rows, *columns = in_vmem(
        to_columns_kernel,
        "to_columns",
        (w_up, w_qkv, w_down, w_out, b_qkv, b_out, b_up, b_down, ln_gain, ln_shift),
        [((40, 1024), BF)] + [((8, 1920), BF)] * 4,
        z_arr,
    )
    there, back_home = [], []
    for d in range(32):
        for s in range(4):
            pair = (d * 4 + s, ((d % 8) * 4 + s) * 4 + d // 8)
            there.append(pair)
            back_home.append(pair[::-1])
    columns = exchange(columns, "z")
    w_rows = lax.ppermute(w_rows, ("x", "y", "c", "z"), there)
    mine0 = pack(0, hidden_in, cotangent, ())
    (payload,) = in_vmem(
        to_payload_kernel,
        "to_payload",
        (*columns, w_rows),
        [((32, 3200), BF)],
        z_arr,
        after=(mine0,),
    )
    weights = lax.all_gather(payload, ("x", "y", "c"), axis=0, tiled=True)

    pieces0 = [mine0] + [send(mine0, "z", -step) for step in range(1, NZ)]
    mine1 = pack(1, hidden_in, cotangent, (pieces0[2],))
    pieces1 = [mine1] + [send(mine1, "z", -step) for step in range(1, NZ)]

    seg = segments[:, 0]
    key_seg = jnp.where(valid_mask[:, 0] > 0, seg, -1)
    seg_row, seg_key = [
        jnp.broadcast_to(s.astype(F32)[:, None, :], (micro_count, 8, row_len)) for s in (seg, key_seg)
    ]
    tables = rotary_tables(doc_positions(seg))

    tables = [[t[m : m + 1] for t in tables] for m in range(micro_count)]

    lines = [[s[m : m + 1] for s in (seg_row, seg_key)] for m in range(micro_count)]

    def run_attend(m, heads, after, limit):
        return attend(z_arr, *heads, *lines[m], *tables[m], after, limit)

    hid0, cot0, n0, act0, dup0, *heads0, stat0, bup0, w_o, vecs = front(
        z_arr, pieces0, weights, (), *tables[0], (*lines[0], *lines[1]), 34
    )
    mix0, dqkv0, bqkv0 = run_attend(0, heads0, (), 30)
    first = grads_mlp0(n0, dup0, act0, cot0, (mix0,))
    cuts0, gain0, shift0 = back(
        z_arr, act0, mix0, dup0, dqkv0, hid0, stat0, weights, w_o, (first, *pieces1[1:]), 46
    )
    sum0 = lax.psum_scatter(cuts0, "z", scatter_dimension=0, tiled=True)
    hid1, cot1, n1, act1, dup1, *heads1, stat1, bup1 = front(
        z_arr, pieces1, weights, (w_o, vecs), *tables[1], (cuts0,), 48
    )
    cot = (cot0, cot1)
    mlp = grads_mlp1(c, n1, dup1, act1, cot1, first)
    mix1, dqkv1, bqkv1 = run_attend(1, heads1, (mlp[0],), 46)
    mlp = add_after(mlp[0], send(mlp[1], "c", 1), (mix1,))
    att = grads_att(c, (n0, n1), (dqkv0, dqkv1), (mix0, mix1), cot, (mlp,))
    mlp = lax.psum_scatter(mlp, "x", scatter_dimension=0, tiled=True)
    cuts1, gain1, shift1 = back(
        z_arr, act1, mix1, dup1, dqkv1, hid1, stat1, weights, w_o, (sum0, att[0]), 58
    )
    sum1 = lax.psum_scatter(cuts1, "z", scatter_dimension=0, tiled=True)
    sums = ((bqkv0, gain0, shift0), (bqkv1, gain1, shift1))
    sum_bup = bup0 + bup1
    sum_bqkv, sum_gain, sum_shift = [jnp.sum(a + b, axis=-2) for a, b in zip(*sums)]

    mine = jnp.arange(NZ) == z
    sum_cot = jnp.sum(cotangent.astype(F32), axis=(0, 1, 2)).reshape(128, 8)
    sum_bqkv = jnp.where(mine[None, :, None], sum_bqkv.reshape(3, 1, 256), 0.0)
    sum_bup = jnp.where(mine[:, None], jnp.sum(sum_bup, axis=0)[None, :], 0.0)
    parts = (
        sum_bqkv.reshape(128, 24),
        sum_cot,
        sum_bup.reshape(128, 32),
        sum_cot,
        sum_gain.reshape(128, 8),
        sum_shift.reshape(128, 8),
    )
    vec_grads = jnp.stack(
        [jnp.pad(p, ((0, 0), (0, 128 - p.shape[1]))) for p in parts] + [jnp.zeros((128, 128), F32)] * 2,
        axis=1,
    ).reshape(1024, 128)
    mlp = in_vmem(
        to_y_kernel,
        "to_y",
        (mlp,),
        [((32, 2048), BF)] * 4,
        lax.axis_index("y").astype(jnp.int32).reshape(1),
    )
    mlp = exchange(mlp, "y")
    (att,) = in_vmem(
        to_xy_kernel,
        "to_xy",
        (att[0], send(att[1], "c", 1), vec_grads, send(vec_grads, "c", 1)),
        [((16, 32, 1152), BF)],
        c,
        limit=32,
    )
    att = lax.all_to_all(att, ("x", "y"), 0, 0, tiled=True)
    home, rows_home = in_vmem(
        to_z_kernel,
        "to_z",
        (att, *mlp),
        [((4, 8, 1920), BF), ((40, 1024), F32)],
    )
    home = lax.all_to_all(home, "z", 0, 0, tiled=True)
    rows_home = lax.ppermute(rows_home, ("x", "y", "c", "z"), back_home)
    final_up, final_qkv, *final_vectors = in_vmem(
        home_kernel,
        "home",
        (home,),
        [((8, 4096), F32), ((8, 3072), F32)] + [((n,), F32) for n in (24, 8, 32, 8, 8, 8)],
    )
    half = finish(0, hidden_in, cotangent, sum0, vecs, ())
    out_hidden, grad_input = finish(1, hidden_in, cotangent, sum1, vecs, half, (final_up,))
    out_hidden, grad_input = out_hidden[:, None], grad_input[:, None]
    return (
        out_hidden,
        grad_input,
        final_qkv,
        rows_home[32:],
        final_up,
        rows_home[:32],
        *final_vectors,
    )


def solution(mesh):
    parts = jax.sharding.Mesh(mesh.devices.reshape(4, 4, 2, NZ), ("x", "y", "c", "z"))
    dp = ("x", "y", "c")
    rows = P(None, dp, "z", None)
    tokens = P(None, dp, None)
    matrix = P(dp + ("z",), None)
    vector = P(dp + ("z",))
    in_specs = (rows, tokens, tokens) + (matrix,) * 4 + (vector,) * 6 + (rows,)
    out_specs = (rows, rows) + (matrix,) * 4 + (vector,) * 6
    return jax.shard_map(body, mesh=parts, in_specs=in_specs, out_specs=out_specs, check_vma=False)
```

```python
import functools

import jax
import jax.numpy as jnp
from jax import lax
from jax.experimental import pallas as pl
from jax.experimental.pallas import tpu as pltpu
from jax.sharding import PartitionSpec as P

BF = jnp.bfloat16
F32 = jnp.float32
MB = 1 << 20
HEAD_DIM = 64
ROT = 32
NZ = 4


def dot(left, right):
    return jnp.dot(left, right, preferred_element_type=F32)


def dot_nt(left, right):
    return lax.dot_general(left, right, (((1,), (1,)), ((), ())), preferred_element_type=F32)


def dot_tn(left, right):
    return lax.dot_general(left, right, (((0,), (0,)), ((), ())), preferred_element_type=F32)


def turn(value, cos, sin, sign):
    right, left = pltpu.roll(value, 16, 1), pltpu.roll(value, 112, 1)
    first = lax.broadcasted_iota(jnp.int32, value.shape, 1) % 32 < 16
    return value * cos + jnp.where(first, left, right) * (sign * sin)


def spread(value, period):
    while period < 128:
        value = value + pltpu.roll(value, period, 1)
        period *= 2
    return value


def lay_out(value, period):
    fold = 128 // period
    lane = lax.broadcasted_iota(jnp.int32, value.shape, 1) // period
    row = lax.broadcasted_iota(jnp.int32, value.shape, 0) % fold
    value = jnp.where(lane == row, spread(value, period), 0.0)
    value = jnp.sum(value.reshape(8, fold, 128), axis=1)
    return jnp.concatenate([value[t : t + 1] for t in range(8)], axis=1)


def unpack_parameters(z, w_ref, wo_ref, vec_ref, block_s):
    rows = w_ref[:, 2816:3072].astype(F32).reshape(32, 4, 8, 256)
    for b in range(4):
        wo_ref[:, b * 256 : b * 256 + 256] = rows[:, b].reshape(256, 256).astype(BF)
    block_s[...] = w_ref[:, 3072:3200].astype(F32)

    def kind(k, first=0, count=128):
        return block_s[pl.ds(first * 8 + k, count, stride=8), :]

    vec_ref[0:1, :] = lay_out(kind(4), 8)
    vec_ref[1:2, :] = lay_out(kind(5), 8)
    vec_ref[2:3, :] = lay_out(kind(2, z * 32, 32), 32)
    vec_ref[4:5, :] = lay_out(kind(1) + kind(3), 8)
    lane = lax.broadcasted_iota(jnp.int32, (128, 128), 1)
    row = lax.broadcasted_iota(jnp.int32, (128, 128), 0)
    qkv = kind(0)
    groups = []
    for g in range(3):
        here = jnp.where(lane < 8, pltpu.roll(qkv, 128 - 8 * g, 1) if g else qkv, 0.0)
        groups.append(spread(here, 8))
    for part in range(3):
        for half in range(2):
            want = (part * 8 + z * 2 + half) * 16 + lane // 8
            total = jnp.zeros((128, 128), F32)
            for g in range(3):
                total = total + jnp.where(3 * row + g == want, groups[g], 0.0)
            at = part * 256 + half * 128
            vec_ref[3:4, at : at + 128] = jnp.sum(total, axis=0, keepdims=True)


def front_kernel(known, z_ref, *rest):
    z = z_ref[0]
    step = pl.program_id(0)
    if not known:
        rest, (wo_ref, vec_ref, block_s) = rest[:-3], rest[-3:]
    x_ref, c_ref, n_ref, act_ref, dup_ref, q_ref, k_ref, v_ref, dm_ref, stat_ref, sum_ref = rest[
        -11:
    ]
    tile = x_ref.shape[1]
    for at, piece in enumerate(rest[:NZ]):

        @pl.when(step == at)
        def _(piece=piece):
            x_ref[0], c_ref[0] = piece[:tile], piece[tile:]

    w_ref = rest[NZ]
    if known:
        wo_ref, vec_ref, cos_ref, sin_ref = rest[NZ + 1 : NZ + 5]
    else:
        cos_ref, sin_ref = rest[NZ + 1 : NZ + 3]

        @pl.when(step == 0)
        def _():
            unpack_parameters(z, w_ref, wo_ref, vec_ref, block_s)

    gain_ref, shift_ref, bu_ref, bq_ref = [vec_ref.at[k : k + 1] for k in range(4)]

    @pl.when(step == 0)
    def _():
        sum_ref[...] = jnp.zeros_like(sum_ref)

    def put(ref, value):
        for r in range(tile // 256):
            row = lax.rem(pl.program_id(0) * (tile // 256) + r + z, 4) * 256
            ref[0, pl.ds(pl.multiple_of(row, 256), 256), :] = value[r * 256 : r * 256 + 256]

    def d_act_of(j):
        return dot_nt(c_ref[0], w_ref[j * 256 : j * 256 + 256, 1792:2816])

    def in_of(j):
        return dot(n_ref[0], w_ref[:, j * 256 : j * 256 + 256])

    d_act = d_act_of(0)
    d_mixed = dot_nt(c_ref[0], wo_ref[...])
    x = x_ref[0].astype(F32)
    average = jnp.mean(x, axis=-1, keepdims=True)
    centered = x - average
    spread = jnp.mean(centered * centered, axis=-1, keepdims=True)
    rs = lax.rsqrt(spread + 1e-05)
    stat_ref[0, :, 0:1] = average
    stat_ref[0, :, 1:2] = rs
    n_ref[0] = (centered * rs * gain_ref[...] + shift_ref[...]).astype(BF)
    put(dm_ref, d_mixed.astype(BF))
    up = in_of(0)
    k0 = 0.7978845608028654
    k1 = k0 * 0.044715
    for j in range(4):
        cols = slice(j * 256, j * 256 + 256)
        if j < 3:
            next_up, next_act = in_of(j + 1), d_act_of(j + 1)
        else:
            q, k, v = in_of(4), in_of(5), in_of(6)
        up = up + bu_ref[:, cols]
        square = up * up
        half = 0.5 + 0.5 * jnp.tanh(up * (k0 + k1 * square))
        act = up * half
        slope = half + 2.0 * act * (1.0 - half) * (k0 + 3.0 * k1 * square)
        d_up = (slope * d_act).astype(BF)
        act_ref[0, :, cols] = act.astype(BF)
        dup_ref[0, :, cols] = d_up
        back = d_up.astype(F32)
        sum_ref[:, cols] += jnp.sum(back.reshape(back.shape[0] // 8, 8, 256), axis=0)
        up, d_act = next_up, next_act
    tabs = (cos_ref[0], sin_ref[0])
    def turn_both(value):
        return jnp.concatenate(
            [turn(value[:, h : h + 128], *tabs, 1.0) for h in (0, 128)], axis=1
        ).astype(BF)

    q = turn_both(q + bq_ref[:, 0:256]) * BF(0.125)
    put(q_ref, q)
    put(k_ref, turn_both(k + bq_ref[:, 256:512]))
    put(v_ref, (v + bq_ref[:, 512:768]).astype(BF))


ANY = pl.BlockSpec(memory_space=pl.ANY)
QUICK = pl.CostEstimate(flops=1024, bytes_accessed=1024, transcendentals=0)


def front(z, pieces, weights, known, cos, sin, after, limit):
    tile, d = pieces[0].shape[-2] // 2, pieces[0].shape[-1]
    n = tile * NZ

    def tok(width):
        return pl.BlockSpec((1, tile, width), lambda j, z: (0, j, 0))

    def turned(width):
        return pl.BlockSpec((1, tile, width), lambda j, z: (0, lax.rem(j + z[0], NZ), 0))

    def row(width):
        return pl.BlockSpec((1, n, width), lambda j, z: (0, 0, 0))

    def whole(a):
        return pl.BlockSpec(a.shape, lambda j, z: (0, 0), pipeline_mode=pl.Buffered(1))

    def keep(*shape):
        return pl.BlockSpec(shape, lambda j, z: (0, 0))

    first = [whole(a) for a in pieces]
    fixed = (weights, *known)
    out_specs = [tok(d)] * 5 + [row(256)] * 4 + [tok(128), keep(8, 1024)]
    out_shape = [jax.ShapeDtypeStruct((1, n, w), BF) for w in [d] * 5 + [256] * 4]
    out_shape += [jax.ShapeDtypeStruct((1, n, 128), F32), jax.ShapeDtypeStruct((8, 1024), F32)]
    scratch = []
    if not known:
        out_specs += [keep(256, d), keep(8, d)]
        out_shape += [jax.ShapeDtypeStruct((256, d), BF), jax.ShapeDtypeStruct((8, d), F32)]
        scratch = [pltpu.VMEM((1024, 128), F32)]
    return pl.pallas_call(
        functools.partial(front_kernel, bool(known)),
        grid_spec=pltpu.PrefetchScalarGridSpec(
            num_scalar_prefetch=1,
            grid=(NZ,),
            in_specs=first + [whole(a) for a in fixed] + [turned(128)] * 2 + [ANY] * len(after),
            out_specs=out_specs,
            scratch_shapes=scratch,
        ),
        out_shape=out_shape,
        compiler_params=pltpu.CompilerParams(vmem_limit_bytes=limit * MB),
        cost_estimate=QUICK,
        name="front",
    )(z, *pieces, *fixed, cos, sin, *after)


def attend_kernel(
    z_ref, q_ref, k_ref, v_ref, dm_ref, row_ref, key_ref, cos_ref, sin_ref, *rest,
):
    mixed_ref, dqkv_ref, sum_ref, bias_s, s_s, dp_s, p_s, ds_s, qm_s, dmm_s, dk_s, dv_s = rest[-12:]
    B = 256
    z = z_ref[0]
    sum_ref[...] = jnp.zeros_like(sum_ref)

    def put(part, a, value):
        rows = pl.ds(pl.multiple_of(lax.rem(a - z + 4, 4) * B, B), B)
        if part is None:
            mixed_ref[0, rows, :] = value
        else:
            dqkv_ref[0, part, rows, :] = value
            sum_ref[part, 0:1, :] += jnp.sum(value.astype(F32), axis=0, keepdims=True)

    key_col = key_ref[0].T
    lane_head = lax.broadcasted_iota(jnp.int32, (B, 128), 1) // 64
    diff = lax.broadcasted_iota(jnp.int32, (B, B), 0) - lax.broadcasted_iota(jnp.int32, (B, B), 1)

    def prepare(aq):
        par, n, here = aq % 2, (aq + 1) * B, slice(aq * B, aq * B + B)
        bias = jnp.where(key_col[0:n, 0:1] == row_ref[0, 0:1, here], 0.0, -1e30)
        if aq:
            bias_s[par, 0 : aq * B, :] = bias[: aq * B]
        edge = jnp.where(diff <= 0, bias[aq * B :], -1e30)
        bias_s[par, here, :] = jnp.where(diff == 0, 0.0, edge)
        q_all, d_all = q_ref[0, here, :], dm_ref[0, here, :]
        for h in range(2):
            cols = slice(h * B, h * B + B)
            qm_s[par, cols, :] = jnp.where(lane_head == h, q_all, jnp.zeros_like(q_all))
            dmm_s[par, cols, :] = jnp.where(lane_head == h, d_all, jnp.zeros_like(d_all))

    def products(aq, h):
        par, n, cols = aq % 2, (aq + 1) * B, slice(h * B, h * B + B)
        s = dot_nt(k_ref[0, 0:n, :], qm_s[par, cols, :]) + bias_s[par, 0:n, :]
        s_s[h, 0:n] = s
        dp_s[h, 0:n] = dot_nt(v_ref[0, 0:n, :], dmm_s[par, cols, :])
        return jnp.max(s, axis=0, keepdims=True)

    def soften(aq, h, top):
        par, n, cols = aq % 2, (aq + 1) * B, slice(h * B, h * B + B)
        e = jnp.exp(s_s[h, 0:n] - top)
        s_s[h, 0:n] = e
        inv = 1.0 / jnp.sum(e, axis=0, keepdims=True)
        mean = jnp.sum(e * dp_s[h, 0:n], axis=0, keepdims=True) * inv
        p = s_s[h, 0:n] * inv
        p_s[par, 0:n, cols] = p.astype(BF)
        ds_s[par, 0:n, cols] = (p * (dp_s[h, 0:n] - mean)).astype(BF)

    def pick(value):
        return jnp.where(lane_head == 0, value[0:B], value[B:])

    def gather(aq, part):
        par, n, here = aq % 2, (aq + 1) * B, slice(aq * B, aq * B + B)
        if part == 0:
            put(None, aq, pick(dot_tn(p_s[par, 0:n, :], v_ref[0, 0:n, :])).astype(BF))
        elif part == 1:
            dq = pick(dot_tn(ds_s[par, 0:n, :], k_ref[0, 0:n, :])) * 0.125
            put(0, aq, turn(dq, cos_ref[0, here, :], sin_ref[0, here, :], -1.0).astype(BF))
        else:
            left, right, to = (p_s, dmm_s, dv_s) if part == 2 else (ds_s, qm_s, dk_s)
            value = dot(left[par, 0:n, :], right[par])
            if aq:
                to[0 : aq * B, :] += value[: aq * B]
            to[here, :] = value[aq * B :]

    prepare(0)
    top = products(0, 0)
    for aq in range(4):
        ahead = products(aq, 1)
        if aq:
            gather(aq - 1, 0)
            gather(aq - 1, 1)
        soften(aq, 0, top)
        if aq:
            gather(aq - 1, 2)
            gather(aq - 1, 3)
        if aq < 3:
            prepare(aq + 1)
            top = products(aq + 1, 0)
        soften(aq, 1, ahead)
    for part in range(4):
        gather(3, part)
    for a in range(4):
        here = slice(a * B, a * B + B)
        put(1, a, turn(dk_s[here, :], cos_ref[0, here, :], sin_ref[0, here, :], -1.0).astype(BF))
        put(2, a, dv_s[here, :].astype(BF))


def attend(z, q, k, v, dm, seg_row, seg_key, cos, sin, after, limit):
    n = q.shape[1]
    half = pl.BlockSpec((1, n, 128), lambda g, z: (0, 0, g))
    table = pl.BlockSpec((1, n, 128), lambda g, z: (0, 0, 0))
    line = pl.BlockSpec((1, 8, n), lambda g, z: (0, 0, 0))
    S = pltpu.VMEM
    return pl.pallas_call(
        attend_kernel,
        grid_spec=pltpu.PrefetchScalarGridSpec(
            num_scalar_prefetch=1,
            grid=(2,),
            in_specs=[half] * 4 + [line] * 2 + [table] * 2 + [ANY] * len(after),
            out_specs=[
                half,
                pl.BlockSpec((1, 3, n, 128), lambda g, z: (0, 0, 0, g)),
                pl.BlockSpec((3, 8, 128), lambda g, z: (0, 0, g)),
            ],
            scratch_shapes=[
                S((2, n, 256), F32), S((2, n, 256), F32), S((2, n, 256), F32),
                S((2, n, 512), BF), S((2, n, 512), BF),
                S((2, 512, 128), BF), S((2, 512, 128), BF),
                S((n, 128), F32), S((n, 128), F32),
            ],
        ),
        out_shape=[
            jax.ShapeDtypeStruct((1, n, 256), BF),
            jax.ShapeDtypeStruct((1, 3, n, 256), BF),
            jax.ShapeDtypeStruct((3, 8, 256), F32),
        ],
        compiler_params=pltpu.CompilerParams(vmem_limit_bytes=limit * MB),
        cost_estimate=QUICK,
        name="attend",
    )(z, q, k, v, dm, seg_row, seg_key, cos, sin, *after)


def back_kernel(
    z_ref, act_ref, mix_ref, dup_ref, dqkv_ref, x_ref, stat_ref, wd_ref, wo_ref, wi_ref, *rest,
):
    cut, gain_ref, shift_ref = rest[-3:]
    z = z_ref[0]
    out = dot(act_ref[0], wd_ref[...]) + dot(mix_ref[0], wo_ref[...])
    dn = dot_nt(dup_ref[0], wi_ref[:, 0:1024])
    for part in range(3):
        at = 1024 + part * 256
        dn = dn + dot_nt(dqkv_ref[0, part], wi_ref[:, at : at + 256])
    xhat = (x_ref[0].astype(F32) - stat_ref[0, :, 0:1]) * stat_ref[0, :, 1:2]
    gain_ref[...] = jnp.sum((dn * xhat).reshape(-1, 8, 256), axis=0)
    shift_ref[...] = jnp.sum(dn.reshape(-1, 8, 256), axis=0)
    for r in range(NZ):
        rows = slice(r * 256, r * 256 + 256)
        first = pl.multiple_of(lax.rem(r + z, NZ) * 512, 512)
        cut[pl.ds(first, 256), :] = out[rows].astype(BF)
        cut[pl.ds(first + 256, 256), :] = dn[rows].astype(BF)


def back(z, act, mixed, d_up, d_qkv, x, stat, weights, w_o, after, limit):
    def rows(a):
        return pl.BlockSpec(a.shape, lambda j, z: (0,) * a.ndim, pipeline_mode=pl.Buffered(1))

    def cols(n, first=0):
        return pl.BlockSpec((n, 256), lambda j, z: (0, first + j))

    return pl.pallas_call(
        back_kernel,
        grid_spec=pltpu.PrefetchScalarGridSpec(
            num_scalar_prefetch=1,
            grid=(4,),
            in_specs=[rows(a) for a in (act, mixed, d_up, d_qkv)]
            + [
                pl.BlockSpec((1, 1024, 256), lambda j, z: (0, 0, j)),
                rows(stat),
                cols(1024, 7),
                cols(256),
                pl.BlockSpec((256, 1792), lambda j, z: (j, 0)),
            ]
            + [ANY] * len(after),
            out_specs=[cols(2048)] + [cols(8)] * 2,
        ),
        out_shape=[jax.ShapeDtypeStruct((2048, 1024), BF)]
        + [jax.ShapeDtypeStruct((8, 1024), F32)] * 2,
        compiler_params=pltpu.CompilerParams(vmem_limit_bytes=limit * MB),
        cost_estimate=QUICK,
        name="back",
    )(z, act, mixed, d_up, d_qkv, x, stat, weights, w_o, weights, *after)


def put_halves(c, value, own_ref, other_ref, lo):
    value = value.reshape(4, 2, 32, value.shape[1])
    first, second = [value[:, k].reshape(128, value.shape[3]) for k in range(2)]
    hi = lo + value.shape[3]
    own_ref[:, lo:hi] = jnp.where(c == 0, first, second).astype(BF)
    other_ref[:, lo:hi] = jnp.where(c == 0, second, first).astype(BF)


def grads_mlp0_kernel(n_ref, dup_ref, act_ref, cot_ref, *rest):
    rest[-1][:, 0:1024] = dot_tn(n_ref[0], dup_ref[0]).astype(BF)
    rest[-1][:, 1024:2048] = dot_tn(act_ref[0], cot_ref[0]).astype(BF)


def grads_mlp1_kernel(c_ref, n_ref, dup_ref, act_ref, cot_ref, sum_ref, own_ref, other_ref):
    c = c_ref[0]
    up = sum_ref[:, 0:1024].astype(F32) + dot_tn(n_ref[0], dup_ref[0])
    put_halves(c, up, own_ref, other_ref, 0)
    down = sum_ref[:, 1024:2048].astype(F32) + dot_tn(act_ref[0], cot_ref[0])
    put_halves(c, down, own_ref, other_ref, 1024)


def grads_mlp0(normed, d_up, act, cot, after):
    tokens, width = normed.shape[1:]
    part = pl.BlockSpec((1, tokens, 256), lambda i: (0, 0, i))
    whole = pl.BlockSpec(d_up.shape, lambda i: (0, 0, 0), pipeline_mode=pl.Buffered(1))
    return pl.pallas_call(
        grads_mlp0_kernel,
        grid=(width // 256,),
        in_specs=[part, whole, part, whole] + [ANY] * len(after),
        out_specs=pl.BlockSpec((256, 2048), lambda i: (i, 0)),
        out_shape=jax.ShapeDtypeStruct((width, 2048), BF),
        compiler_params=pltpu.CompilerParams(vmem_limit_bytes=24 * MB),
        cost_estimate=QUICK,
        name="grads_mlp0",
    )(normed, d_up, act, cot, *after)


def grads_mlp1(c, normed, d_up, act, cot, first):
    tokens, width = normed.shape[1:]
    part = pl.BlockSpec((1, tokens, 256), lambda i, c: (0, 0, i))
    whole = pl.BlockSpec(d_up.shape, lambda i, c: (0, 0, 0), pipeline_mode=pl.Buffered(1))
    return pl.pallas_call(
        grads_mlp1_kernel,
        grid_spec=pltpu.PrefetchScalarGridSpec(
            num_scalar_prefetch=1,
            grid=(width // 256,),
            in_specs=[part, whole, part, whole, pl.BlockSpec((256, 2048), lambda i, c: (i, 0))],
            out_specs=[pl.BlockSpec((128, 2048), lambda i, c: (i, 0))] * 2,
        ),
        out_shape=[jax.ShapeDtypeStruct((width // 2, 2048), BF)] * 2,
        compiler_params=pltpu.CompilerParams(vmem_limit_bytes=46 * MB),
        cost_estimate=QUICK,
        name="grads_mlp1",
    )(c, normed, d_up, act, cot, first)


def grads_att_kernel(
    c_ref, n0_ref, n1_ref, dqkv0_ref, dqkv1_ref, mix0_ref, mix1_ref, cot0_ref, cot1_ref,
    *rest,
):
    own_ref, other_ref, out_s = rest[-3:]
    c = c_ref[0]
    i = pl.program_id(0)

    @pl.when(i == 0)
    def _():
        out_s[...] = dot_tn(mix0_ref[0], cot0_ref[0]) + dot_tn(mix1_ref[0], cot1_ref[0])

    for part in range(3):
        both = dot_tn(n0_ref[0], dqkv0_ref[0, part]) + dot_tn(n1_ref[0], dqkv1_ref[0, part])
        put_halves(c, both, own_ref, other_ref, part * 256)
    rows = out_s[pl.ds(pl.multiple_of(i * 64, 64), 64), :]
    rows = [rows[d * 8 : d * 8 + 8, b * 256 : b * 256 + 256] for d in range(8) for b in range(4)]
    put_halves(c, jnp.concatenate(rows), own_ref, other_ref, 768)


def grads_att(c, normed, d_qkv, mixed, cot, after):
    tokens, width = normed[0].shape[1:]

    def whole(a):
        return pl.BlockSpec(a.shape, lambda i, c: (0,) * a.ndim, pipeline_mode=pl.Buffered(1))

    return pl.pallas_call(
        grads_att_kernel,
        grid_spec=pltpu.PrefetchScalarGridSpec(
            num_scalar_prefetch=1,
            grid=(4,),
            in_specs=[pl.BlockSpec((1, tokens, 256), lambda i, c: (0, 0, i))] * 2
            + [whole(a) for a in (*d_qkv, *mixed, *cot)]
            + [ANY] * len(after),
            out_specs=[pl.BlockSpec((128, 1024), lambda i, c: (i, 0))] * 2,
            scratch_shapes=[pltpu.VMEM((256, 1024), F32)],
        ),
        out_shape=[jax.ShapeDtypeStruct((512, 1024), BF)] * 2,
        compiler_params=pltpu.CompilerParams(vmem_limit_bytes=58 * MB),
        cost_estimate=QUICK,
        name="grads_att",
    )(c, *normed, *d_qkv, *mixed, *cot, *after)


def finish_kernel(x_ref, c_ref, vec_ref, part_ref, *rest):
    out_ref, dx_ref = rest[-2:]
    x = x_ref[0, 0].astype(F32)
    branch, g = part_ref[0].astype(F32), part_ref[1].astype(F32)
    out_ref[0] = (x + (branch + vec_ref[4:5, :])).astype(BF)
    centered = x - jnp.mean(x, axis=-1, keepdims=True)
    rs = lax.rsqrt(jnp.mean(centered * centered, axis=-1, keepdims=True) + 1e-05)
    xhat = centered * rs
    g = g * vec_ref[0:1, :]
    mean_g = jnp.mean(g, axis=-1, keepdims=True)
    mean_gx = jnp.mean(g * xhat, axis=-1, keepdims=True)
    dx_ref[0] = c_ref[0, 0].astype(F32) + rs * (g - mean_g - xhat * mean_gx)


def finish(micro, x, cot, part, vectors, others, after=()):
    n, d = x.shape[2:]
    tile = pl.BlockSpec((1, 1, 128, d), lambda i: (micro, 0, i, 0))
    out = pl.BlockSpec((1, 128, d), lambda i: (micro, i, 0))
    return pl.pallas_call(
        finish_kernel,
        grid=(n // 128,),
        in_specs=[tile] * 2
        + [
            pl.BlockSpec((8, d), lambda i: (0, 0)),
            pl.BlockSpec((2, 128, d), lambda i: (0, i, 0)),
        ]
        + [ANY] * (len(others) + len(after)),
        out_specs=[out] * 2,
        out_shape=[jax.ShapeDtypeStruct((2, n, d), BF), jax.ShapeDtypeStruct((2, n, d), F32)],
        input_output_aliases={4 + k: k for k in range(len(others))},
        compiler_params=pltpu.CompilerParams(vmem_limit_bytes=58 * MB),
        cost_estimate=QUICK,
        name="finish",
    )(x, cot, vectors, part.reshape(2, n, d), *others, *after)


def add_kernel(a_ref, b_ref, *rest):
    rest[-1][...] = (a_ref[...].astype(F32) + b_ref[...].astype(F32)).astype(BF)


def add_after(a, b, after):
    n, d = a.shape
    part = pl.BlockSpec((n // 4, d), lambda i: (i, 0))
    return pl.pallas_call(
        add_kernel,
        grid=(4,),
        in_specs=[part, part] + [ANY] * len(after),
        out_specs=part,
        out_shape=jax.ShapeDtypeStruct((n, d), BF),
        compiler_params=pltpu.CompilerParams(vmem_limit_bytes=32 * MB),
        cost_estimate=QUICK,
        name="add_after",
    )(a, b, *after)


def to_columns_kernel(z_ref, up_ref, qkv_ref, down_ref, out_ref, *rest):
    vectors, rows_ref, pieces = rest[:6], rest[6], rest[7:]
    lines = [v[...].astype(F32).reshape(1, -1) for v in vectors]
    lines = [jnp.concatenate([v, jnp.zeros((1, 128 - v.shape[1]), F32)], axis=1) for v in lines]
    block = jnp.concatenate(lines + [jnp.zeros((2, 128), F32)], axis=0).astype(BF)
    for k, piece in enumerate(pieces):
        to = lax.rem(z_ref[0] + k, NZ)
        piece[:, 0:1024] = up_ref[:, pl.ds(pl.multiple_of(to * 1024, 1024), 1024)]
        for part in range(3):
            first = pl.multiple_of(part * 1024 + to * 256, 256)
            at = 1024 + part * 256
            piece[:, at : at + 256] = qkv_ref[:, pl.ds(first, 256)]
        piece[:, 1792:1920] = block
    rows = jnp.concatenate([down_ref[...].astype(F32), out_ref[...].astype(F32)], axis=0)
    rows_ref[...] = rows.astype(BF)


def to_payload_kernel(z_ref, g0_ref, g1_ref, g2_ref, g3_ref, rows_ref, after_ref, out_ref):
    got = [g[...].astype(F32) for g in (g0_ref, g1_ref, g2_ref, g3_ref)]
    columns = []
    for source in range(NZ):
        k = lax.rem(z_ref[0] - source + NZ, NZ)
        value = got[3]
        for j in range(3):
            value = jnp.where(k == j, got[j], value)
        columns.append(value)
    columns = jnp.concatenate(columns, axis=0)
    rows = rows_ref[...].astype(F32)
    w_out = jnp.concatenate([rows[32:40, b * 256 : b * 256 + 256] for b in range(4)], axis=0)
    out_ref[:, 0:1792] = columns[:, 0:1792].astype(BF)
    out_ref[:, 1792:2816] = rows[0:32].astype(BF)
    out_ref[:, 2816:3072] = w_out.astype(BF)
    out_ref[:, 3072:3200] = columns[:, 1792:1920].astype(BF)


def total_of(refs, rows):
    return sum([r[rows, :].astype(F32) for r in refs[1:]], refs[0][rows, :].astype(F32))


def to_xy_kernel(c_ref, own_ref, got_ref, va_ref, vb_ref, out_ref):
    total = total_of((own_ref, got_ref), slice(None))
    out_ref[:, :, 0:1024] = total.astype(BF).reshape(16, 32, 1024)
    vec = (va_ref[...] + vb_ref[...]).reshape(16, 2, 32, 128)
    out_ref[:, :, 1024:1152] = jnp.where(c_ref[0] == 0, vec[:, 0], vec[:, 1]).astype(BF)


def to_y_kernel(at_ref, mlp_ref, *outs):
    for k, out in enumerate(outs):
        rows = pl.ds(pl.multiple_of(lax.rem(at_ref[0] + k, 4) * 32, 32), 32)
        out[...] = mlp_ref[rows, :]


def to_z_kernel(att_ref, a_ref, b_ref, c_ref, d_ref, home_ref, rows_ref):
    mlp = total_of((a_ref, b_ref, c_ref, d_ref), slice(0, 32))
    att = att_ref[0].astype(F32)
    for k in range(1, 16):
        att = att + att_ref[k].astype(F32)
    home = jnp.concatenate([mlp[:, :1024], att[:, :768], att[:, 1024:1152]], axis=1)
    home_ref[...] = home.reshape(4, 8, 1920).astype(BF)
    rows_ref[0:32, :] = mlp[:, 1024:2048]
    out = att[:, 768:1024].reshape(4, 8, 256)
    for b in range(4):
        rows_ref[32:40, b * 256 : b * 256 + 256] = out[b]


def home_kernel(home_ref, up_ref, qkv_ref, *vectors):
    for k in range(NZ):
        up_ref[:, k * 1024 : k * 1024 + 1024] = home_ref[k, :, 0:1024].astype(F32)
        for part in range(3):
            at = part * 1024 + k * 256
            own = 1024 + part * 256
            qkv_ref[:, at : at + 256] = home_ref[k, :, own : own + 256].astype(F32)
    total = jnp.sum(home_ref[:, :, 1792:1920].astype(F32), axis=0)
    for k, ref in enumerate(vectors):
        ref[...] = total[k, : ref.shape[0]]


def in_vmem(kernel, name, operands, shapes, scalars=None, after=(), limit=58):
    def whole(shape):
        return pl.BlockSpec(shape, lambda i: (0,) * len(shape))

    specs = [whole(a.shape) for a in operands] + [ANY] * len(after)
    operands = (*operands, *after)
    if scalars is not None:
        specs = [pl.BlockSpec(memory_space=pltpu.SMEM)] + specs
        operands = (scalars, *operands)
    return pl.pallas_call(
        kernel,
        grid=(1,),
        in_specs=specs,
        out_specs=[whole(s[0]) for s in shapes],
        out_shape=[jax.ShapeDtypeStruct(*s) for s in shapes],
        compiler_params=pltpu.CompilerParams(vmem_limit_bytes=limit * MB),
        cost_estimate=QUICK,
        name=name,
    )(*operands)


def pack_kernel(a_ref, b_ref, *rest):
    rest[-1][0] = a_ref[0, 0]
    rest[-1][1] = b_ref[0, 0]


def pack(micro, a, b, after):
    n, d = a.shape[2:]
    part = pl.BlockSpec((1, 1, n // 2, d), lambda i: (micro, 0, i, 0))
    return pl.pallas_call(
        pack_kernel,
        grid=(2,),
        in_specs=[part, part] + [ANY] * len(after),
        out_specs=pl.BlockSpec((2, n // 2, d), lambda i: (0, i, 0)),
        out_shape=jax.ShapeDtypeStruct((2, n, d), BF),
        compiler_params=pltpu.CompilerParams(vmem_limit_bytes=58 * MB),
        cost_estimate=QUICK,
        name="pack",
    )(a, b, *after).reshape(2 * n, d)


def doc_positions(seg_row):
    length = seg_row.shape[-1]
    token_index = jnp.arange(length, dtype=jnp.int32)
    previous = jnp.concatenate([seg_row[..., :1], seg_row[..., :-1]], axis=-1)
    starts = jnp.where((token_index == 0) | (seg_row != previous), token_index, 0)
    doc_start = lax.cummax(starts, axis=seg_row.ndim - 1)
    return token_index - doc_start


def rotary_tables(positions):
    dim = jnp.arange(128, dtype=jnp.int32) % HEAD_DIM
    frequency = 10000.0 ** (-(dim % (ROT // 2)).astype(F32) * 2.0 / ROT)
    frequency = jnp.where(dim < ROT, frequency, 0.0)
    angles = positions.astype(F32)[..., None] * frequency
    return jnp.cos(angles), jnp.sin(angles) * jnp.where(dim < ROT // 2, -1.0, 1.0)


def send(value, axis, step):
    size = lax.axis_size(axis)
    return lax.ppermute(value, axis, [(i, (i + step) % size) for i in range(size)])


def exchange(parts, axis):
    return [parts[0]] + [send(parts[k], axis, k) for k in range(1, 4)]


def body(
    hidden_in,
    segments,
    valid_mask,
    w_qkv,
    w_out,
    w_up,
    w_down,
    b_qkv,
    b_out,
    b_up,
    b_down,
    ln_gain,
    ln_shift,
    cotangent,
):
    z = lax.axis_index("z")
    c = lax.axis_index("c").astype(jnp.int32).reshape(1)
    micro_count, _, group, width = hidden_in.shape
    row_len = group * NZ
    z_arr = z.astype(jnp.int32).reshape(1)

    w_rows, *columns = in_vmem(
        to_columns_kernel,
        "to_columns",
        (w_up, w_qkv, w_down, w_out, b_qkv, b_out, b_up, b_down, ln_gain, ln_shift),
        [((40, 1024), BF)] + [((8, 1920), BF)] * 4,
        z_arr,
    )
    there, back_home = [], []
    for d in range(32):
        for s in range(4):
            pair = (d * 4 + s, ((d % 8) * 4 + s) * 4 + d // 8)
            there.append(pair)
            back_home.append(pair[::-1])
    columns = exchange(columns, "z")
    w_rows = lax.ppermute(w_rows, ("x", "y", "c", "z"), there)
    mine0 = pack(0, hidden_in, cotangent, ())
    (payload,) = in_vmem(
        to_payload_kernel,
        "to_payload",
        (*columns, w_rows),
        [((32, 3200), BF)],
        z_arr,
        after=(mine0,),
    )
    weights = lax.all_gather(payload, ("x", "y", "c"), axis=0, tiled=True)

    pieces0 = [mine0] + [send(mine0, "z", -step) for step in range(1, NZ)]
    mine1 = pack(1, hidden_in, cotangent, (pieces0[2],))
    pieces1 = [mine1] + [send(mine1, "z", -step) for step in range(1, NZ)]

    seg = segments[:, 0]
    key_seg = jnp.where(valid_mask[:, 0] > 0, seg, -1)
    seg_row, seg_key = [
        jnp.broadcast_to(s.astype(F32)[:, None, :], (micro_count, 8, row_len)) for s in (seg, key_seg)
    ]
    tables = rotary_tables(doc_positions(seg))

    tables = [[t[m : m + 1] for t in tables] for m in range(micro_count)]

    lines = [[s[m : m + 1] for s in (seg_row, seg_key)] for m in range(micro_count)]

    def run_attend(m, heads, after, limit):
        return attend(z_arr, *heads, *lines[m], *tables[m], after, limit)

    hid0, cot0, n0, act0, dup0, *heads0, stat0, bup0, w_o, vecs = front(
        z_arr, pieces0, weights, (), *tables[0], (*lines[0], *lines[1]), 34
    )
    mix0, dqkv0, bqkv0 = run_attend(0, heads0, (), 30)
    first = grads_mlp0(n0, dup0, act0, cot0, (mix0,))
    cuts0, gain0, shift0 = back(
        z_arr, act0, mix0, dup0, dqkv0, hid0, stat0, weights, w_o, (first, *pieces1[1:]), 24
    )
    sum0 = lax.psum_scatter(cuts0, "z", scatter_dimension=0, tiled=True)
    hid1, cot1, n1, act1, dup1, *heads1, stat1, bup1 = front(
        z_arr, pieces1, weights, (w_o, vecs), *tables[1], (cuts0,), 48
    )
    cot = (cot0, cot1)
    mlp = grads_mlp1(c, n1, dup1, act1, cot1, first)
    mix1, dqkv1, bqkv1 = run_attend(1, heads1, (mlp[0],), 46)
    mlp = add_after(mlp[0], send(mlp[1], "c", 1), (mix1,))
    att = grads_att(c, (n0, n1), (dqkv0, dqkv1), (mix0, mix1), cot, (mlp,))
    mlp = lax.psum_scatter(mlp, "x", scatter_dimension=0, tiled=True)
    cuts1, gain1, shift1 = back(
        z_arr, act1, mix1, dup1, dqkv1, hid1, stat1, weights, w_o, (sum0, att[0]), 58
    )
    sum1 = lax.psum_scatter(cuts1, "z", scatter_dimension=0, tiled=True)
    sums = ((bqkv0, gain0, shift0), (bqkv1, gain1, shift1))
    sum_bup = bup0 + bup1
    sum_bqkv, sum_gain, sum_shift = [jnp.sum(a + b, axis=-2) for a, b in zip(*sums)]

    mine = jnp.arange(NZ) == z
    sum_cot = jnp.sum(cotangent.astype(F32), axis=(0, 1, 2)).reshape(128, 8)
    sum_bqkv = jnp.where(mine[None, :, None], sum_bqkv.reshape(3, 1, 256), 0.0)
    sum_bup = jnp.where(mine[:, None], jnp.sum(sum_bup, axis=0)[None, :], 0.0)
    parts = (
        sum_bqkv.reshape(128, 24),
        sum_cot,
        sum_bup.reshape(128, 32),
        sum_cot,
        sum_gain.reshape(128, 8),
        sum_shift.reshape(128, 8),
    )
    vec_grads = jnp.stack(
        [jnp.pad(p, ((0, 0), (0, 128 - p.shape[1]))) for p in parts] + [jnp.zeros((128, 128), F32)] * 2,
        axis=1,
    ).reshape(1024, 128)
    mlp = in_vmem(
        to_y_kernel,
        "to_y",
        (mlp,),
        [((32, 2048), BF)] * 4,
        lax.axis_index("y").astype(jnp.int32).reshape(1),
    )
    mlp = exchange(mlp, "y")
    (att,) = in_vmem(
        to_xy_kernel,
        "to_xy",
        (att[0], send(att[1], "c", 1), vec_grads, send(vec_grads, "c", 1)),
        [((16, 32, 1152), BF)],
        c,
        limit=32,
    )
    att = lax.all_to_all(att, ("x", "y"), 0, 0, tiled=True)
    home, rows_home = in_vmem(
        to_z_kernel,
        "to_z",
        (att, *mlp),
        [((4, 8, 1920), BF), ((40, 1024), F32)],
    )
    home = lax.all_to_all(home, "z", 0, 0, tiled=True)
    rows_home = lax.ppermute(rows_home, ("x", "y", "c", "z"), back_home)
    final_up, final_qkv, *final_vectors = in_vmem(
        home_kernel,
        "home",
        (home,),
        [((8, 4096), F32), ((8, 3072), F32)] + [((n,), F32) for n in (24, 8, 32, 8, 8, 8)],
    )
    half = finish(0, hidden_in, cotangent, sum0, vecs, ())
    out_hidden, grad_input = finish(1, hidden_in, cotangent, sum1, vecs, half, (final_up,))
    out_hidden, grad_input = out_hidden[:, None], grad_input[:, None]
    return (
        out_hidden,
        grad_input,
        final_qkv,
        rows_home[32:],
        final_up,
        rows_home[:32],
        *final_vectors,
    )


def solution(mesh):
    parts = jax.sharding.Mesh(mesh.devices.reshape(4, 4, 2, NZ), ("x", "y", "c", "z"))
    dp = ("x", "y", "c")
    rows = P(None, dp, "z", None)
    tokens = P(None, dp, None)
    matrix = P(dp + ("z",), None)
    vector = P(dp + ("z",))
    in_specs = (rows, tokens, tokens) + (matrix,) * 4 + (vector,) * 6 + (rows,)
    out_specs = (rows, rows) + (matrix,) * 4 + (vector,) * 6
    return jax.shard_map(body, mesh=parts, in_specs=in_specs, out_specs=out_specs, check_vma=False)
```
